512 devices in a mesh: leaf: 128 (over z, y, core), vec: 4 (over x).
Axes of the slice: x: 4, y: 8, z: 8, core: 2. Of those that a mesh axis runs over, the one named last changes fastest.
Arguments:
- vectors: bfloat16 [64, 131072], P('vec', 'leaf'), may hold values from -6 to 6
- points: float32 [3, 131072], P(None, 'leaf'), may hold values from 0 to 1
- near_cols: int32 [12, 2048], P(None, 'leaf'), may hold values from 0 to 2047, as said below
- near_count: int32 [2048], P('leaf'), may hold values from 3 to 12, as said below
- basis: bfloat16 [32, 131072], P(None, 'leaf'), may hold values from -0.75 to 0.75
- xfer_low: bfloat16 [3840, 1024], P('leaf'), may hold values from -0.75 to 0.75
- couple_low: bfloat16 [3, 3968, 1024], P(None, 'leaf'), may hold values from -0.4375 to 0.4375
- xfer_top: bfloat16 [254, 1024], replicated, may hold values from -0.75 to 0.75
- couple_top: bfloat16 [3, 124, 1024], replicated, may hold values from -0.4375 to 0.4375
Outputs:
- result: bfloat16 [64, 131072], P('vec', 'leaf')
The draws below stay inside these ranges and needn't reach their ends.
Inputs may be any that keep to these rules, and one draw needn't show every extreme that they name: `near_cols`: entries of leaf i name leaves within 8 of i; entries 0, 1 and 2 of leaf i are i, min(i + 8, 2047) and max(i - 8, 0). Entries 0 to near_count[i] - 1 of leaf i are live; some leaf has 12.
All inputs are finite; a program needn't handle non-finite values.
Results may differ from the reference program's by a relative error of at most 0.0034.
Values may be sent and summed in bfloat16 or wider, within the bound.
No kernel may reach another device: no remote copies, remote signals or barrier semaphores. Data moves between devices by JAX's collectives and lax.ppermute only.
A program may use at most 64 MiB of HBM per device.

```python
import math
import jax
import jax.numpy as jnp
from jax import lax

LEAF = 64
RANK = 32
VECS = 64
NEAR = 12
MATVECS = 2
HALO = 8
LEAF_DEV = 16
LEAVES = 2048
POINTS = 131072
N_LEAF = 128


def draw_near_cols(key, part):
    key = jax.random.fold_in(key, 11)
    leaf_ids = jnp.arange(LEAVES, dtype=jnp.int32)
    offsets = jax.random.randint(key, (NEAR, LEAVES), -HALO, HALO + 1, dtype=jnp.int32)
    leading = jnp.stack([jnp.zeros_like(leaf_ids), jnp.full_like(leaf_ids, HALO), jnp.full_like(leaf_ids, -HALO)])
    offsets = jnp.concatenate([leading, offsets[3:]], axis=0)
    return jnp.clip(leaf_ids[None, :] + offsets, 0, LEAVES - 1).astype(jnp.int32)


def draw_near_count(key, part):
    key = jax.random.fold_in(key, 23)
    ceiling_key, leaf_key = jax.random.split(key)
    ceiling = jax.random.randint(ceiling_key, (N_LEAF, 1), 3, NEAR + 1, dtype=jnp.int32)
    ceiling = ceiling.at[0, 0].set(NEAR)
    fresh = jax.random.randint(leaf_key, (N_LEAF, LEAF_DEV), 0, 1 << 20, dtype=jnp.int32)
    counts = 3 + fresh % (ceiling - 2)
    counts = counts.at[0, 0].set(NEAR)
    counts = counts.at[0, 1].set(3)
    return counts.reshape(LEAVES).astype(jnp.int32)


def level_of(stream_key, dims, cuts, smallest, high):
    factor_of, own = 1.0, jax.random.fold_in(stream_key, 6)
    for axis_at, parts in cuts:
        steps = jnp.exp(jax.random.uniform(jax.random.fold_in(own, axis_at), (parts,), jnp.float32, smallest / len(cuts), high / len(cuts)))
        factor_of = factor_of * jnp.repeat(steps, dims[axis_at] // parts).reshape([-1 if axis == axis_at else 1 for axis in range(len(dims))])
    return factor_of


def noise(key, dims, deviation, limit, shards=(), kind=jnp.bfloat16):
    loudness = level_of(key, dims, shards, -0.22, 0.18) if shards else 1.0
    entries = jax.random.normal(key, dims, jnp.float32) * deviation * loudness
    return jnp.minimum(jnp.maximum(entries, -limit), limit).astype(kind)


def setup_inputs(seed: int = 0) -> dict:
    arg_keys = jax.random.split(jax.random.key(seed), 10)
    return {
        "vectors": noise(arg_keys[0], (VECS, POINTS), 1.0, 6.0, ((0, 4), (1, 128))),
        "points": jnp.clip(1.0 * jax.random.uniform(arg_keys[1], (3, POINTS), jnp.float32) ** level_of(arg_keys[1], (3, POINTS), ((1, 128),), -0.2, 0.2), 0.0, 1.0),
        "near_cols": draw_near_cols(jax.random.fold_in(arg_keys[9], 71), 0),
        "near_count": draw_near_count(jax.random.fold_in(arg_keys[9], 71), 0),
        "basis": noise(arg_keys[4], (RANK, POINTS), LEAF ** -0.5, 0.75, ((1, 128),)),
        "xfer_low": noise(arg_keys[5], (2 * LEAVES - 2 * N_LEAF, RANK * RANK), (2 * RANK) ** -0.5, 0.75, ((0, 128),)),
        "couple_low": noise(arg_keys[6], (3, 2 * LEAVES - N_LEAF, RANK * RANK), (6 * RANK) ** -0.5, 0.4375, ((1, 128),)),
        "xfer_top": noise(arg_keys[7], (2 * N_LEAF - 2, RANK * RANK), (2 * RANK) ** -0.5, 0.75),
        "couple_top": noise(arg_keys[8], (3, N_LEAF - 4, RANK * RANK), (6 * RANK) ** -0.5, 0.4375),
    }


KERNEL_LENGTH = 0.25
SOFTEN = 0.01
HIGHEST = lax.Precision.HIGHEST

def kernel_block(target, source, active, kernel_gain):
    squares = jnp.zeros((target.shape[1], target.shape[2], source.shape[2]), jnp.float32)
    for coord in range(3):
        spread = target[coord][:, :, None] - source[coord][:, None, :]
        squares = squares + spread * spread
    values = kernel_gain * jnp.exp(-jnp.sqrt(squares + SOFTEN) / KERNEL_LENGTH)
    return jnp.where(active[:, None, None], values, 0.0).astype(jnp.bfloat16)

def square_table(xfer, rank_size):
    return xfer.astype(jnp.float32).reshape(xfer.shape[:-1] + (rank_size, rank_size))

def raise_level(children, xfer):
    weights = square_table(xfer, children.shape[1])
    terms = jnp.einsum('vsn,nsr->vrn', children, weights, precision=HIGHEST)
    return terms.reshape(terms.shape[0], terms.shape[1], terms.shape[2] // 2, 2).sum(axis=3)

def lower_level(parents, xfer):
    widened = jnp.repeat(parents, 2, axis=2)
    weights = square_table(xfer, parents.shape[1])
    return jnp.einsum('vrn,nsr->vsn', widened, weights, precision=HIGHEST)

def interact(padded, table, first_node):
    node_count = table.shape[1]
    parity = (jnp.arange(node_count, dtype=jnp.int32) + first_node) % 2
    minus_three = padded[:, :, 0:node_count]
    minus_two = padded[:, :, 1:1 + node_count]
    plus_two = padded[:, :, 5:5 + node_count]
    plus_three = padded[:, :, 6:6 + node_count]
    third = jnp.where((parity == 0)[None, None, :], plus_three, minus_three)
    weights = square_table(table, padded.shape[1])
    result = jnp.einsum('vsn,nrs->vrn', minus_two, weights[0], precision=HIGHEST)
    result = result + jnp.einsum('vsn,nrs->vrn', plus_two, weights[1], precision=HIGHEST)
    return result + jnp.einsum('vsn,nrs->vrn', third, weights[2], precision=HIGHEST)

def pad_nodes(values):
    return jnp.pad(values, ((0, 0), (0, 0), (3, 3)))

def device_slice(table, per_device, height):
    node_count = LEAF_DEV >> height
    first_node = 2 * LEAF_DEV - 2 * node_count
    leading = table.shape[:-2]
    tail = table.shape[-1]
    pieces = table.reshape(leading + (N_LEAF, per_device, tail))[..., first_node:first_node + node_count, :]
    return pieces.reshape(leading + (N_LEAF * node_count, tail))

def near_field(signal, points, near_cols, near_count):
    vector_count = signal.shape[0]
    blocks = signal.reshape(vector_count, LEAVES, LEAF)
    places = points.reshape(3, LEAVES, LEAF)
    kernel_gain = 4.0 / math.sqrt(LEAF * NEAR)

    def one_slot(carry, inputs):
        columns, slot_index = inputs
        source = jnp.take(blocks, columns, axis=1)
        kernel_tile = kernel_block(places, jnp.take(places, columns, axis=1), slot_index < near_count, kernel_gain)
        update = jnp.einsum('nab,vnb->vna', kernel_tile.astype(jnp.float32), source.astype(jnp.float32), precision=HIGHEST)
        return (carry + update, None)
    initial = jnp.zeros((vector_count, LEAVES, LEAF), jnp.float32)
    result, _ = lax.scan(one_slot, initial, (near_cols, jnp.arange(NEAR, dtype=jnp.int32)))
    return result.reshape(vector_count, POINTS)

def far_field(signal, basis, xfer_low, couple_low, xfer_top, couple_top):
    vector_count = signal.shape[0]
    levels_dev = LEAF_DEV.bit_length() - 1
    levels_top = N_LEAF.bit_length() - 1
    blocks = signal.reshape(vector_count, LEAVES, LEAF).astype(jnp.float32)
    basis_wide = basis.astype(jnp.float32).reshape(RANK, LEAVES, LEAF)
    upward = [jnp.einsum('vnp,rnp->vrn', blocks, basis_wide, precision=HIGHEST)]
    for height in range(levels_dev):
        upward.append(raise_level(upward[height], device_slice(xfer_low, 2 * LEAF_DEV - 2, height)))
    for height in range(levels_top):
        node_count = N_LEAF >> height
        first_node = 2 * N_LEAF - 2 * node_count
        upward.append(raise_level(upward[levels_dev + height], xfer_top[first_node:first_node + node_count]))
    couplings = []
    for height in range(levels_dev + 1):
        couplings.append(interact(pad_nodes(upward[height]), device_slice(couple_low, 2 * LEAF_DEV - 1, height), 0))
    downward = jnp.zeros((vector_count, RANK, 1), jnp.float32)
    for height in range(levels_top - 1, 0, -1):
        node_count = N_LEAF >> height
        first_node = 2 * N_LEAF - 2 * node_count
        downward = lower_level(downward, xfer_top[first_node:first_node + node_count])
        if height <= levels_top - 2:
            couple_first = N_LEAF - 2 * node_count
            table = couple_top[:, couple_first:couple_first + node_count]
            downward = downward + interact(pad_nodes(upward[levels_dev + height]), table, 0)
    downward = couplings[levels_dev] + lower_level(downward, xfer_top[0:N_LEAF])
    for height in range(levels_dev - 1, -1, -1):
        downward = couplings[height] + lower_level(downward, device_slice(xfer_low, 2 * LEAF_DEV - 2, height))
    result = jnp.einsum('vrn,rnp->vnp', downward, basis_wide, precision=HIGHEST)
    return result.reshape(vector_count, POINTS)

def reference(vectors, points, near_cols, near_count, basis, xfer_low, couple_low, xfer_top, couple_top):
    signal = vectors
    for repeat in range(MATVECS):
        near_part = near_field(signal, points, near_cols, near_count)
        far_part = far_field(signal, basis, xfer_low, couple_low, xfer_top, couple_top)
        signal = (near_part + far_part).astype(jnp.bfloat16)
    return signal
```

```python
import math

import jax
import jax.numpy as jnp
from jax import lax
from jax.experimental import pallas as pl
from jax.experimental.pallas import tpu as pltpu
from jax.sharding import PartitionSpec as P

F32 = jnp.float32
BF16 = jnp.bfloat16
HALO = 8
LEAF_DEV = 16
RANK = 32
NEAR = 12
VEC = 16
DEVICES = 128
CHUNKS = 8
LOW = (0, 16, 24, 28, 30)
NODES = (16, 8, 4, 2)
TOP_XFER = (0, 128, 192, 224, 240, 248)
TOP_COUPLE = (0, 0, 64, 96, 112, 120)
SCALE = 4.0 * math.log2(math.e)
SOFT = 0.01 * SCALE * SCALE
LOG_GAIN = math.log2(4.0 / math.sqrt(64 * NEAR))
VMEM_LIMIT = 48 * 1024 * 1024


def nn(a, b):
    return lax.dot_general(a, b, (((1,), (0,)), ((), ())), preferred_element_type=F32)


def nt(a, b):
    return lax.dot_general(a, b, (((1,), (1,)), ((), ())), preferred_element_type=F32)


def tn(a, b):
    return lax.dot_general(a, b, (((0,), (0,)), ((), ())), preferred_element_type=F32)


def halves(x):
    high = x.astype(BF16)
    return high, (x - high.astype(F32)).astype(BF16)


def lanes_in(rows, lo, size, dtype):
    lane = lax.broadcasted_iota(jnp.int32, (rows, 128), 1)
    return ((lane >= lo) & (lane < lo + size)).astype(F32).astype(dtype)


class Masks:
    def __init__(self):
        self.group = [lanes_in(16, 32 * g, 32, BF16) for g in range(4)]
        self.groupf = [lanes_in(16, 32 * g, 32, F32) for g in range(4)]
        self.half = [lanes_in(16, 64 * g, 64, BF16) for g in range(2)]
        self.halff = [lanes_in(16, 64 * g, 64, F32) for g in range(2)]


def spread_matrix():
    row = lax.broadcasted_iota(jnp.int32, (128, 512), 0)
    col = lax.broadcasted_iota(jnp.int32, (128, 512), 1)
    return (row == ((col >> 7) << 5) + (col & 31)).astype(F32).astype(BF16)


def spread_table(table, spread, out, first):
    count = table.shape[0]
    for c in range(8):
        wide = nn(table[:, 128 * c : 128 * c + 128], spread)
        for q in range(4):
            out[pl.ds(first * 32 + 4 * c + q, count, stride=32), :] = wide[:, 128 * q : 128 * q + 128]


def up_pass(signal, basis, xfer, m):
    total = [0.0] * 4
    for c in range(CHUNKS):
        wide = jnp.concatenate([basis[:, 128 * c : 128 * c + 128]] * 4, axis=0)
        both = nt(jnp.concatenate([signal[c] * m.half[0], signal[c] * m.half[1]], axis=0), wide)
        g = (2 * c) % 4
        total[c // 2] = total[c // 2] + both[:16] * m.groupf[g] + both[16:] * m.groupf[g + 1]
    heights = []
    for h in range(4):
        split = [halves(t) for t in total]
        heights.append(split)
        first = LOW[h] * 32
        if h == 3:
            both = nn(jnp.concatenate(split[0], axis=0), xfer[first : first + 128, :])
            return heights, both[:16] + both[16:]
        count = NODES[h] // 4
        total = [0.0] * max(1, count // 2)
        for t in range(count):
            high, low = split[t]
            left = jnp.concatenate(
                [high * m.half[0], high * m.half[1], low * m.half[0], low * m.half[1]], axis=0
            )
            both = nn(left, xfer[first + 128 * t : first + 128 * t + 128, :])
            both = both[:32] + both[32:]
            g = (2 * t) % 4
            total[t // 2] = total[t // 2] + both[:16] * m.groupf[g] + both[16:] * m.groupf[g + 1]


def write_sends(signal, heights, root, left, right, gather, m):
    for c in range(4):
        left[16 * c : 16 * c + 16, :] = signal[c]
        right[16 * c : 16 * c + 16, :] = signal[c + 4]
    for h in range(4):
        for part in range(2):
            at = 64 * (part + 1) + 16 * h
            left[at : at + 16, :] = heights[h][0][part]
            right[at : at + 16, :] = heights[h][-1][part]
    packed = root[0:4] * m.groupf[0][0:4]
    for g in range(1, 4):
        packed = packed + root[4 * g : 4 * g + 4] * m.groupf[g][0:4]
    block = jnp.concatenate([packed] * 4, axis=0).astype(BF16)
    for q in range(DEVICES // 4):
        gather[16 * q : 16 * q + 16, :] = block


def couple_low(heights, from_left, from_right, table, m):
    result = []
    for h in range(4):
        nodes = NODES[h]
        own = heights[h]
        before = [from_left[at : at + 16, :] for at in (64 + 16 * h, 128 + 16 * h)]
        after = [from_right[at : at + 16, :] for at in (64 + 16 * h, 128 + 16 * h)]

        def node(n, part):
            if n < 0:
                return before[part] * m.group[(nodes + n) % 4]
            if n >= nodes:
                return after[part] * m.group[n - nodes]
            return own[n // 4][part] * m.group[n % 4]

        chunks = []
        for t in range(max(1, nodes // 4)):
            targets = range(4 * t, min(4 * t + 4, nodes))
            thirds = [j + 3 if j % 2 == 0 else j - 3 for j in targets]
            left = [
                jnp.concatenate([node(n, part) for part in range(2) for n in slot], axis=0)
                for slot in ([j - 2 for j in targets], [j + 2 for j in targets], thirds)
            ]
            rows = [(31 * k + LOW[h] + 4 * t) * 32 for k in range(3)]
            right = [table[r : r + 128, :] for r in rows]
            wide = nt(jnp.concatenate(left, axis=1), jnp.concatenate(right, axis=1))
            wide = wide[: 16 * len(targets)] + wide[16 * len(targets) :]
            chunk = wide[0:16] * m.groupf[0]
            for j in range(1, len(targets)):
                chunk = chunk + wide[16 * j : 16 * j + 16] * m.groupf[j]
            chunks.append(chunk)
        result.append(chunks)
    return result


def top_apply(gathered, table, m):
    left = []
    for g in range(4):
        left.append(jnp.concatenate([gathered[16 * c : 16 * c + 16, :] * m.group[g] for c in range(32)], axis=1))
    right = [
        jnp.concatenate([table[at + 32 * (c // 4) : at + 32 * (c // 4) + 32, :] for c in range(128)], axis=0)
        for at in (0, 1024)
    ]
    wide = nn(jnp.concatenate(left, axis=0), jnp.concatenate(right, axis=1))
    wide = wide[:, :128] + wide[:, 128:]
    row = lax.broadcasted_iota(jnp.int32, (64, 128), 0)
    lane = lax.broadcasted_iota(jnp.int32, (64, 128), 1)
    wide = jnp.where(((row >> 2) & 3) == (lane >> 5), wide, 0.0)
    parts = []
    for g in range(4):
        block = wide[16 * g : 16 * g + 8] + wide[16 * g + 8 : 16 * g + 16]
        parts.append(block[0:4] + block[4:8])
    total = jnp.concatenate(parts, axis=0)
    total = total + pltpu.roll(total, 64, 1)
    return total + pltpu.roll(total, 32, 1)


def down_pass(root, couplings, xfer, m):
    high, low = halves(root)
    first = LOW[3] * 32
    both = nt(jnp.concatenate([high * m.group[0], low * m.group[0]], axis=0), xfer[first : first + 128, :])
    down = [couplings[3][0] + both[:16] + both[16:]]
    for h in (2, 1, 0):
        first = LOW[h] * 32
        split = [halves(d) for d in down]
        down = []
        for t in range(NODES[h] // 4):
            high, low = split[t // 2]
            g = (2 * t) % 4
            left = [high * m.group[g], high * m.group[g + 1], low * m.group[g], low * m.group[g + 1]]
            both = nt(jnp.concatenate(left, axis=0), xfer[first + 128 * t : first + 128 * t + 128, :])
            both = both[:32] + both[32:]
            down.append(couplings[h][t] + both[:16] * m.halff[0] + both[16:] * m.halff[1])
    return down


def build_top(place, xfer_top, own_couple, couple_top, spread, wide_xfer, wide_couple, levels, top, m):
    spread_table(xfer_top[...], spread, wide_xfer, 0)
    row = lax.broadcasted_iota(jnp.int32, (8, 124), 0)
    col = lax.broadcasted_iota(jnp.int32, (8, 124), 1)
    wanted = jnp.zeros((8, 124), jnp.int32) - 1
    for level in range(1, 6):
        wanted = jnp.where(row == level - 1, TOP_COUPLE[level] + (place >> level), wanted)
    pick = (col == wanted).astype(F32).astype(BF16)
    for k in range(3):
        spread_table(nn(pick, couple_top[k]).astype(BF16), spread, wide_couple, 8 * k)
    row = lax.broadcasted_iota(jnp.int32, (32, 128), 0)
    lane = lax.broadcasted_iota(jnp.int32, (32, 128), 1)
    path = (row == (lane & 31)).astype(F32)
    groupf = [lanes_in(32, 32 * g, 32, F32) for g in range(4)]
    slots = []
    for level in range(6):
        if level == 0:
            tables = [own_couple[(31 * k + 30) * 32 : (31 * k + 31) * 32, :].astype(F32) for k in range(3)]
        else:
            tables = [wide_couple[(8 * k + level - 1) * 32 : (8 * k + level) * 32, :] for k in range(3)]
        at = pl.multiple_of((TOP_XFER[level] + (place >> level)) * 32, 32)
        tables.append(wide_xfer[pl.ds(at, 32), :])
        left = tables[0] * groupf[0]
        for g in range(1, 4):
            left = left + tables[g] * groupf[g]
        left = left.astype(BF16)
        high, low = halves(path)
        both = tn(jnp.concatenate([left, left], axis=0), jnp.concatenate([high, low], axis=0))
        slots.append([both[32 * k : 32 * k + 32] for k in range(3)])
        path = both[96:128]
    row = lax.broadcasted_iota(jnp.int32, (256, 128), 0)
    lane = lax.broadcasted_iota(jnp.int32, (256, 128), 1)
    family = ((row >> 6) == (lane >> 5)).astype(F32)
    for level in range(5, -1, -1):
        here = levels[level]
        count = DEVICES >> level
        if level == 5:
            here[...] = jnp.zeros((128, 128), F32)
        else:
            for t in range(count // 8):
                first = (TOP_XFER[level] + 8 * t) * 32
                left = (wide_xfer[first : first + 256, :] * family).astype(BF16)
                high, low = halves(levels[level + 1][128 * t : 128 * t + 128, :])
                here[256 * t : 256 * t + 256, :] = nn(
                    jnp.concatenate([left, left], axis=1), jnp.concatenate([high, low], axis=0)
                )
        node = place >> level
        third = jnp.where(node % 2 == 0, node + 3, node - 3)
        for k, other in enumerate((node - 2, node + 2, third)):
            live = ((other >= 0) & (other < count)).astype(F32)
            at = pl.multiple_of(jnp.clip(other, 0, count - 1) * 32, 32)
            here[pl.ds(at, 32), :] = here[pl.ds(at, 32), :] + slots[level][k] * live
    for c in range(32):
        block = levels[0][128 * c : 128 * c + 32, :] * groupf[0]
        for g in range(1, 4):
            block = block + levels[0][128 * c + 32 * g : 128 * c + 32 * g + 32, :] * groupf[g]
        top[32 * c : 32 * c + 32, :], top[1024 + 32 * c : 1056 + 32 * c, :] = halves(block)


def point_parts(points):
    high = points.astype(BF16).astype(F32)
    rest = points - high
    mid = rest.astype(BF16).astype(F32)
    low = rest - mid
    return jnp.concatenate([high, mid, low, jnp.zeros((7, points.shape[1]), F32)], axis=0).astype(BF16)


def build_tiles(place, parts, cols, counts, from_left, from_right, near_left, near_right, tiles):
    half = lanes_in(8, 0, 64, F32)
    other = 1.0 - half
    blocks = [from_left[192 + 16 * c : 208 + 16 * c, :] for c in range(4)]
    blocks += [parts[:, 128 * c : 128 * c + 128] for c in range(CHUNKS)]
    blocks += [from_right[192 + 16 * c : 208 + 16 * c, :] for c in range(4)]
    row = lax.broadcasted_iota(jnp.int32, (8, 16), 0)
    col = lax.broadcasted_iota(jnp.int32, (8, 16), 1)
    adder = ((col % 3 == row) & (col < 9) & (row < 3)).astype(F32).astype(BF16)
    for c in range(16):
        joined = nn(adder, blocks[c]) * SCALE
        turned = pltpu.roll(joined, 64, 1)
        near_left[2 * c] = joined * half
        near_right[2 * c + 1] = joined * other
        near_left[2 * c + 1] = turned * half
        near_right[2 * c] = turned * other
    row = lax.broadcasted_iota(jnp.int32, (16, 384), 0)
    col = lax.broadcasted_iota(jnp.int32, (16, 384), 1)
    column = ((row % 3 == (col >> 7)) & (row < 9)).astype(F32).astype(BF16)
    lane = lax.broadcasted_iota(jnp.int32, (1, 128), 1)
    base = place * LEAF_DEV - HALO
    for c in range(CHUNKS):
        targets = tn(parts[:, 128 * c : 128 * c + 128], column) * SCALE
        for e in range(2):
            leaf = 2 * c + e
            count = counts[leaf]
            mine = [targets[64 * e : 64 * e + 64, 128 * x : 128 * x + 128] for x in range(3)]
            for pair in range(NEAR // 2):
                first = cols[2 * pair, leaf] - base
                second = cols[2 * pair + 1, leaf] - base
                source = near_left[first] + near_right[second]
                squares = SOFT
                for x in range(3):
                    gap = mine[x] - source[x : x + 1, :]
                    squares = squares + gap * gap
                slot = jnp.where(lane < 64, 2 * pair, 2 * pair + 1)
                gain = jnp.where(slot < count, LOG_GAIN, -2000.0)
                value = jnp.exp2(gain - squares * lax.rsqrt(squares))
                tiles[64 * leaf : 64 * leaf + 64, 128 * pair : 128 * pair + 128] = value.astype(BF16)


def finish(place, signal, from_left, from_right, cols, tiles, down, basis, near_left, near_right, m):
    chunks = [from_left[16 * c : 16 * c + 16, :] for c in range(4)]
    chunks += signal
    chunks += [from_right[16 * c : 16 * c + 16, :] for c in range(4)]
    for c in range(16):
        turned = pltpu.roll(chunks[c].astype(F32), 64, 1).astype(BF16)
        near_left[2 * c] = chunks[c] * m.half[0]
        near_right[2 * c + 1] = chunks[c] * m.half[1]
        near_left[2 * c + 1] = turned * m.half[0]
        near_right[2 * c] = turned * m.half[1]
    base = place * LEAF_DEV - HALO
    result = []
    split = [halves(d) for d in down]
    for c in range(CHUNKS):
        rows = []
        for leaf in (2 * c, 2 * c + 1):
            parts = []
            for pair in range(NEAR // 2):
                first = cols[2 * pair, leaf] - base
                second = cols[2 * pair + 1, leaf] - base
                parts.append(near_left[first] + near_right[second])
            rows.append(jnp.concatenate(parts, axis=1))
        both = nt(jnp.concatenate(rows, axis=0), tiles[128 * c : 128 * c + 128, :])
        high, low = split[c // 2]
        g = (2 * c) % 4
        left = [high * m.group[g], high * m.group[g + 1], low * m.group[g], low * m.group[g + 1]]
        wide = jnp.concatenate([basis[:, 128 * c : 128 * c + 128]] * 4, axis=0)
        far = nn(jnp.concatenate(left, axis=0), wide)
        both = both + far[:32] + far[32:]
        result.append((both[:16] * m.halff[0] + both[16:] * m.halff[1]).astype(BF16))
    return result


def first_kernel(vectors, points, basis, xfer_low, left, right, gather, heights_out, xfer_out, wide):
    m = Masks()
    spread = spread_matrix()
    wide[960:1024, :] = jnp.zeros((64, 128), F32)
    spread_table(xfer_low[...], spread, wide, 0)
    xfer_out[...] = wide[...].astype(BF16)
    signal = [vectors[:, 128 * c : 128 * c + 128] for c in range(CHUNKS)]
    heights, root = up_pass(signal, basis, xfer_out, m)
    write_sends(signal, heights, root, left, right, gather, m)
    parts = point_parts(points[...])
    for c in range(4):
        left[192 + 16 * c : 208 + 16 * c, :] = parts[:, 128 * c : 128 * c + 128]
        right[192 + 16 * c : 208 + 16 * c, :] = parts[:, 512 + 128 * c : 640 + 128 * c]
    store_heights(heights, heights_out)


def store_heights(heights, out):
    at = 0
    for chunks in heights:
        for high, low in chunks:
            out[at : at + 16, :] = high
            out[at + 128 : at + 144, :] = low
            at += 16


def load_heights(source):
    heights, at = [], 0
    for count in (4, 2, 1, 1):
        heights.append(
            [(source[b : b + 16, :], source[b + 128 : b + 144, :]) for b in range(at, at + 16 * count, 16)]
        )
        at += 16 * count
    return heights


def second_kernel(
    cols, counts, vectors, points, basis, xfer, couple, xfer_top, couple_top, heights_in, from_left, from_right, gathered,
    left, right, gather, signal_out, heights_out, tiles, couple_out, top,
    wide, wide_xfer, wide_couple, places_left, places_right, near_left, near_right, *levels,
):
    m = Masks()
    place = lax.axis_index("leaf")
    spread = spread_matrix()
    wide[93 * 32 :, :] = jnp.zeros((96, 128), F32)
    for k in range(3):
        spread_table(couple[k], spread, wide, 31 * k)
    couple_out[...] = wide[...].astype(BF16)
    build_tiles(
        place, point_parts(points[...]), cols, counts, from_left, from_right, places_left, places_right, tiles
    )
    build_top(place, xfer_top, couple_out, couple_top, spread, wide_xfer, wide_couple, levels, top, m)
    heights = load_heights(heights_in)
    signal = [vectors[:, 128 * c : 128 * c + 128] for c in range(CHUNKS)]
    couplings = couple_low(heights, from_left, from_right, couple_out, m)
    down = down_pass(top_apply(gathered, top, m), couplings, xfer, m)
    signal = finish(place, signal, from_left, from_right, cols, tiles, down, basis, near_left, near_right, m)
    for c in range(CHUNKS):
        signal_out[:, 128 * c : 128 * c + 128] = signal[c]
    heights, root = up_pass(signal, basis, xfer, m)
    write_sends(signal, heights, root, left, right, gather, m)
    store_heights(heights, heights_out)


def third_kernel(
    cols, vectors, basis, xfer, couple, top, tiles, heights_in, from_left, from_right, gathered, out, near_left, near_right
):
    m = Masks()
    place = lax.axis_index("leaf")
    heights = load_heights(heights_in)
    signal = [vectors[:, 128 * c : 128 * c + 128] for c in range(CHUNKS)]
    couplings = couple_low(heights, from_left, from_right, couple, m)
    down = down_pass(top_apply(gathered, top, m), couplings, xfer, m)
    signal = finish(place, signal, from_left, from_right, cols, tiles, down, basis, near_left, near_right, m)
    for c in range(CHUNKS):
        out[:, 128 * c : 128 * c + 128] = signal[c]


def call(kernel, name, inputs, scalars, outputs, scratch):
    in_specs = [pl.BlockSpec(memory_space=pltpu.SMEM)] * scalars
    in_specs += [pl.BlockSpec(memory_space=pltpu.VMEM)] * (len(inputs) - scalars)
    return pl.pallas_call(
        kernel,
        out_shape=[jax.ShapeDtypeStruct(shape, BF16) for shape in outputs],
        in_specs=in_specs,
        out_specs=[pl.BlockSpec(memory_space=pltpu.VMEM)] * len(outputs),
        scratch_shapes=scratch,
        compiler_params=pltpu.CompilerParams(vmem_limit_bytes=VMEM_LIMIT),
        name=name,
    )(*inputs)


def exchange(left, right, gather):
    count = lax.axis_size("leaf")
    from_right = lax.ppermute(left, "leaf", [(i + 1, i) for i in range(count - 1)])
    from_left = lax.ppermute(right, "leaf", [(i, i + 1) for i in range(count - 1)])
    blocks = gather.reshape(count, 4, 128)
    gathered = lax.all_to_all(blocks, "leaf", 0, 0, tiled=True)
    return from_left, from_right, gathered.reshape(count * 4, 128)


def body(vectors, points, near_cols, near_count, basis, xfer_low, couple, xfer_top, couple_top):
    left, right, gather, heights, xfer = call(
        first_kernel, "up_first", (vectors, points, basis, xfer_low), 0,
        [(256, 128), (256, 128), (512, 128), (256, 128), (1024, 128)],
        [pltpu.VMEM((1024, 128), F32)],
    )
    from_left, from_right, gathered = exchange(left, right, gather)
    blocks = [pltpu.VMEM((32, 16, 128), BF16)] * 2
    left, right, gather, signal, heights, tiles, couple, top = call(
        second_kernel, "down_up",
        (near_cols, near_count, vectors, points, basis, xfer, couple, xfer_top, couple_top, heights, from_left, from_right,
         gathered), 2,
        [(192, 128), (192, 128), (512, 128), (16, 1024), (256, 128), (1024, 768), (3072, 128), (2048, 128)],
        [pltpu.VMEM((3072, 128), F32), pltpu.VMEM((8128, 128), F32), pltpu.VMEM((768, 128), F32)]
        + [pltpu.VMEM((32, 8, 128), F32)] * 2 + blocks
        + [pltpu.VMEM((4096 >> level, 128), F32) for level in range(6)],
    )
    from_left, from_right, gathered = exchange(left, right, gather)
    (result,) = call(
        third_kernel, "down_last",
        (near_cols, signal, basis, xfer, couple, top, tiles, heights, from_left, from_right, gathered), 1,
        [(16, 1024)], blocks,
    )
    return result


def solution(mesh):
    placed = (
        P("vec", "leaf"),
        P(None, "leaf"),
        P(None, "leaf"),
        P("leaf"),
        P(None, "leaf"),
        P("leaf", None),
        P(None, "leaf", None),
        P(),
        P(),
    )
    return jax.shard_map(body, mesh=mesh, in_specs=placed, out_specs=P("vec", "leaf"), check_vma=False)
```

```python
import math

import jax
import jax.numpy as jnp
from jax import lax
from jax.experimental import pallas as pl
from jax.experimental.pallas import tpu as pltpu
from jax.sharding import PartitionSpec as P

F32 = jnp.float32
BF16 = jnp.bfloat16
HALO = 8
LEAF_DEV = 16
RANK = 32
NEAR = 12
VEC = 16
DEVICES = 128
CHUNKS = 8
LOW = (0, 16, 24, 28, 30)
NODES = (16, 8, 4, 2)
TOP_XFER = (0, 128, 192, 224, 240, 248)
TOP_COUPLE = (0, 0, 64, 96, 112, 120)
SCALE = 4.0 * math.log2(math.e)
SOFT = 0.01 * SCALE * SCALE
LOG_GAIN = math.log2(4.0 / math.sqrt(64 * NEAR))
VMEM_LIMIT = 48 * 1024 * 1024
VMEM_MOST = 60 * 1024 * 1024


def nn(a, b):
    return lax.dot_general(a, b, (((1,), (0,)), ((), ())), preferred_element_type=F32)


def nt(a, b):
    return lax.dot_general(a, b, (((1,), (1,)), ((), ())), preferred_element_type=F32)


def tn(a, b):
    return lax.dot_general(a, b, (((0,), (0,)), ((), ())), preferred_element_type=F32)


def halves(x):
    high = x.astype(BF16)
    return high, (x - high.astype(F32)).astype(BF16)


def lanes_in(rows, lo, size, dtype):
    lane = lax.broadcasted_iota(jnp.int32, (rows, 128), 1)
    return ((lane >= lo) & (lane < lo + size)).astype(F32).astype(dtype)


class Masks:
    def __init__(self):
        self.group = [lanes_in(16, 32 * g, 32, BF16) for g in range(4)]
        self.groupf = [lanes_in(16, 32 * g, 32, F32) for g in range(4)]
        self.half = [lanes_in(16, 64 * g, 64, BF16) for g in range(2)]
        self.halff = [lanes_in(16, 64 * g, 64, F32) for g in range(2)]


def spread_matrix():
    row = lax.broadcasted_iota(jnp.int32, (128, 512), 0)
    col = lax.broadcasted_iota(jnp.int32, (128, 512), 1)
    return (row == ((col >> 7) << 5) + (col & 31)).astype(F32).astype(BF16)


def spread_table(table, spread, out, first):
    count = table.shape[0]
    for c in range(8):
        wide = nn(table[:, 128 * c : 128 * c + 128], spread)
        for q in range(4):
            out[pl.ds(first * 32 + 4 * c + q, count, stride=32), :] = wide[:, 128 * q : 128 * q + 128]


def up_pass(signal, basis, xfer, m):
    total = [0.0] * 4
    for c in range(CHUNKS):
        wide = jnp.concatenate([basis[:, 128 * c : 128 * c + 128]] * 4, axis=0)
        both = nt(jnp.concatenate([signal[c] * m.half[0], signal[c] * m.half[1]], axis=0), wide)
        g = (2 * c) % 4
        total[c // 2] = total[c // 2] + both[:16] * m.groupf[g] + both[16:] * m.groupf[g + 1]
    heights = []
    for h in range(4):
        split = [halves(t) for t in total]
        heights.append(split)
        first = LOW[h] * 32
        if h == 3:
            both = nn(jnp.concatenate(split[0], axis=0), xfer[first : first + 128, :])
            return heights, both[:16] + both[16:]
        count = NODES[h] // 4
        total = [0.0] * max(1, count // 2)
        for t in range(count):
            high, low = split[t]
            left = jnp.concatenate(
                [high * m.half[0], high * m.half[1], low * m.half[0], low * m.half[1]], axis=0
            )
            both = nn(left, xfer[first + 128 * t : first + 128 * t + 128, :])
            both = both[:32] + both[32:]
            g = (2 * t) % 4
            total[t // 2] = total[t // 2] + both[:16] * m.groupf[g] + both[16:] * m.groupf[g + 1]


def write_sends(signal, heights, root, left, right, gather, m):
    for c in range(4):
        left[16 * c : 16 * c + 16, :] = signal[c]
        right[16 * c : 16 * c + 16, :] = signal[c + 4]
    for h in range(4):
        for part in range(2):
            at = 64 * (part + 1) + 16 * h
            left[at : at + 16, :] = heights[h][0][part]
            right[at : at + 16, :] = heights[h][-1][part]
    packed = root[0:4] * m.groupf[0][0:4]
    for g in range(1, 4):
        packed = packed + root[4 * g : 4 * g + 4] * m.groupf[g][0:4]
    block = jnp.concatenate([packed] * 4, axis=0).astype(BF16)
    for q in range(DEVICES // 4):
        gather[16 * q : 16 * q + 16, :] = block


def couple_low(heights, from_left, from_right, table, m):
    result = []
    for h in range(4):
        nodes = NODES[h]
        own = heights[h]
        before = [from_left[at : at + 16, :] for at in (64 + 16 * h, 128 + 16 * h)]
        after = [from_right[at : at + 16, :] for at in (64 + 16 * h, 128 + 16 * h)]

        def node(n, part):
            if n < 0:
                return before[part] * m.group[(nodes + n) % 4]
            if n >= nodes:
                return after[part] * m.group[n - nodes]
            return own[n // 4][part] * m.group[n % 4]

        chunks = []
        for t in range(max(1, nodes // 4)):
            targets = range(4 * t, min(4 * t + 4, nodes))
            thirds = [j + 3 if j % 2 == 0 else j - 3 for j in targets]
            left = [
                jnp.concatenate([node(n, part) for part in range(2) for n in slot], axis=0)
                for slot in ([j - 2 for j in targets], [j + 2 for j in targets], thirds)
            ]
            rows = [(31 * k + LOW[h] + 4 * t) * 32 for k in range(3)]
            right = [table[r : r + 128, :] for r in rows]
            wide = nt(jnp.concatenate(left, axis=1), jnp.concatenate(right, axis=1))
            wide = wide[: 16 * len(targets)] + wide[16 * len(targets) :]
            chunk = wide[0:16] * m.groupf[0]
            for j in range(1, len(targets)):
                chunk = chunk + wide[16 * j : 16 * j + 16] * m.groupf[j]
            chunks.append(chunk)
        result.append(chunks)
    return result


def top_apply(gathered, table, m):
    left = []
    for g in range(4):
        left.append(jnp.concatenate([gathered[16 * c : 16 * c + 16, :] * m.group[g] for c in range(32)], axis=1))
    right = [
        jnp.concatenate([table[at + 32 * (c // 4) : at + 32 * (c // 4) + 32, :] for c in range(128)], axis=0)
        for at in (0, 1024)
    ]
    wide = nn(jnp.concatenate(left, axis=0), jnp.concatenate(right, axis=1))
    wide = wide[:, :128] + wide[:, 128:]
    row = lax.broadcasted_iota(jnp.int32, (64, 128), 0)
    lane = lax.broadcasted_iota(jnp.int32, (64, 128), 1)
    wide = jnp.where(((row >> 2) & 3) == (lane >> 5), wide, 0.0)
    parts = []
    for g in range(4):
        block = wide[16 * g : 16 * g + 8] + wide[16 * g + 8 : 16 * g + 16]
        parts.append(block[0:4] + block[4:8])
    total = jnp.concatenate(parts, axis=0)
    total = total + pltpu.roll(total, 64, 1)
    return total + pltpu.roll(total, 32, 1)


def down_pass(root, couplings, xfer, m):
    high, low = halves(root)
    first = LOW[3] * 32
    both = nt(jnp.concatenate([high * m.group[0], low * m.group[0]], axis=0), xfer[first : first + 128, :])
    down = [couplings[3][0] + both[:16] + both[16:]]
    for h in (2, 1, 0):
        first = LOW[h] * 32
        split = [halves(d) for d in down]
        down = []
        for t in range(NODES[h] // 4):
            high, low = split[t // 2]
            g = (2 * t) % 4
            left = [high * m.group[g], high * m.group[g + 1], low * m.group[g], low * m.group[g + 1]]
            both = nt(jnp.concatenate(left, axis=0), xfer[first + 128 * t : first + 128 * t + 128, :])
            both = both[:32] + both[32:]
            down.append(couplings[h][t] + both[:16] * m.halff[0] + both[16:] * m.halff[1])
    return down


def build_top(place, xfer_top, couple, couple_top, spread, wide_xfer, wide_own, wide_couple, levels, top, m):
    spread_table(xfer_top[...], spread, wide_xfer, 0)
    for k in range(3):
        spread_table(couple[k, 30:31, :], spread, wide_own, k)
    row = lax.broadcasted_iota(jnp.int32, (8, 124), 0)
    col = lax.broadcasted_iota(jnp.int32, (8, 124), 1)
    wanted = jnp.zeros((8, 124), jnp.int32) - 1
    for level in range(1, 6):
        wanted = jnp.where(row == level - 1, TOP_COUPLE[level] + (place >> level), wanted)
    pick = (col == wanted).astype(F32).astype(BF16)
    for k in range(3):
        spread_table(nn(pick, couple_top[k]).astype(BF16), spread, wide_couple, 8 * k)
    row = lax.broadcasted_iota(jnp.int32, (32, 128), 0)
    lane = lax.broadcasted_iota(jnp.int32, (32, 128), 1)
    path = (row == (lane & 31)).astype(F32)
    groupf = [lanes_in(32, 32 * g, 32, F32) for g in range(4)]
    slots = []
    for level in range(6):
        if level == 0:
            tables = [wide_own[32 * k : 32 * k + 32, :] for k in range(3)]
        else:
            tables = [wide_couple[(8 * k + level - 1) * 32 : (8 * k + level) * 32, :] for k in range(3)]
        at = pl.multiple_of((TOP_XFER[level] + (place >> level)) * 32, 32)
        tables.append(wide_xfer[pl.ds(at, 32), :])
        left = tables[0] * groupf[0]
        for g in range(1, 4):
            left = left + tables[g] * groupf[g]
        left = left.astype(BF16)
        high, low = halves(path)
        both = tn(jnp.concatenate([left, left], axis=0), jnp.concatenate([high, low], axis=0))
        slots.append([both[32 * k : 32 * k + 32] for k in range(3)])
        path = both[96:128]
    row = lax.broadcasted_iota(jnp.int32, (256, 128), 0)
    lane = lax.broadcasted_iota(jnp.int32, (256, 128), 1)
    family = ((row >> 6) == (lane >> 5)).astype(F32)
    for level in range(5, -1, -1):
        here = levels[level]
        count = DEVICES >> level
        if level == 5:
            here[...] = jnp.zeros((128, 128), F32)
        else:
            for t in range(count // 8):
                first = (TOP_XFER[level] + 8 * t) * 32
                left = (wide_xfer[first : first + 256, :] * family).astype(BF16)
                high, low = halves(levels[level + 1][128 * t : 128 * t + 128, :])
                here[256 * t : 256 * t + 256, :] = nn(
                    jnp.concatenate([left, left], axis=1), jnp.concatenate([high, low], axis=0)
                )
        node = place >> level
        third = jnp.where(node % 2 == 0, node + 3, node - 3)
        for k, other in enumerate((node - 2, node + 2, third)):
            live = ((other >= 0) & (other < count)).astype(F32)
            at = pl.multiple_of(jnp.clip(other, 0, count - 1) * 32, 32)
            here[pl.ds(at, 32), :] = here[pl.ds(at, 32), :] + slots[level][k] * live
    for c in range(32):
        block = levels[0][128 * c : 128 * c + 32, :] * groupf[0]
        for g in range(1, 4):
            block = block + levels[0][128 * c + 32 * g : 128 * c + 32 * g + 32, :] * groupf[g]
        top[32 * c : 32 * c + 32, :], top[1024 + 32 * c : 1056 + 32 * c, :] = halves(block)


def point_parts(points):
    high = points.astype(BF16).astype(F32)
    rest = points - high
    mid = rest.astype(BF16).astype(F32)
    low = rest - mid
    return jnp.concatenate([high, mid, low, jnp.zeros((7, points.shape[1]), F32)], axis=0).astype(BF16)


def build_tiles(place, parts, cols, counts, from_left, from_right, near_left, near_right, tiles):
    half = lanes_in(8, 0, 64, F32)
    other = 1.0 - half
    blocks = [from_left[192 + 16 * c : 208 + 16 * c, :] for c in range(4)]
    blocks += [parts[:, 128 * c : 128 * c + 128] for c in range(CHUNKS)]
    blocks += [from_right[192 + 16 * c : 208 + 16 * c, :] for c in range(4)]
    row = lax.broadcasted_iota(jnp.int32, (8, 16), 0)
    col = lax.broadcasted_iota(jnp.int32, (8, 16), 1)
    adder = ((col % 3 == row) & (col < 9) & (row < 3)).astype(F32).astype(BF16)
    for c in range(16):
        joined = nn(adder, blocks[c]) * SCALE
        turned = pltpu.roll(joined, 64, 1)
        near_left[2 * c] = joined * half
        near_right[2 * c + 1] = joined * other
        near_left[2 * c + 1] = turned * half
        near_right[2 * c] = turned * other
    row = lax.broadcasted_iota(jnp.int32, (16, 384), 0)
    col = lax.broadcasted_iota(jnp.int32, (16, 384), 1)
    column = ((row % 3 == (col >> 7)) & (row < 9)).astype(F32).astype(BF16)
    lane = lax.broadcasted_iota(jnp.int32, (1, 128), 1)
    base = place * LEAF_DEV - HALO
    for c in range(CHUNKS):
        targets = tn(parts[:, 128 * c : 128 * c + 128], column) * SCALE
        for e in range(2):
            leaf = 2 * c + e
            count = counts[leaf]
            mine = [targets[64 * e : 64 * e + 64, 128 * x : 128 * x + 128] for x in range(3)]
            for pair in range(NEAR // 2):
                first = cols[2 * pair, leaf] - base
                second = cols[2 * pair + 1, leaf] - base
                source = near_left[first] + near_right[second]
                squares = SOFT
                for x in range(3):
                    gap = mine[x] - source[x : x + 1, :]
                    squares = squares + gap * gap
                slot = jnp.where(lane < 64, 2 * pair, 2 * pair + 1)
                gain = jnp.where(slot < count, LOG_GAIN, -2000.0)
                value = jnp.exp2(gain - squares * lax.rsqrt(squares))
                tiles[64 * leaf : 64 * leaf + 64, 128 * pair : 128 * pair + 128] = value.astype(BF16)


def near_field(place, signal, from_left, from_right, cols, tiles, near_left, near_right, m):
    chunks = [from_left[16 * c : 16 * c + 16, :] for c in range(4)]
    chunks += signal
    chunks += [from_right[16 * c : 16 * c + 16, :] for c in range(4)]
    for c in range(16):
        turned = pltpu.roll(chunks[c].astype(F32), 64, 1).astype(BF16)
        near_left[2 * c] = chunks[c] * m.half[0]
        near_right[2 * c + 1] = chunks[c] * m.half[1]
        near_left[2 * c + 1] = turned * m.half[0]
        near_right[2 * c] = turned * m.half[1]
    base = place * LEAF_DEV - HALO
    result = []
    for c in range(CHUNKS):
        rows = []
        for leaf in (2 * c, 2 * c + 1):
            parts = []
            for pair in range(NEAR // 2):
                first = cols[2 * pair, leaf] - base
                second = cols[2 * pair + 1, leaf] - base
                parts.append(near_left[first] + near_right[second])
            rows.append(jnp.concatenate(parts, axis=1))
        both = nt(jnp.concatenate(rows, axis=0), tiles[128 * c : 128 * c + 128, :])
        result.append(both[:16] * m.halff[0] + both[16:] * m.halff[1])
    return result


def far_field(down, basis, near, m):
    result = []
    split = [halves(d) for d in down]
    for c in range(CHUNKS):
        high, low = split[c // 2]
        g = (2 * c) % 4
        left = [high * m.group[g], high * m.group[g + 1], low * m.group[g], low * m.group[g + 1]]
        wide = jnp.concatenate([basis[:, 128 * c : 128 * c + 128]] * 4, axis=0)
        far = nn(jnp.concatenate(left, axis=0), wide)
        far = far[:32] + far[32:]
        far = far[:16] * m.halff[0] + far[16:] * m.halff[1]
        result.append((near[:, 128 * c : 128 * c + 128] + far).astype(BF16))
    return result


def store_heights(heights, out):
    at = 0
    for chunks in heights:
        for high, low in chunks:
            out[at : at + 16, :] = high
            out[at + 128 : at + 144, :] = low
            at += 16


def load_heights(source):
    heights, at = [], 0
    for count in (4, 2, 1, 1):
        heights.append(
            [(source[b : b + 16, :], source[b + 128 : b + 144, :]) for b in range(at, at + 16 * count, 16)]
        )
        at += 16 * count
    return heights


def store_local(near, couplings, near_out, couplings_out):
    for c in range(CHUNKS):
        near_out[:, 128 * c : 128 * c + 128] = near[c]
    at = 0
    for chunks in couplings:
        for chunk in chunks:
            couplings_out[at : at + 16, :] = chunk
            at += 16


def load_couplings(source):
    couplings, at = [], 0
    for count in (4, 2, 1, 1):
        couplings.append([source[b : b + 16, :] for b in range(at, at + 16 * count, 16)])
        at += 16 * count
    return couplings


def chunks_of(signal):
    return [signal[:, 128 * c : 128 * c + 128] for c in range(CHUNKS)]


def fetch(sources, targets, sems):
    copies = [pltpu.make_async_copy(s, t, sems.at[i]) for i, (s, t) in enumerate(zip(sources, targets, strict=True))]
    for copy in copies:
        copy.start()
    return copies


def first_kernel(
    vectors_hbm, points_hbm, basis_hbm, xfer_hbm, left, right, gather, heights_out, xfer_out,
    vectors, points, basis, xfer_low, wide, sems,
):
    copies = fetch((xfer_hbm, vectors_hbm, basis_hbm, points_hbm), (xfer_low, vectors, basis, points), sems)
    m = Masks()
    spread = spread_matrix()
    wide[960:1024, :] = jnp.zeros((64, 128), F32)
    copies[0].wait()
    spread_table(xfer_low[...], spread, wide, 0)
    xfer_out[...] = wide[...].astype(BF16)
    copies[1].wait()
    copies[2].wait()
    signal = chunks_of(vectors)
    heights, root = up_pass(signal, basis, xfer_out, m)
    write_sends(signal, heights, root, left, right, gather, m)
    store_heights(heights, heights_out)
    copies[3].wait()
    parts = point_parts(points[...])
    for c in range(4):
        left[192 + 16 * c : 208 + 16 * c, :] = parts[:, 128 * c : 128 * c + 128]
        right[192 + 16 * c : 208 + 16 * c, :] = parts[:, 512 + 128 * c : 640 + 128 * c]


def table_kernel(
    xfer_hbm, couple_top_hbm, couple_hbm, after, top,
    xfer_top, couple_top, couple, wide, wide_xfer, wide_couple, sems, *levels,
):
    del after
    copies = fetch((xfer_hbm, couple_top_hbm, couple_hbm), (xfer_top, couple_top, couple), sems)
    m = Masks()
    place = lax.axis_index("leaf")
    for copy in copies:
        copy.wait()
    build_top(place, xfer_top, couple, couple_top, spread_matrix(), wide_xfer, wide, wide_couple, levels, top, m)


def local_first_kernel(
    cols_hbm, counts_hbm, vectors_hbm, points_hbm, couple_hbm, from_left, from_right, heights_in,
    tiles, near_out, couplings_out,
    cols, counts, vectors, points, couple, wide, couple_wide, places_left, places_right, near_left, near_right, sems,
):
    copies = fetch(
        (cols_hbm, counts_hbm, vectors_hbm, points_hbm, couple_hbm), (cols, counts, vectors, points, couple), sems
    )
    m = Masks()
    place = lax.axis_index("leaf")
    for copy in copies:
        copy.wait()
    build_tiles(
        place, point_parts(points[...]), cols, counts, from_left, from_right, places_left, places_right, tiles
    )
    spread_couple(couple, wide, couple_wide)
    couplings = couple_low(load_heights(heights_in), from_left, from_right, couple_wide, m)
    near = near_field(place, chunks_of(vectors), from_left, from_right, cols, tiles, near_left, near_right, m)
    store_local(near, couplings, near_out, couplings_out)


def spread_couple(couple, wide, out):
    spread = spread_matrix()
    wide[93 * 32 :, :] = jnp.zeros((96, 128), F32)
    for k in range(3):
        spread_table(couple[k], spread, wide, 31 * k)
    out[...] = wide[...].astype(BF16)


def local_next_kernel(
    cols_hbm, couple_hbm, vectors, tiles, from_left, from_right, heights_in, near_out, couplings_out,
    cols, couple, wide, couple_wide, near_left, near_right, sems,
):
    copies = fetch((couple_hbm, cols_hbm), (couple, cols), sems)
    m = Masks()
    place = lax.axis_index("leaf")
    copies[0].wait()
    spread_couple(couple, wide, couple_wide)
    couplings = couple_low(load_heights(heights_in), from_left, from_right, couple_wide, m)
    copies[1].wait()
    near = near_field(place, chunks_of(vectors), from_left, from_right, cols, tiles, near_left, near_right, m)
    store_local(near, couplings, near_out, couplings_out)


def down_up_kernel(
    basis_hbm, gathered, top, xfer, near, couplings, left, right, gather, signal_out, heights_out, basis, sems
):
    copies = fetch((basis_hbm,), (basis,), sems)
    m = Masks()
    down = down_pass(top_apply(gathered, top, m), load_couplings(couplings), xfer, m)
    copies[0].wait()
    signal = far_field(down, basis, near, m)
    for c in range(CHUNKS):
        signal_out[:, 128 * c : 128 * c + 128] = signal[c]
    heights, root = up_pass(signal, basis, xfer, m)
    write_sends(signal, heights, root, left, right, gather, m)
    store_heights(heights, heights_out)


def down_last_kernel(basis_hbm, gathered, top, xfer, near, couplings, out, basis, sems):
    copies = fetch((basis_hbm,), (basis,), sems)
    m = Masks()
    down = down_pass(top_apply(gathered, top, m), load_couplings(couplings), xfer, m)
    copies[0].wait()
    signal = far_field(down, basis, near, m)
    for c in range(CHUNKS):
        out[:, 128 * c : 128 * c + 128] = signal[c]


def call(kernel, name, arguments, arrays, outputs, scratch, flops, limit=VMEM_LIMIT):
    inputs = tuple(arguments) + tuple(arrays)
    in_specs = [pl.BlockSpec(memory_space=pltpu.HBM)] * len(arguments)
    in_specs += [pl.BlockSpec(memory_space=pltpu.VMEM)] * len(arrays)
    return pl.pallas_call(
        kernel,
        out_shape=[jax.ShapeDtypeStruct(shape, dtype) for shape, dtype in outputs],
        in_specs=in_specs,
        out_specs=[pl.BlockSpec(memory_space=pltpu.VMEM)] * len(outputs),
        scratch_shapes=scratch,
        compiler_params=pltpu.CompilerParams(vmem_limit_bytes=limit),
        cost_estimate=pl.CostEstimate(flops=flops, bytes_accessed=1 << 20, transcendentals=0),
        name=name,
    )(*inputs)


def exchange(left, right, gather):
    count = lax.axis_size("leaf")
    blocks = gather.reshape(count, 4, 128)
    gathered = lax.all_to_all(blocks, "leaf", 0, 0, tiled=True)
    from_right = lax.ppermute(left, "leaf", [(i + 1, i) for i in range(count - 1)])
    from_left = lax.ppermute(right, "leaf", [(i, i + 1) for i in range(count - 1)])
    return from_left, from_right, gathered.reshape(count * 4, 128)


def body(vectors, points, near_cols, near_count, basis, xfer_low, couple, xfer_top, couple_top):
    vm, sm = pltpu.VMEM, pltpu.SMEM
    sems = pltpu.SemaphoreType.DMA
    signal_buf, basis_buf, points_buf = vm((16, 1024), BF16), vm((32, 1024), BF16), vm((3, 1024), F32)
    couple_buf = [vm((3, 31, 1024), BF16), vm((3072, 128), F32)]
    blocks = [vm((32, 16, 128), BF16)] * 2
    sends = [((512, 128), BF16), ((256, 128), BF16)]
    local = [((16, 1024), F32), ((128, 128), F32)]
    left, right, gather, heights, xfer = call(
        first_kernel, "up_first", (vectors, points, basis, xfer_low), (),
        [((256, 128), BF16)] * 2 + sends + [((1024, 128), BF16)],
        [signal_buf, points_buf, basis_buf, vm((30, 1024), BF16), vm((1024, 128), F32), sems((4,))], 1 << 20, VMEM_MOST,
    )
    from_left, from_right, gathered = exchange(left, right, gather)
    (top,) = call(
        table_kernel, "tables", (xfer_top, couple_top, couple, heights), (), [((2048, 128), BF16)],
        [vm((254, 1024), BF16), vm((3, 124, 1024), BF16), vm((3, 31, 1024), BF16), vm((96, 128), F32),
         vm((8128, 128), F32), vm((768, 128), F32), sems((3,))] + [vm((4096 >> level, 128), F32) for level in range(6)],
        1 << 32, VMEM_MOST,
    )
    tiles, near, couplings = call(
        local_first_kernel, "local_first", (near_cols, near_count, vectors, points, couple),
        (from_left, from_right, heights), [((1024, 768), BF16)] + local,
        [sm((12, 16), jnp.int32), sm((16,), jnp.int32), signal_buf, points_buf] + couple_buf + [vm((3072, 128), BF16)]
        + [vm((32, 8, 128), F32)] * 2 + blocks + [sems((5,))], 1 << 32,
    )
    left, right, gather, signal, heights = call(
        down_up_kernel, "down_up", (basis,), (gathered, top, xfer, near, couplings),
        [((192, 128), BF16)] * 2 + [sends[0], ((16, 1024), BF16), sends[1]], [basis_buf, sems((1,))], 1 << 20,
    )
    from_left, from_right, gathered = exchange(left, right, gather)
    near, couplings = call(
        local_next_kernel, "local_next", (near_cols, couple), (signal, tiles, from_left, from_right, heights), local,
        [sm((12, 16), jnp.int32)] + couple_buf + [vm((3072, 128), BF16)] + blocks + [sems((2,))], 1 << 32,
    )
    (result,) = call(
        down_last_kernel, "down_last", (basis,), (gathered, top, xfer, near, couplings), [((16, 1024), BF16)],
        [basis_buf, sems((1,))], 1 << 20,
    )
    return result


def solution(mesh):
    placed = (
        P("vec", "leaf"),
        P(None, "leaf"),
        P(None, "leaf"),
        P("leaf"),
        P(None, "leaf"),
        P("leaf", None),
        P(None, "leaf", None),
        P(),
        P(),
    )
    return jax.shard_map(body, mesh=mesh, in_specs=placed, out_specs=P("vec", "leaf"), check_vma=False)
```

```python
import math

import jax
import jax.numpy as jnp
from jax import lax
from jax.experimental import pallas as pl
from jax.experimental.pallas import tpu as pltpu
from jax.sharding import PartitionSpec as P

F32 = jnp.float32
BF16 = jnp.bfloat16
HALO = 8
LEAF_DEV = 16
RANK = 32
NEAR = 12
VEC = 16
DEVICES = 128
CHUNKS = 8
LOW = (0, 16, 24, 28, 30)
NODES = (16, 8, 4, 2)
TOP_XFER = (0, 128, 192, 224, 240, 248)
TOP_COUPLE = (0, 0, 64, 96, 112, 120)
SCALE = 4.0 * math.log2(math.e)
SOFT = 0.01 * SCALE * SCALE
LOG_GAIN = math.log2(4.0 / math.sqrt(64 * NEAR))
VMEM_LIMIT = 48 * 1024 * 1024
VMEM_MOST = 60 * 1024 * 1024


def nn(a, b):
    return lax.dot_general(a, b, (((1,), (0,)), ((), ())), preferred_element_type=F32)


def nt(a, b):
    return lax.dot_general(a, b, (((1,), (1,)), ((), ())), preferred_element_type=F32)


def tn(a, b):
    return lax.dot_general(a, b, (((0,), (0,)), ((), ())), preferred_element_type=F32)


def halves(x):
    high = x.astype(BF16)
    return high, (x - high.astype(F32)).astype(BF16)


def lanes_in(rows, lo, size, dtype):
    lane = lax.broadcasted_iota(jnp.int32, (rows, 128), 1)
    return ((lane >= lo) & (lane < lo + size)).astype(F32).astype(dtype)


class Masks:
    def __init__(self):
        self.group = [lanes_in(16, 32 * g, 32, BF16) for g in range(4)]
        self.groupf = [lanes_in(16, 32 * g, 32, F32) for g in range(4)]
        self.half = [lanes_in(16, 64 * g, 64, BF16) for g in range(2)]
        self.halff = [lanes_in(16, 64 * g, 64, F32) for g in range(2)]


def repeat_matrix():
    row = lax.broadcasted_iota(jnp.int32, (128, 128), 0)
    col = lax.broadcasted_iota(jnp.int32, (128, 128), 1)
    return ((row & 31) == (col & 31)).astype(F32).astype(BF16)


def spread_table(table, out, first=0):
    table = table.astype(F32)
    row = lax.broadcasted_iota(jnp.int32, (8, 128), 0)
    lane = lax.broadcasted_iota(jnp.int32, (8, 128), 1)
    mine = ((row & 3) == (lane >> 5)).astype(F32)
    upper = row < 4
    repeat = repeat_matrix()
    count = table.shape[0]
    for n in range(0, count, 4):
        parts = []
        for node in range(n, min(n + 4, count)):
            for j in range(4):
                one = table[node : node + 1, 256 * j : 256 * j + 128]
                two = table[node : node + 1, 256 * j + 128 : 256 * j + 256]
                parts.append(jnp.where(upper, one, two) * mine)
        wide = nn(jnp.concatenate(parts, axis=0).astype(BF16), repeat)
        at = (first + n) * 32
        out[at : at + wide.shape[0], :] = wide.astype(out.dtype)


def up_pass(signal, basis, xfer, m):
    total = [0.0] * 4
    for c in range(CHUNKS):
        wide = jnp.concatenate([basis[:, 128 * c : 128 * c + 128]] * 4, axis=0)
        both = nt(jnp.concatenate([signal[c] * m.half[0], signal[c] * m.half[1]], axis=0), wide)
        g = (2 * c) % 4
        total[c // 2] = total[c // 2] + both[:16] * m.groupf[g] + both[16:] * m.groupf[g + 1]
    heights = []
    for h in range(4):
        split = [halves(t) for t in total]
        heights.append(split)
        first = LOW[h] * 32
        if h == 3:
            both = nn(jnp.concatenate(split[0], axis=0), xfer[first : first + 128, :])
            return heights, both[:16] + both[16:]
        count = NODES[h] // 4
        total = [0.0] * max(1, count // 2)
        for t in range(count):
            high, low = split[t]
            left = jnp.concatenate(
                [high * m.half[0], high * m.half[1], low * m.half[0], low * m.half[1]], axis=0
            )
            both = nn(left, xfer[first + 128 * t : first + 128 * t + 128, :])
            both = both[:32] + both[32:]
            g = (2 * t) % 4
            total[t // 2] = total[t // 2] + both[:16] * m.groupf[g] + both[16:] * m.groupf[g + 1]


def write_sends(signal, heights, root, left, right, gather, m):
    for c in range(4):
        left[16 * c : 16 * c + 16, :] = signal[c]
        right[16 * c : 16 * c + 16, :] = signal[c + 4]
    for h in range(4):
        for part in range(2):
            at = 64 * (part + 1) + 16 * h
            left[at : at + 16, :] = heights[h][0][part]
            right[at : at + 16, :] = heights[h][-1][part]
    packed = root[0:4] * m.groupf[0][0:4]
    for g in range(1, 4):
        packed = packed + root[4 * g : 4 * g + 4] * m.groupf[g][0:4]
    block = jnp.concatenate([packed] * 4, axis=0).astype(BF16)
    for q in range(DEVICES // 4):
        gather[16 * q : 16 * q + 16, :] = block


def couple_low(heights, from_left, from_right, table, m):
    result = []
    for h in range(4):
        nodes = NODES[h]
        own = heights[h]
        before = [from_left[at : at + 16, :] for at in (64 + 16 * h, 128 + 16 * h)]
        after = [from_right[at : at + 16, :] for at in (64 + 16 * h, 128 + 16 * h)]

        def node(n, part):
            if n < 0:
                return before[part] * m.group[(nodes + n) % 4]
            if n >= nodes:
                return after[part] * m.group[n - nodes]
            return own[n // 4][part] * m.group[n % 4]

        chunks = []
        for t in range(max(1, nodes // 4)):
            targets = range(4 * t, min(4 * t + 4, nodes))
            thirds = [j + 3 if j % 2 == 0 else j - 3 for j in targets]
            left = [
                jnp.concatenate([node(n, part) for part in range(2) for n in slot], axis=0)
                for slot in ([j - 2 for j in targets], [j + 2 for j in targets], thirds)
            ]
            rows = [(31 * k + LOW[h] + 4 * t) * 32 for k in range(3)]
            right = [table[r : r + 128, :] for r in rows]
            wide = nt(jnp.concatenate(left, axis=1), jnp.concatenate(right, axis=1))
            wide = wide[: 16 * len(targets)] + wide[16 * len(targets) :]
            chunk = wide[0:16] * m.groupf[0]
            for j in range(1, len(targets)):
                chunk = chunk + wide[16 * j : 16 * j + 16] * m.groupf[j]
            chunks.append(chunk)
        result.append(chunks)
    return result


def top_apply(gathered, table, m):
    left = []
    for g in range(4):
        left.append(jnp.concatenate([gathered[16 * c : 16 * c + 16, :] * m.group[g] for c in range(32)], axis=1))
    right = [
        jnp.concatenate([table[at + 32 * (c // 4) : at + 32 * (c // 4) + 32, :] for c in range(128)], axis=0)
        for at in (0, 1024)
    ]
    wide = nn(jnp.concatenate(left, axis=0), jnp.concatenate(right, axis=1))
    wide = wide[:, :128] + wide[:, 128:]
    row = lax.broadcasted_iota(jnp.int32, (64, 128), 0)
    lane = lax.broadcasted_iota(jnp.int32, (64, 128), 1)
    wide = jnp.where(((row >> 2) & 3) == (lane >> 5), wide, 0.0)
    parts = []
    for g in range(4):
        block = wide[16 * g : 16 * g + 8] + wide[16 * g + 8 : 16 * g + 16]
        parts.append(block[0:4] + block[4:8])
    total = jnp.concatenate(parts, axis=0)
    total = total + pltpu.roll(total, 64, 1)
    return total + pltpu.roll(total, 32, 1)


def down_pass(root, couplings, xfer, m):
    high, low = halves(root)
    first = LOW[3] * 32
    both = nt(jnp.concatenate([high * m.group[0], low * m.group[0]], axis=0), xfer[first : first + 128, :])
    down = [couplings[3][0] + both[:16] + both[16:]]
    for h in (2, 1, 0):
        first = LOW[h] * 32
        split = [halves(d) for d in down]
        down = []
        for t in range(NODES[h] // 4):
            high, low = split[t // 2]
            g = (2 * t) % 4
            left = [high * m.group[g], high * m.group[g + 1], low * m.group[g], low * m.group[g + 1]]
            both = nt(jnp.concatenate(left, axis=0), xfer[first + 128 * t : first + 128 * t + 128, :])
            both = both[:32] + both[32:]
            down.append(couplings[h][t] + both[:16] * m.halff[0] + both[16:] * m.halff[1])
    return down


def one_hot(wanted, count):
    col = lax.broadcasted_iota(jnp.int32, wanted.shape, 1)
    return (col == wanted).astype(F32).astype(BF16)


def pack_matrix():
    row = lax.broadcasted_iota(jnp.int32, (512, 512), 0)
    col = lax.broadcasted_iota(jnp.int32, (512, 512), 1)
    same = ((row >> 7) == ((col >> 5) & 3)) & (((row >> 5) & 3) == (col >> 7)) & ((row & 31) == (col & 31))
    return same.astype(F32).astype(BF16)


def pack_xfer(xfer_top, wide_xfer):
    row = lax.broadcasted_iota(jnp.int32, (256, 254), 0)
    at = row & 63
    wanted = jnp.zeros((256, 254), jnp.int32) - 1
    for level in range(4, -1, -1):
        first = 64 - (64 >> level)
        node = TOP_XFER[level] + (row >> 6) * (32 >> level) + at - first
        wanted = jnp.where((at >= first) & (at < first + (32 >> level)), node, wanted)
    packed = nn(one_hot(wanted, 254), xfer_top[...]).astype(BF16)
    pack = pack_matrix()
    for c in range(8):
        left = jnp.concatenate([packed[64 * g : 64 * g + 64, 128 * c : 128 * c + 128] for g in range(4)], axis=1)
        wide = nn(left, pack)
        for q in range(4):
            wide_xfer[pl.ds(4 * c + q, 64, stride=32), :] = wide[:, 128 * q : 128 * q + 128]


def build_top(place, xfer_top, couple, couple_top, wide_xfer, wide_path, levels, top):
    row = lax.broadcasted_iota(jnp.int32, (8, 254), 0)
    wanted = jnp.zeros((8, 254), jnp.int32) - 1
    for level in range(5):
        wanted = jnp.where(row == level, TOP_XFER[level] + (place >> level), wanted)
    rows = [nn(one_hot(wanted, 254), xfer_top[...])]
    row = lax.broadcasted_iota(jnp.int32, (8, 124), 0)
    wanted = jnp.zeros((8, 124), jnp.int32) - 1
    for level in range(1, 6):
        wanted = jnp.where(row == level, TOP_COUPLE[level] + (place >> level), wanted)
    pick = one_hot(wanted, 124)
    row = lax.broadcasted_iota(jnp.int32, (8, 31), 0)
    pick_own = one_hot(jnp.where(row == 0, LOW[4], -1), 31)
    for k in range(3):
        rows.append(nn(pick, couple_top[k]) + nn(pick_own, couple[k]))
    spread_table(jnp.concatenate(rows, axis=0), wide_path)

    row = lax.broadcasted_iota(jnp.int32, (32, 128), 0)
    lane = lax.broadcasted_iota(jnp.int32, (32, 128), 1)
    repeat = (row == (lane & 31)).astype(F32).astype(BF16)
    repeat = jnp.concatenate([repeat, repeat], axis=0)
    groupf = [lanes_in(32, 32 * g, 32, F32) for g in range(4)]
    path = (lax.broadcasted_iota(jnp.int32, (32, 32), 0) == lax.broadcasted_iota(jnp.int32, (32, 32), 1)).astype(F32)
    slots = []
    for level in range(6):
        at = [level, 8 + level, 16 + level, 24 + level]
        right = wide_path[32 * at[0] : 32 * at[0] + 32, :] * groupf[0]
        for g in range(1, 4):
            right = right + wide_path[32 * at[g] : 32 * at[g] + 32, :] * groupf[g]
        both = nn(jnp.concatenate(halves(path), axis=0), right.astype(BF16))
        both = both[:32] + both[32:]
        path = both[:, 0:32]
        turned = tn(jnp.concatenate(halves(both), axis=0), repeat)
        slots.append([turned[32 * k + 32 : 32 * k + 64] for k in range(3)])

    row = lax.broadcasted_iota(jnp.int32, (128, 128), 0)
    diagonal = ((row >> 5) == (lax.broadcasted_iota(jnp.int32, (128, 128), 1) >> 5)).astype(F32).astype(BF16)
    for level in range(5, -1, -1):
        here = levels[level]
        blocks = 32 >> level
        if level == 5:
            here[...] = jnp.zeros((32, 128), F32)
        else:
            first = 64 - (64 >> level)
            for b in range(blocks // 2):
                high, low = halves(levels[level + 1][32 * b : 32 * b + 32, :])
                right = [jnp.concatenate([part] * 4, axis=0) * diagonal for part in (high, low)]
                left = wide_xfer[(first + 2 * b) * 32 : (first + 2 * b + 2) * 32, :].astype(BF16)
                here[64 * b : 64 * b + 64, :] = nn(
                    jnp.concatenate([left, left], axis=1), jnp.concatenate(right, axis=0)
                )
        node = place >> level
        third = jnp.where(node % 2 == 0, node + 3, node - 3)
        for k, other in enumerate((node - 2, node + 2, third)):
            other = jnp.where((other >= 0) & (other < 4 * blocks), other, -blocks)
            at = pl.multiple_of((other & (blocks - 1)) * 32, 32)
            mine = jnp.where((lane >> 5) == (other >> (5 - level)), slots[level][k], 0.0)
            here[pl.ds(at, 32), :] = here[pl.ds(at, 32), :] + mine
    top[:1024, :], top[1024:, :] = halves(levels[0][...])


def point_parts(points):
    high = points.astype(BF16).astype(F32)
    rest = points - high
    mid = rest.astype(BF16).astype(F32)
    low = rest - mid
    return jnp.concatenate([high, mid, low, jnp.zeros((7, points.shape[1]), F32)], axis=0).astype(BF16)


def build_tiles(place, parts, cols, counts, from_left, from_right, near_left, near_right, tiles):
    half = lanes_in(8, 0, 64, F32)
    other = 1.0 - half
    blocks = [from_left[192 + 16 * c : 208 + 16 * c, :] for c in range(4)]
    blocks += [parts[:, 128 * c : 128 * c + 128] for c in range(CHUNKS)]
    blocks += [from_right[192 + 16 * c : 208 + 16 * c, :] for c in range(4)]
    row = lax.broadcasted_iota(jnp.int32, (8, 16), 0)
    col = lax.broadcasted_iota(jnp.int32, (8, 16), 1)
    adder = ((col % 3 == row) & (col < 9) & (row < 3)).astype(F32).astype(BF16)
    for c in range(16):
        joined = nn(adder, blocks[c]) * SCALE
        turned = pltpu.roll(joined, 64, 1)
        near_left[2 * c] = joined * half
        near_right[2 * c + 1] = joined * other
        near_left[2 * c + 1] = turned * half
        near_right[2 * c] = turned * other
    row = lax.broadcasted_iota(jnp.int32, (16, 384), 0)
    col = lax.broadcasted_iota(jnp.int32, (16, 384), 1)
    column = ((row % 3 == (col >> 7)) & (row < 9)).astype(F32).astype(BF16)
    lane = lax.broadcasted_iota(jnp.int32, (1, 128), 1)
    base = place * LEAF_DEV - HALO
    for c in range(CHUNKS):
        targets = tn(parts[:, 128 * c : 128 * c + 128], column) * SCALE
        for e in range(2):
            leaf = 2 * c + e
            count = counts[leaf]
            mine = [targets[64 * e : 64 * e + 64, 128 * x : 128 * x + 128] for x in range(3)]
            for pair in range(NEAR // 2):
                first = cols[2 * pair, leaf] - base
                second = cols[2 * pair + 1, leaf] - base
                source = near_left[first] + near_right[second]
                squares = SOFT
                for x in range(3):
                    gap = mine[x] - source[x : x + 1, :]
                    squares = squares + gap * gap
                slot = jnp.where(lane < 64, 2 * pair, 2 * pair + 1)
                gain = jnp.where(slot < count, LOG_GAIN, -2000.0)
                value = jnp.exp2(gain - squares * lax.rsqrt(squares))
                tiles[64 * leaf : 64 * leaf + 64, 128 * pair : 128 * pair + 128] = value.astype(BF16)


def near_field(place, signal, from_left, from_right, cols, tiles, near_left, near_right, m):
    chunks = [from_left[16 * c : 16 * c + 16, :] for c in range(4)]
    chunks += signal
    chunks += [from_right[16 * c : 16 * c + 16, :] for c in range(4)]
    for c in range(16):
        turned = pltpu.roll(chunks[c].astype(F32), 64, 1).astype(BF16)
        near_left[2 * c] = chunks[c] * m.half[0]
        near_right[2 * c + 1] = chunks[c] * m.half[1]
        near_left[2 * c + 1] = turned * m.half[0]
        near_right[2 * c] = turned * m.half[1]
    base = place * LEAF_DEV - HALO
    result = []
    for c in range(CHUNKS):
        rows = []
        for leaf in (2 * c, 2 * c + 1):
            parts = []
            for pair in range(NEAR // 2):
                first = cols[2 * pair, leaf] - base
                second = cols[2 * pair + 1, leaf] - base
                parts.append(near_left[first] + near_right[second])
            rows.append(jnp.concatenate(parts, axis=1))
        both = nt(jnp.concatenate(rows, axis=0), tiles[128 * c : 128 * c + 128, :])
        result.append(both[:16] * m.halff[0] + both[16:] * m.halff[1])
    return result


def far_field(down, basis, near, m):
    result = []
    split = [halves(d) for d in down]
    for c in range(CHUNKS):
        high, low = split[c // 2]
        g = (2 * c) % 4
        left = [high * m.group[g], high * m.group[g + 1], low * m.group[g], low * m.group[g + 1]]
        wide = jnp.concatenate([basis[:, 128 * c : 128 * c + 128]] * 4, axis=0)
        far = nn(jnp.concatenate(left, axis=0), wide)
        far = far[:32] + far[32:]
        far = far[:16] * m.halff[0] + far[16:] * m.halff[1]
        result.append((near[:, 128 * c : 128 * c + 128] + far).astype(BF16))
    return result


def store_heights(heights, out):
    at = 0
    for chunks in heights:
        for high, low in chunks:
            out[at : at + 16, :] = high
            out[at + 128 : at + 144, :] = low
            at += 16


def load_heights(source):
    heights, at = [], 0
    for count in (4, 2, 1, 1):
        heights.append(
            [(source[b : b + 16, :], source[b + 128 : b + 144, :]) for b in range(at, at + 16 * count, 16)]
        )
        at += 16 * count
    return heights


def store_local(near, couplings, near_out, couplings_out):
    for c in range(CHUNKS):
        near_out[:, 128 * c : 128 * c + 128] = near[c]
    at = 0
    for chunks in couplings:
        for chunk in chunks:
            couplings_out[at : at + 16, :] = chunk
            at += 16


def load_couplings(source):
    couplings, at = [], 0
    for count in (4, 2, 1, 1):
        couplings.append([source[b : b + 16, :] for b in range(at, at + 16 * count, 16)])
        at += 16 * count
    return couplings


def chunks_of(signal):
    return [signal[:, 128 * c : 128 * c + 128] for c in range(CHUNKS)]


def fetch(sources, targets, sems):
    copies = [pltpu.make_async_copy(s, t, sems.at[i]) for i, (s, t) in enumerate(zip(sources, targets, strict=True))]
    for copy in copies:
        copy.start()
    return copies


def first_kernel(
    vectors_hbm, points_hbm, basis_hbm, xfer_hbm, left, right, gather, heights_out, xfer_out,
    vectors, points, basis, xfer_low, sems,
):
    copies = fetch((xfer_hbm, vectors_hbm, basis_hbm, points_hbm), (xfer_low, vectors, basis, points), sems)
    m = Masks()
    xfer_out[960:1024, :] = jnp.zeros((64, 128), BF16)
    copies[0].wait()
    spread_table(xfer_low[...], xfer_out)
    copies[1].wait()
    copies[2].wait()
    signal = chunks_of(vectors)
    heights, root = up_pass(signal, basis, xfer_out, m)
    write_sends(signal, heights, root, left, right, gather, m)
    store_heights(heights, heights_out)
    copies[3].wait()
    parts = point_parts(points[...])
    for c in range(4):
        left[192 + 16 * c : 208 + 16 * c, :] = parts[:, 128 * c : 128 * c + 128]
        right[192 + 16 * c : 208 + 16 * c, :] = parts[:, 512 + 128 * c : 640 + 128 * c]


def table_kernel(
    xfer_hbm, couple_top_hbm, couple_hbm, after, top,
    xfer_top, couple_top, couple, wide_xfer, wide_path, sems, *levels,
):
    del after
    copies = fetch((xfer_hbm, couple_hbm, couple_top_hbm), (xfer_top, couple, couple_top), sems)
    copies[0].wait()
    pack_xfer(xfer_top, wide_xfer)
    copies[1].wait()
    copies[2].wait()
    build_top(lax.axis_index("leaf"), xfer_top, couple, couple_top, wide_xfer, wide_path, levels, top)


def local_first_kernel(
    cols_hbm, counts_hbm, vectors_hbm, points_hbm, couple_hbm, from_left, from_right, heights_in,
    tiles, near_out, couplings_out,
    cols, counts, vectors, points, couple, couple_wide, places_left, places_right, near_left, near_right, sems,
):
    copies = fetch(
        (cols_hbm, counts_hbm, vectors_hbm, points_hbm, couple_hbm), (cols, counts, vectors, points, couple), sems
    )
    m = Masks()
    place = lax.axis_index("leaf")
    for copy in copies:
        copy.wait()
    build_tiles(
        place, point_parts(points[...]), cols, counts, from_left, from_right, places_left, places_right, tiles
    )
    spread_couple(couple, couple_wide)
    couplings = couple_low(load_heights(heights_in), from_left, from_right, couple_wide, m)
    near = near_field(place, chunks_of(vectors), from_left, from_right, cols, tiles, near_left, near_right, m)
    store_local(near, couplings, near_out, couplings_out)


def spread_couple(couple, out):
    out[93 * 32 :, :] = jnp.zeros((96, 128), BF16)
    for k in range(3):
        spread_table(couple[k], out, 31 * k)


def spread_kernel(couple_hbm, after, out, couple, sems):
    del after
    fetch((couple_hbm,), (couple,), sems)[0].wait()
    spread_couple(couple, out)


def local_next_kernel(
    cols_hbm, couple_wide, vectors, tiles, from_left, from_right, heights_in, near_out, couplings_out,
    cols, near_left, near_right, sems,
):
    copies = fetch((cols_hbm,), (cols,), sems)
    m = Masks()
    place = lax.axis_index("leaf")
    couplings = couple_low(load_heights(heights_in), from_left, from_right, couple_wide, m)
    copies[0].wait()
    near = near_field(place, chunks_of(vectors), from_left, from_right, cols, tiles, near_left, near_right, m)
    store_local(near, couplings, near_out, couplings_out)


def down_up_kernel(
    basis_hbm, gathered, top, xfer, near, couplings, left, right, gather, signal_out, heights_out, basis, sems
):
    copies = fetch((basis_hbm,), (basis,), sems)
    m = Masks()
    down = down_pass(top_apply(gathered, top, m), load_couplings(couplings), xfer, m)
    copies[0].wait()
    signal = far_field(down, basis, near, m)
    for c in range(CHUNKS):
        signal_out[:, 128 * c : 128 * c + 128] = signal[c]
    heights, root = up_pass(signal, basis, xfer, m)
    write_sends(signal, heights, root, left, right, gather, m)
    store_heights(heights, heights_out)


def down_last_kernel(basis_hbm, gathered, top, xfer, near, couplings, out, basis, sems):
    copies = fetch((basis_hbm,), (basis,), sems)
    m = Masks()
    down = down_pass(top_apply(gathered, top, m), load_couplings(couplings), xfer, m)
    copies[0].wait()
    signal = far_field(down, basis, near, m)
    for c in range(CHUNKS):
        out[:, 128 * c : 128 * c + 128] = signal[c]


def call(kernel, name, arguments, arrays, outputs, scratch, flops, limit=VMEM_LIMIT):
    inputs = tuple(arguments) + tuple(arrays)
    in_specs = [pl.BlockSpec(memory_space=pltpu.HBM)] * len(arguments)
    in_specs += [pl.BlockSpec(memory_space=pltpu.VMEM)] * len(arrays)
    return pl.pallas_call(
        kernel,
        out_shape=[jax.ShapeDtypeStruct(shape, dtype) for shape, dtype in outputs],
        in_specs=in_specs,
        out_specs=[pl.BlockSpec(memory_space=pltpu.VMEM)] * len(outputs),
        scratch_shapes=scratch,
        compiler_params=pltpu.CompilerParams(vmem_limit_bytes=limit),
        cost_estimate=pl.CostEstimate(flops=flops, bytes_accessed=1 << 20, transcendentals=0),
        name=name,
    )(*inputs)


def exchange(left, right, gather):
    count = lax.axis_size("leaf")
    blocks = gather.reshape(count, 4, 128)
    quarter = count // 4
    order = [g * quarter + b for b in range(quarter) for g in range(4)]
    gathered = lax.all_to_all(blocks, "leaf", 0, 0, tiled=True, axis_index_groups=[order])
    from_right = lax.ppermute(left, "leaf", [(i + 1, i) for i in range(count - 1)])
    from_left = lax.ppermute(right, "leaf", [(i, i + 1) for i in range(count - 1)])
    return from_left, from_right, gathered.reshape(count * 4, 128)


def body(vectors, points, near_cols, near_count, basis, xfer_low, couple, xfer_top, couple_top):
    vm, sm = pltpu.VMEM, pltpu.SMEM
    sems = pltpu.SemaphoreType.DMA
    signal_buf, basis_buf, points_buf = vm((16, 1024), BF16), vm((32, 1024), BF16), vm((3, 1024), F32)
    couple_buf = [vm((3, 31, 1024), BF16)]
    blocks = [vm((32, 16, 128), BF16)] * 2
    sends = [((512, 128), BF16), ((256, 128), BF16)]
    local = [((16, 1024), F32), ((128, 128), F32)]
    left, right, gather, heights, xfer = call(
        first_kernel, "up_first", (vectors, points, basis, xfer_low), (),
        [((256, 128), BF16)] * 2 + sends + [((1024, 128), BF16)],
        [signal_buf, points_buf, basis_buf, vm((30, 1024), BF16), sems((4,))], 1 << 20, VMEM_MOST,
    )
    from_left, from_right, gathered = exchange(left, right, gather)
    (top,) = call(
        table_kernel, "tables", (xfer_top, couple_top, couple, heights), (), [((2048, 128), BF16)],
        [vm((254, 1024), BF16), vm((3, 124, 1024), BF16), vm((3, 31, 1024), BF16), vm((2048, 128), F32),
         vm((1024, 128), F32), sems((3,))] + [vm((1024 >> level, 128), F32) for level in range(6)],
        1 << 32, VMEM_MOST,
    )
    tiles, near, couplings = call(
        local_first_kernel, "local_first", (near_cols, near_count, vectors, points, couple),
        (from_left, from_right, heights), [((1024, 768), BF16)] + local,
        [sm((12, 16), jnp.int32), sm((16,), jnp.int32), signal_buf, points_buf] + couple_buf + [vm((3072, 128), BF16)]
        + [vm((32, 8, 128), F32)] * 2 + blocks + [sems((5,))], 1 << 32,
    )
    left, right, gather, signal, heights = call(
        down_up_kernel, "down_up", (basis,), (gathered, top, xfer, near, couplings),
        [((192, 128), BF16)] * 2 + [sends[0], ((16, 1024), BF16), sends[1]], [basis_buf, sems((1,))], 1 << 20,
    )
    from_left, from_right, gathered = exchange(left, right, gather)
    (couple_wide,) = call(
        spread_kernel, "spread", (couple, heights), (), [((3072, 128), BF16)], couple_buf + [sems((1,))], 1 << 32
    )
    near, couplings = call(
        local_next_kernel, "local_next", (near_cols,),
        (couple_wide, signal, tiles, from_left, from_right, heights), local,
        [sm((12, 16), jnp.int32)] + blocks + [sems((1,))], 1 << 32,
    )
    (result,) = call(
        down_last_kernel, "down_last", (basis,), (gathered, top, xfer, near, couplings), [((16, 1024), BF16)],
        [basis_buf, sems((1,))], 1 << 20,
    )
    return result


def solution(mesh):
    placed = (
        P("vec", "leaf"),
        P(None, "leaf"),
        P(None, "leaf"),
        P("leaf"),
        P(None, "leaf"),
        P("leaf", None),
        P(None, "leaf", None),
        P(),
        P(),
    )
    return jax.shard_map(body, mesh=mesh, in_specs=placed, out_specs=P("vec", "leaf"), check_vma=False)
```

```python
import math

import jax
import jax.numpy as jnp
from jax import lax
from jax.experimental import pallas as pl
from jax.experimental.pallas import tpu as pltpu
from jax.sharding import PartitionSpec as P

F32 = jnp.float32
BF16 = jnp.bfloat16
HALO = 8
LEAF_DEV = 16
RANK = 32
NEAR = 12
VEC = 16
DEVICES = 128
CHUNKS = 8
LOW = (0, 16, 24, 28, 30)
NODES = (16, 8, 4, 2)
TOP_XFER = (0, 128, 192, 224, 240, 248)
TOP_COUPLE = (0, 0, 64, 96, 112, 120)
SCALE = 4.0 * math.log2(math.e)
SOFT = 0.01 * SCALE * SCALE
LOG_GAIN = math.log2(4.0 / math.sqrt(64 * NEAR))
VMEM_LIMIT = 48 * 1024 * 1024


def nn(a, b):
    return lax.dot_general(a, b, (((1,), (0,)), ((), ())), preferred_element_type=F32)


def nt(a, b):
    return lax.dot_general(a, b, (((1,), (1,)), ((), ())), preferred_element_type=F32)


def tn(a, b):
    return lax.dot_general(a, b, (((0,), (0,)), ((), ())), preferred_element_type=F32)


def halves(x):
    high = x.astype(BF16)
    return high, (x - high.astype(F32)).astype(BF16)


def lanes_in(rows, lo, size, dtype):
    lane = lax.broadcasted_iota(jnp.int32, (rows, 128), 1)
    return ((lane >= lo) & (lane < lo + size)).astype(F32).astype(dtype)


class Masks:
    def __init__(self):
        self.group = [lanes_in(16, 32 * g, 32, BF16) for g in range(4)]
        self.groupf = [lanes_in(16, 32 * g, 32, F32) for g in range(4)]
        self.half = [lanes_in(16, 64 * g, 64, BF16) for g in range(2)]
        self.halff = [lanes_in(16, 64 * g, 64, F32) for g in range(2)]


def repeat_matrix():
    row = lax.broadcasted_iota(jnp.int32, (128, 128), 0)
    col = lax.broadcasted_iota(jnp.int32, (128, 128), 1)
    return ((row & 31) == (col & 31)).astype(F32).astype(BF16)


def spread_rows(table, nodes):
    row = lax.broadcasted_iota(jnp.int32, (8, 128), 0)
    lane = lax.broadcasted_iota(jnp.int32, (8, 128), 1)
    mine = ((row & 3) == (lane >> 5)).astype(F32)
    parts = []
    for node in nodes:
        for j in range(4):
            one = table[node : node + 1, 256 * j : 256 * j + 128]
            two = table[node : node + 1, 256 * j + 128 : 256 * j + 256]
            parts.append(jnp.where(row < 4, one, two) * mine)
    return jnp.concatenate(parts, axis=0).astype(BF16)


def spread_table(table, out, first=0):
    table = table.astype(F32)
    repeat = repeat_matrix()
    count = table.shape[0]
    for n in range(0, count, 4):
        wide = nn(spread_rows(table, range(n, min(n + 4, count))), repeat)
        at = (first + n) * 32
        out[at : at + wide.shape[0], :] = wide.astype(out.dtype)


def spread_couple(couple, out):
    tables = [couple[k].astype(F32) for k in range(3)]
    row = lax.broadcasted_iota(jnp.int32, (384, 128), 0)
    col = lax.broadcasted_iota(jnp.int32, (384, 128), 1)
    fold = (((row & 31) == (col & 31)) & ((row >> 7) == (col >> 5))).astype(F32).astype(BF16)
    for n in range(0, 31, 4):
        nodes = range(n, min(n + 4, 31))
        wide = nn(jnp.concatenate([spread_rows(table, nodes) for table in tables], axis=1), fold)
        out[32 * n : 32 * n + wide.shape[0], :] = wide.astype(BF16)
    out[992:1024, :] = jnp.zeros((32, 128), BF16)


def up_pass(signal, basis, xfer, m):
    nodes = []
    for c in range(CHUNKS):
        wide = jnp.concatenate([basis[:, 128 * c : 128 * c + 128]] * 4, axis=0)
        both = nt(jnp.concatenate([signal[c] * m.half[0], signal[c] * m.half[1]], axis=0), wide)
        nodes += [both[:16], both[16:]]
    heights = []
    for h in range(4):
        split = [halves(node) for node in nodes]
        heights.append(split)
        nodes = []
        for t in range(0, NODES[h], 4):
            family = split[t : t + 4]
            left = [
                family[i][part] * m.group[i] + family[i + 1][part] * m.group[i + 1]
                for part in range(2)
                for i in range(0, len(family), 2)
            ]
            first = (LOW[h] + t) * 32
            both = nn(jnp.concatenate(left, axis=0), xfer[first : first + 128, :])
            size = 8 * len(family)
            both = both[:size] + both[size:]
            nodes += [both[i : i + 16] for i in range(0, size, 16)]
    return heights, nodes[0]


def exchange_rows(place, to_left, to_right, near, far, first):
    even = (place & 1) == 0
    for i, (one, two) in enumerate(zip(to_left, to_right, strict=True)):
        at = first + 16 * i
        near[at : at + 16, :] = jnp.where(even, two, one)
        far[at : at + 16, :] = jnp.where(even, one, two)


def sides(place, near, far, left, right):
    even = (place & 1) == 0
    for at in range(0, near.shape[0], 16):
        one, two = near[at : at + 16, :], far[at : at + 16, :]
        left[at : at + 16, :] = jnp.where(even, two, one)
        right[at : at + 16, :] = jnp.where(even, one, two)


def write_sends(place, signal, heights, root, weights, near, far, gather):
    exchange_rows(place, signal[:4], signal[4:], near, far, 0)
    to_left = [heights[h][i][part] for h in range(4) for i in (0, 1) for part in range(2)]
    to_right = [heights[h][i][part] for h in range(4) for i in (-2, -1) for part in range(2)]
    exchange_rows(place, to_left, to_right, near, far, 64)
    both = nn(jnp.concatenate([part[:, 0:64] for part in halves(root)], axis=0), weights[...])
    both = both[:16] + both[16:]
    row = lax.broadcasted_iota(jnp.int32, (16, 128), 0)
    mine = ((row >> 2) == (lax.broadcasted_iota(jnp.int32, (16, 128), 1) >> 5)).astype(F32)
    packed = []
    for level in range(6):
        one = both[:, 128 * level : 128 * level + 128] * mine
        one = one[0:8] + one[8:16]
        packed.append(one[0:4] + one[4:8])
    packed = jnp.concatenate(packed, axis=0)
    packed = jnp.concatenate([packed] * 3 + [jnp.zeros((56, 128), F32)], axis=0).astype(BF16)
    gather[...] = nn(relation(place), packed).astype(BF16)


def couple_low(heights, from_left, from_right, table, m):
    result = []
    for h in range(4):
        count = NODES[h]

        def node(n, part, h=h, count=count):
            if n < 0:
                at = 64 + (4 * h + 2 * (n + 2) + part) * 16
                return from_left[at : at + 16, :]
            if n >= count:
                at = 64 + (4 * h + 2 * (n - count) + part) * 16
                return from_right[at : at + 16, :]
            return heights[h][n][part]

        chunks = []
        for t in range(0, count, 4):
            targets = range(t, min(t + 4, count))
            left = []
            for part in range(2):
                for j in targets:
                    third = j + 3 if j % 2 == 0 else j - 3
                    slots = (node(j - 2, part), node(j + 2, part), node(third, part))
                    left.append(slots[0] * m.group[0] + slots[1] * m.group[1] + slots[2] * m.group[2])
            first = (LOW[h] + t) * 32
            wide = nt(jnp.concatenate(left, axis=0), table[first : first + 128, :])
            wide = wide[: 16 * len(targets)] + wide[16 * len(targets) :]
            chunk = wide[0:16] * m.groupf[0]
            for j in range(1, len(targets)):
                chunk = chunk + wide[16 * j : 16 * j + 16] * m.groupf[j]
            chunks.append(chunk)
        result.append(chunks)
    return result


def top_apply(place, gathered, top):
    sums = tn(relation(place), gathered[...])
    row = lax.broadcasted_iota(jnp.int32, (16, 128), 0)
    mine = ((row >> 2) == (lax.broadcasted_iota(jnp.int32, (16, 128), 1) >> 5)).astype(F32)
    left = [jnp.concatenate([sums[4 * i : 4 * i + 4]] * 4, axis=0) * mine for i in range(18)]
    left = halves(jnp.concatenate(left, axis=1))
    total = nt(jnp.concatenate(left, axis=0), top[...])
    total = jnp.concatenate([total[:16] + total[16:], jnp.zeros((16, 64), F32)], axis=1)
    total = total + pltpu.roll(total, 64, 1)
    return total + pltpu.roll(total, 32, 1)


def down_pass(root, couplings, xfer, m):
    high, low = halves(root)
    first = LOW[3] * 32
    both = nt(jnp.concatenate([high * m.group[0], low * m.group[0]], axis=0), xfer[first : first + 128, :])
    down = [couplings[3][0] + both[:16] + both[16:]]
    for h in (2, 1, 0):
        first = LOW[h] * 32
        split = [halves(d) for d in down]
        down = []
        for t in range(NODES[h] // 4):
            high, low = split[t // 2]
            g = (2 * t) % 4
            left = [high * m.group[g], high * m.group[g + 1], low * m.group[g], low * m.group[g + 1]]
            both = nt(jnp.concatenate(left, axis=0), xfer[first + 128 * t : first + 128 * t + 128, :])
            both = both[:32] + both[32:]
            down.append(couplings[h][t] + both[:16] * m.halff[0] + both[16:] * m.halff[1])
    return down


def one_hot(wanted, count):
    col = lax.broadcasted_iota(jnp.int32, wanted.shape, 1)
    return (col == wanted).astype(F32).astype(BF16)


def pick_rows(table, level_rows):
    count = table.shape[0]
    row = lax.broadcasted_iota(jnp.int32, (8, count), 0)
    col = lax.broadcasted_iota(jnp.int32, (8, count), 1)
    wanted = jnp.zeros((8, count), jnp.int32) - 1
    for level, at in level_rows.items():
        wanted = jnp.where(row == level, at, wanted)
    return nn((col == wanted).astype(F32).astype(BF16), table)


def build_paths(place, xfer_top, wide_path, paths, weights):
    rows = pick_rows(xfer_top[...], {level: TOP_XFER[level] + (place >> level) for level in range(5)})
    spread_table(rows[0:5], wide_path)
    row = lax.broadcasted_iota(jnp.int32, (32, 128), 0)
    lane = lax.broadcasted_iota(jnp.int32, (32, 128), 1)
    step = [wide_path[32 * level : 32 * level + 32, :] for level in range(5)]

    def times(left, right):
        both = nn(jnp.concatenate([part[:, 0:32] for part in halves(left)], axis=0), right)
        return both[:32] + both[32:]

    pair = halves(nn(step[2][:, 0:32], step[3]))
    second = nn(step[0][:, 0:32], step[1])
    fourth = times(second, jnp.concatenate(pair, axis=1))
    fourth = fourth[:, :128] + fourth[:, 128:]
    products = [(row == (lane & 31)).astype(F32), step[0].astype(F32), second, times(second, step[2]), fourth]
    products.append(times(fourth, step[4]))
    for level in range(6):
        paths[32 * level : 32 * level + 32, :] = products[level]
        high, low = halves(products[level])
        weights[0:32, 128 * level : 128 * level + 128] = high
        weights[32:64, 128 * level : 128 * level + 128] = low


def build_top(place, couple, couple_top, paths, wide_couple, top):
    at = {level: TOP_COUPLE[level] + (place >> level) for level in range(1, 6)}
    for k in range(3):
        rows = pick_rows(couple_top[k], at) + pick_rows(couple[k], {0: LOW[4]})
        spread_table(rows[0:6], wide_couple, 6 * k)
    for level in range(6):
        high, low = halves(paths[32 * level : 32 * level + 32, :])
        left = jnp.concatenate([high[:, 0:32], low[:, 0:32]], axis=0)
        right = [wide_couple[(6 * k + level) * 32 : (6 * k + level + 1) * 32, :] for k in range(3)]
        both = nn(left, jnp.concatenate(right, axis=1))
        high, low = halves(both[:32] + both[32:])
        for k in range(3):
            at = (6 * k + level) * 128
            top[0:32, at : at + 128] = high[:, 128 * k : 128 * k + 128]
            top[32:64, at : at + 128] = low[:, 128 * k : 128 * k + 128]


def relation(place):
    lane = lax.broadcasted_iota(jnp.int32, (1, 128), 1)
    k = (lane >= 24).astype(jnp.int32) + (lane >= 48).astype(jnp.int32) + (lane >= 72).astype(jnp.int32)
    level = (lane - 24 * k) >> 2
    node = place >> level
    third = jnp.where((node & 1) == 0, node + 3, node - 3)
    slot = jnp.where(k == 0, node - 2, jnp.where(k == 1, node + 2, jnp.where(k == 2, third, -1)))
    row = lax.broadcasted_iota(jnp.int32, (4 * DEVICES, 128), 0)
    match = (((row >> 2) >> level) == slot) & ((row & 3) == (lane & 3))
    return match.astype(F32).astype(BF16)


def point_parts(points):
    high = points.astype(BF16).astype(F32)
    rest = points - high
    mid = rest.astype(BF16).astype(F32)
    low = rest - mid
    return jnp.concatenate([high, mid, low, jnp.zeros((7, points.shape[1]), F32)], axis=0).astype(BF16)


def build_tiles(place, parts, cols, counts, from_left, from_right, near_left, near_right, tiles):
    half = lanes_in(8, 0, 64, F32)
    other = 1.0 - half
    blocks = [from_left[320 + 16 * c : 336 + 16 * c, :] for c in range(4)]
    blocks += [parts[:, 128 * c : 128 * c + 128] for c in range(CHUNKS)]
    blocks += [from_right[320 + 16 * c : 336 + 16 * c, :] for c in range(4)]
    row = lax.broadcasted_iota(jnp.int32, (8, 16), 0)
    col = lax.broadcasted_iota(jnp.int32, (8, 16), 1)
    adder = ((col % 3 == row) & (col < 9) & (row < 3)).astype(F32).astype(BF16)
    for c in range(16):
        joined = nn(adder, blocks[c]) * SCALE
        turned = pltpu.roll(joined, 64, 1)
        near_left[2 * c] = joined * half
        near_right[2 * c + 1] = joined * other
        near_left[2 * c + 1] = turned * half
        near_right[2 * c] = turned * other
    row = lax.broadcasted_iota(jnp.int32, (16, 384), 0)
    col = lax.broadcasted_iota(jnp.int32, (16, 384), 1)
    column = ((row % 3 == (col >> 7)) & (row < 9)).astype(F32).astype(BF16)
    lane = lax.broadcasted_iota(jnp.int32, (1, 128), 1)
    base = place * LEAF_DEV - HALO
    for c in range(CHUNKS):
        targets = tn(parts[:, 128 * c : 128 * c + 128], column) * SCALE
        for e in range(2):
            leaf = 2 * c + e
            count = counts[leaf]
            mine = [targets[64 * e : 64 * e + 64, 128 * x : 128 * x + 128] for x in range(3)]
            for pair in range(NEAR // 2):
                first = cols[2 * pair, leaf] - base
                second = cols[2 * pair + 1, leaf] - base
                source = near_left[first] + near_right[second]
                squares = SOFT
                for x in range(3):
                    gap = mine[x] - source[x : x + 1, :]
                    squares = squares + gap * gap
                slot = jnp.where(lane < 64, 2 * pair, 2 * pair + 1)
                gain = jnp.where(slot < count, LOG_GAIN, -2000.0)
                value = jnp.exp2(gain - squares * lax.rsqrt(squares))
                tiles[64 * leaf : 64 * leaf + 64, 128 * pair : 128 * pair + 128] = value.astype(BF16)


def near_field(place, signal, from_left, from_right, cols, tiles, near_left, near_right, m):
    chunks = [from_left[16 * c : 16 * c + 16, :] for c in range(4)]
    chunks += signal
    chunks += [from_right[16 * c : 16 * c + 16, :] for c in range(4)]
    for c in range(16):
        turned = pltpu.roll(chunks[c].astype(F32), 64, 1).astype(BF16)
        near_left[2 * c] = chunks[c] * m.half[0]
        near_right[2 * c + 1] = chunks[c] * m.half[1]
        near_left[2 * c + 1] = turned * m.half[0]
        near_right[2 * c] = turned * m.half[1]
    base = place * LEAF_DEV - HALO
    result = []
    for c in range(CHUNKS):
        rows = []
        for leaf in (2 * c, 2 * c + 1):
            parts = []
            for pair in range(NEAR // 2):
                first = cols[2 * pair, leaf] - base
                second = cols[2 * pair + 1, leaf] - base
                parts.append(near_left[first] + near_right[second])
            rows.append(jnp.concatenate(parts, axis=1))
        both = nt(jnp.concatenate(rows, axis=0), tiles[128 * c : 128 * c + 128, :])
        result.append(both[:16] * m.halff[0] + both[16:] * m.halff[1])
    return result


def far_field(down, basis, near, m):
    result = []
    split = [halves(d) for d in down]
    for c in range(CHUNKS):
        high, low = split[c // 2]
        g = (2 * c) % 4
        left = [high * m.group[g], high * m.group[g + 1], low * m.group[g], low * m.group[g + 1]]
        wide = jnp.concatenate([basis[:, 128 * c : 128 * c + 128]] * 4, axis=0)
        far = nn(jnp.concatenate(left, axis=0), wide)
        far = far[:32] + far[32:]
        far = far[:16] * m.halff[0] + far[16:] * m.halff[1]
        result.append((near[:, 128 * c : 128 * c + 128] + far).astype(BF16))
    return result


def store_heights(heights, out):
    at = 0
    for nodes in heights:
        for node in nodes:
            for part in node:
                out[at : at + 16, :] = part
                at += 16


def load_heights(source):
    heights, at = [], 0
    for count in NODES:
        heights.append([(source[b : b + 16, :], source[b + 16 : b + 32, :]) for b in range(at, at + 32 * count, 32)])
        at += 32 * count
    return heights


def store_local(near, couplings, near_out, couplings_out):
    for c in range(CHUNKS):
        near_out[:, 128 * c : 128 * c + 128] = near[c]
    at = 0
    for chunks in couplings:
        for chunk in chunks:
            couplings_out[at : at + 16, :] = chunk
            at += 16


def load_couplings(source):
    couplings, at = [], 0
    for count in (4, 2, 1, 1):
        couplings.append([source[b : b + 16, :] for b in range(at, at + 16 * count, 16)])
        at += 16 * count
    return couplings


def chunks_of(signal):
    return [signal[:, 128 * c : 128 * c + 128] for c in range(CHUNKS)]


def fetch(sources, targets, sems):
    copies = [pltpu.make_async_copy(s, t, sems.at[i]) for i, (s, t) in enumerate(zip(sources, targets, strict=True))]
    for copy in copies:
        copy.start()
    return copies


def first_kernel(
    vectors_hbm, points_hbm, basis_hbm, xfer_hbm, xfer_top_hbm, near, far, gather, heights_out, xfer_out, paths, weights,
    vectors, points, basis, xfer_low, xfer_top, wide_path, sems,
):
    copies = fetch(
        (xfer_top_hbm, xfer_hbm, vectors_hbm, basis_hbm, points_hbm), (xfer_top, xfer_low, vectors, basis, points), sems
    )
    place = lax.axis_index("leaf")
    m = Masks()
    xfer_out[960:1024, :] = jnp.zeros((64, 128), BF16)
    copies[1].wait()
    spread_table(xfer_low[...], xfer_out)
    copies[0].wait()
    copies[2].wait()
    copies[3].wait()
    signal = chunks_of(vectors)
    build_paths(place, xfer_top, wide_path, paths, weights)
    heights, root = up_pass(signal, basis, xfer_out, m)
    write_sends(place, signal, heights, root, weights, near, far, gather)
    store_heights(heights, heights_out)
    copies[4].wait()
    parts = chunks_of(point_parts(points[...]))
    exchange_rows(place, parts[:4], parts[4:], near, far, 320)


def table_kernel(
    couple_top_hbm, couple_hbm, paths, top, couple_wide, couple_top, couple, wide_couple, sems
):
    copies = fetch((couple_hbm, couple_top_hbm), (couple, couple_top), sems)
    copies[0].wait()
    spread_couple(couple, couple_wide)
    copies[1].wait()
    build_top(lax.axis_index("leaf"), couple, couple_top, paths, wide_couple, top)


def local_first_kernel(
    cols_hbm, counts_hbm, vectors_hbm, points_hbm, couple_wide, near, far, heights_in,
    tiles, near_out, couplings_out,
    cols, counts, vectors, points, from_left, from_right, places_left, places_right, near_left, near_right, sems,
):
    copies = fetch((cols_hbm, counts_hbm, vectors_hbm, points_hbm), (cols, counts, vectors, points), sems)
    m = Masks()
    place = lax.axis_index("leaf")
    sides(place, near, far, from_left, from_right)
    for copy in copies:
        copy.wait()
    build_tiles(
        place, point_parts(points[...]), cols, counts, from_left, from_right, places_left, places_right, tiles
    )
    couplings = couple_low(load_heights(heights_in), from_left, from_right, couple_wide, m)
    near = near_field(place, chunks_of(vectors), from_left, from_right, cols, tiles, near_left, near_right, m)
    store_local(near, couplings, near_out, couplings_out)


def spread_kernel(couple_hbm, basis_hbm, vectors, xfer, couple_wide, heights_out, couple, basis, sems):
    copies = fetch((couple_hbm, basis_hbm), (couple, basis), sems)
    m = Masks()
    copies[0].wait()
    copies[1].wait()
    spread_couple(couple, couple_wide)
    store_heights(up_pass(chunks_of(vectors), basis, xfer, m)[0], heights_out)


def local_next_kernel(
    cols_hbm, couple_wide, vectors, tiles, near, far, heights_in, near_out, couplings_out,
    cols, from_left, from_right, near_left, near_right, sems,
):
    copies = fetch((cols_hbm,), (cols,), sems)
    m = Masks()
    place = lax.axis_index("leaf")
    sides(place, near, far, from_left, from_right)
    couplings = couple_low(load_heights(heights_in), from_left, from_right, couple_wide, m)
    copies[0].wait()
    near = near_field(place, chunks_of(vectors), from_left, from_right, cols, tiles, near_left, near_right, m)
    store_local(near, couplings, near_out, couplings_out)


def down_up_kernel(
    basis_hbm, gathered, top, xfer, near, couplings, weights, near_pack, far_pack, gather, signal_out, basis, sems
):
    copies = fetch((basis_hbm,), (basis,), sems)
    m = Masks()
    place = lax.axis_index("leaf")
    down = down_pass(top_apply(place, gathered, top), load_couplings(couplings), xfer, m)
    copies[0].wait()
    signal = far_field(down, basis, near, m)
    for c in range(CHUNKS):
        signal_out[:, 128 * c : 128 * c + 128] = signal[c]
    heights, root = up_pass(signal, basis, xfer, m)
    write_sends(place, signal, heights, root, weights, near_pack, far_pack, gather)


def down_last_kernel(basis_hbm, gathered, top, xfer, near, couplings, out, basis, sems):
    copies = fetch((basis_hbm,), (basis,), sems)
    m = Masks()
    place = lax.axis_index("leaf")
    down = down_pass(top_apply(place, gathered, top), load_couplings(couplings), xfer, m)
    copies[0].wait()
    signal = far_field(down, basis, near, m)
    for c in range(CHUNKS):
        out[:, 128 * c : 128 * c + 128] = signal[c]


def call(kernel, name, arguments, arrays, outputs, scratch, flops, pinned=False):
    if pinned:
        arguments = [pltpu.with_memory_space_constraint(a, pltpu.HBM) for a in arguments]
    inputs = tuple(arguments) + tuple(arrays)
    in_specs = [pl.BlockSpec(memory_space=pltpu.HBM)] * len(arguments)
    in_specs += [pl.BlockSpec(memory_space=pltpu.VMEM)] * len(arrays)
    return pl.pallas_call(
        kernel,
        out_shape=[jax.ShapeDtypeStruct(shape, dtype) for shape, dtype in outputs],
        in_specs=in_specs,
        out_specs=[pl.BlockSpec(memory_space=pltpu.VMEM)] * len(outputs),
        scratch_shapes=scratch,
        compiler_params=pltpu.CompilerParams(vmem_limit_bytes=VMEM_LIMIT),
        cost_estimate=pl.CostEstimate(flops=flops, bytes_accessed=1 << 20, transcendentals=0),
        name=name,
    )(*inputs)


def exchange(near, far, gather):
    count = lax.axis_size("leaf")
    blocks = gather.reshape(count, 4, 128)
    gathered = lax.all_to_all(blocks, "leaf", 0, 0, tiled=True)
    near = lax.ppermute(near, "leaf", [(i, i ^ 1) for i in range(count)])
    far = lax.ppermute(far, "leaf", [(i, ((i + 1) ^ 1) - 1) for i in range(1, count - 1)])
    return near, far, gathered.reshape(count * 4, 128)


def body(vectors, points, near_cols, near_count, basis, xfer_low, couple, xfer_top, couple_top):
    vm, sm = pltpu.VMEM, pltpu.SMEM
    sems = pltpu.SemaphoreType.DMA
    signal_buf, basis_buf, points_buf = vm((16, 1024), BF16), vm((32, 1024), BF16), vm((3, 1024), F32)
    couple_buf = vm((3, 31, 1024), BF16)
    blocks = [vm((32, 16, 128), BF16)] * 2
    sends = [((512, 128), BF16), ((960, 128), BF16)]
    local = [((16, 1024), F32), ((128, 128), F32)]
    near, far, gather, heights, xfer, paths, weights = call(
        first_kernel, "up_first", (vectors, points, basis, xfer_low, xfer_top), (),
        [((384, 128), BF16)] * 2 + sends + [((1024, 128), BF16), ((192, 128), F32), ((64, 768), BF16)],
        [signal_buf, points_buf, basis_buf, vm((30, 1024), BF16), vm((254, 1024), BF16), vm((160, 128), BF16), sems((5,))],
        1 << 20, True,
    )
    near, far, gathered = exchange(near, far, gather)
    top, couple_wide = call(
        table_kernel, "tables", (couple_top, couple), (paths,), [((64, 2304), BF16), ((1024, 128), BF16)],
        [vm((3, 124, 1024), BF16), couple_buf, vm((576, 128), BF16), sems((2,))], 1 << 32, True,
    )
    tiles, near, couplings = call(
        local_first_kernel, "local_first", (near_cols, near_count, vectors, points),
        (couple_wide, near, far, heights), [((1024, 768), BF16)] + local,
        [sm((12, 16), jnp.int32), sm((16,), jnp.int32), signal_buf, points_buf] + [vm((384, 128), BF16)] * 2
        + [vm((32, 8, 128), F32)] * 2 + blocks + [sems((4,))], 1 << 32,
    )
    near, far, gather, signal = call(
        down_up_kernel, "down_up", (basis,), (gathered, top, xfer, near, couplings, weights),
        [((320, 128), BF16)] * 2 + [sends[0], ((16, 1024), BF16)], [basis_buf, sems((1,))], 1 << 20,
    )
    near, far, gathered = exchange(near, far, gather)
    couple_wide, heights = call(
        spread_kernel, "spread", (couple, basis), (signal, xfer), [((1024, 128), BF16), sends[1]],
        [couple_buf, basis_buf, sems((2,))], 1 << 32,
    )
    near, couplings = call(
        local_next_kernel, "local_next", (near_cols,), (couple_wide, signal, tiles, near, far, heights), local,
        [sm((12, 16), jnp.int32)] + [vm((320, 128), BF16)] * 2 + blocks + [sems((1,))], 1 << 32,
    )
    (result,) = call(
        down_last_kernel, "down_last", (basis,), (gathered, top, xfer, near, couplings), [((16, 1024), BF16)],
        [basis_buf, sems((1,))], 1 << 20,
    )
    return result


def solution(mesh):
    placed = (
        P("vec", "leaf"),
        P(None, "leaf"),
        P(None, "leaf"),
        P("leaf"),
        P(None, "leaf"),
        P("leaf", None),
        P(None, "leaf", None),
        P(),
        P(),
    )
    return jax.shard_map(body, mesh=mesh, in_specs=placed, out_specs=P("vec", "leaf"), check_vma=False)
```

```python
import math

import jax
import jax.numpy as jnp
from jax import lax
from jax.experimental import pallas as pl
from jax.experimental.pallas import tpu as pltpu
from jax.sharding import PartitionSpec as P

F32 = jnp.float32
BF16 = jnp.bfloat16
HALO = 8
LEAF_DEV = 16
RANK = 32
NEAR = 12
VEC = 16
DEVICES = 128
CHUNKS = 8
LOW = (0, 16, 24, 28, 30)
NODES = (16, 8, 4, 2)
TOP_XFER = (0, 128, 192, 224, 240, 248)
TOP_COUPLE = (0, 0, 64, 96, 112, 120)
SCALE = 4.0 * math.log2(math.e)
SOFT = 0.01 * SCALE * SCALE
LOG_GAIN = math.log2(4.0 / math.sqrt(64 * NEAR))
VMEM_LIMIT = 48 * 1024 * 1024


def nn(a, b):
    return lax.dot_general(a, b, (((1,), (0,)), ((), ())), preferred_element_type=F32)


def nt(a, b):
    return lax.dot_general(a, b, (((1,), (1,)), ((), ())), preferred_element_type=F32)


def tn(a, b):
    return lax.dot_general(a, b, (((0,), (0,)), ((), ())), preferred_element_type=F32)


def halves(x):
    high = x.astype(BF16)
    return high, (x - high.astype(F32)).astype(BF16)


def lanes_in(rows, lo, size, dtype):
    lane = lax.broadcasted_iota(jnp.int32, (rows, 128), 1)
    return ((lane >= lo) & (lane < lo + size)).astype(F32).astype(dtype)


class Masks:
    def __init__(self, rows=16):
        self.rows = rows
        self.group = [lanes_in(rows, 32 * g, 32, BF16) for g in range(4)]
        self.groupf = [lanes_in(rows, 32 * g, 32, F32) for g in range(4)]
        self.half = [lanes_in(rows, 64 * g, 64, BF16) for g in range(2)]
        self.halff = [lanes_in(rows, 64 * g, 64, F32) for g in range(2)]


def repeat_matrix():
    row = lax.broadcasted_iota(jnp.int32, (128, 128), 0)
    col = lax.broadcasted_iota(jnp.int32, (128, 128), 1)
    return ((row & 31) == (col & 31)).astype(F32).astype(BF16)


def spread_rows(table, nodes):
    row = lax.broadcasted_iota(jnp.int32, (8, 128), 0)
    lane = lax.broadcasted_iota(jnp.int32, (8, 128), 1)
    mine = ((row & 3) == (lane >> 5)).astype(F32)
    parts = []
    for node in nodes:
        for j in range(4):
            one = table[node : node + 1, 256 * j : 256 * j + 128]
            two = table[node : node + 1, 256 * j + 128 : 256 * j + 256]
            parts.append(jnp.where(row < 4, one, two) * mine)
    return jnp.concatenate(parts, axis=0).astype(BF16)


def spread_table(table, out, first=0):
    table = table.astype(F32)
    repeat = repeat_matrix()
    count = table.shape[0]
    for n in range(0, count, 4):
        wide = nn(spread_rows(table, range(n, min(n + 4, count))), repeat)
        at = (first + n) * 32
        out[at : at + wide.shape[0], :] = wide.astype(out.dtype)


def spread_couple(couple, out):
    tables = [couple[k].astype(F32) for k in range(3)]
    row = lax.broadcasted_iota(jnp.int32, (384, 128), 0)
    col = lax.broadcasted_iota(jnp.int32, (384, 128), 1)
    fold = (((row & 31) == (col & 31)) & ((row >> 7) == (col >> 5))).astype(F32).astype(BF16)
    for n in range(0, 31, 4):
        nodes = range(n, min(n + 4, 31))
        wide = nn(jnp.concatenate([spread_rows(table, nodes) for table in tables], axis=1), fold)
        out[32 * n : 32 * n + wide.shape[0], :] = wide.astype(BF16)
    out[992:1024, :] = jnp.zeros((32, 128), BF16)


def up_pass(signal, basis, xfer, m):
    nodes = []
    for c in range(CHUNKS):
        wide = jnp.concatenate([basis[:, 128 * c : 128 * c + 128]] * 4, axis=0)
        both = nt(jnp.concatenate([signal[c] * m.half[0], signal[c] * m.half[1]], axis=0), wide)
        nodes += [both[:16], both[16:]]
    heights = []
    for h in range(4):
        split = [halves(node) for node in nodes]
        heights.append(split)
        nodes = []
        for t in range(0, NODES[h], 4):
            family = split[t : t + 4]
            left = [
                family[i][part] * m.group[i] + family[i + 1][part] * m.group[i + 1]
                for part in range(2)
                for i in range(0, len(family), 2)
            ]
            first = (LOW[h] + t) * 32
            both = nn(jnp.concatenate(left, axis=0), xfer[first : first + 128, :])
            size = 8 * len(family)
            both = both[:size] + both[size:]
            nodes += [both[i : i + 16] for i in range(0, size, 16)]
    return heights, nodes[0]


def exchange_rows(place, to_left, to_right, near, far, first):
    even = (place & 1) == 0
    for i, (one, two) in enumerate(zip(to_left, to_right, strict=True)):
        at = first + 16 * i
        near[at : at + 16, :] = jnp.where(even, two, one)
        far[at : at + 16, :] = jnp.where(even, one, two)


def sides(place, near, far, left, right):
    even = (place & 1) == 0
    for at in range(0, near.shape[0], 16):
        one, two = near[at : at + 16, :], far[at : at + 16, :]
        left[at : at + 16, :] = jnp.where(even, two, one)
        right[at : at + 16, :] = jnp.where(even, one, two)


def write_halo(place, signal, heights, near, far):
    exchange_rows(place, signal[:4], signal[4:], near, far, 0)
    to_left = [heights[h][i][part] for h in range(4) for i in (0, 1) for part in range(2)]
    to_right = [heights[h][i][part] for h in range(4) for i in (-2, -1) for part in range(2)]
    exchange_rows(place, to_left, to_right, near, far, 64)


def write_sends(place, root, weights, gather):
    both = nn(jnp.concatenate([part[:, 0:64] for part in halves(root)], axis=0), weights[...])
    both = both[:16] + both[16:]
    row = lax.broadcasted_iota(jnp.int32, (16, 128), 0)
    mine = ((row >> 2) == (lax.broadcasted_iota(jnp.int32, (16, 128), 1) >> 5)).astype(F32)
    packed = []
    for level in range(6):
        one = both[:, 128 * level : 128 * level + 128] * mine
        one = one[0:8] + one[8:16]
        packed.append(one[0:4] + one[4:8])
    packed = jnp.concatenate(packed, axis=0)
    packed = jnp.concatenate([packed] * 3 + [jnp.zeros((56, 128), F32)], axis=0).astype(BF16)
    gather[...] = nn(relation(place), packed).astype(BF16)


def couple_low(heights, from_left, from_right, table, m):
    result = []
    for h in range(4):
        count = NODES[h]

        def node(n, part, h=h, count=count):
            if n < 0:
                at = 64 + (4 * h + 2 * (n + 2) + part) * 16
                return from_left[at : at + 16, :]
            if n >= count:
                at = 64 + (4 * h + 2 * (n - count) + part) * 16
                return from_right[at : at + 16, :]
            return heights[h][n][part]

        chunks = []
        for t in range(0, count, 4):
            targets = range(t, min(t + 4, count))
            left = []
            for part in range(2):
                for j in targets:
                    third = j + 3 if j % 2 == 0 else j - 3
                    slots = (node(j - 2, part), node(j + 2, part), node(third, part))
                    left.append(slots[0] * m.group[0] + slots[1] * m.group[1] + slots[2] * m.group[2])
            first = (LOW[h] + t) * 32
            wide = nt(jnp.concatenate(left, axis=0), table[first : first + 128, :])
            wide = wide[: 16 * len(targets)] + wide[16 * len(targets) :]
            chunk = wide[0:16] * m.groupf[0]
            for j in range(1, len(targets)):
                chunk = chunk + wide[16 * j : 16 * j + 16] * m.groupf[j]
            chunks.append(chunk)
        result.append(chunks)
    return result


def top_apply(place, gathered, top):
    sums = tn(relation(place), gathered[...])
    row = lax.broadcasted_iota(jnp.int32, (16, 128), 0)
    mine = ((row >> 2) == (lax.broadcasted_iota(jnp.int32, (16, 128), 1) >> 5)).astype(F32)
    left = [jnp.concatenate([sums[4 * i : 4 * i + 4]] * 4, axis=0) * mine for i in range(18)]
    left = halves(jnp.concatenate(left, axis=1))
    total = nt(jnp.concatenate(left, axis=0), top[...])
    return everywhere(total[:16] + total[16:])


def down_pass(root, couplings, xfer, m):
    n = m.rows
    down = [0.0] if couplings is None else couplings[3]
    if root is not None:
        high, low = halves(root)
        first = LOW[3] * 32
        both = nt(jnp.concatenate([high * m.group[0], low * m.group[0]], axis=0), xfer[first : first + 128, :])
        down = [down[0] + both[:n] + both[n:]]
    for h in (2, 1, 0):
        first = LOW[h] * 32
        split = [halves(d) for d in down]
        down = []
        for t in range(NODES[h] // 4):
            high, low = split[t // 2]
            g = (2 * t) % 4
            left = [high * m.group[g], high * m.group[g + 1], low * m.group[g], low * m.group[g + 1]]
            both = nt(jnp.concatenate(left, axis=0), xfer[first + 128 * t : first + 128 * t + 128, :])
            both = both[: 2 * n] + both[2 * n :]
            both = both[:n] * m.halff[0] + both[n:] * m.halff[1]
            down.append(both if couplings is None else couplings[h][t] + both)
    return down


def pick_rows(table, level_rows):
    count = table.shape[0]
    row = lax.broadcasted_iota(jnp.int32, (8, count), 0)
    col = lax.broadcasted_iota(jnp.int32, (8, count), 1)
    wanted = jnp.zeros((8, count), jnp.int32) - 1
    for level, at in level_rows.items():
        wanted = jnp.where(row == level, at, wanted)
    return nn((col == wanted).astype(F32).astype(BF16), table)


def build_paths(place, xfer_top, wide_path, paths, weights):
    rows = pick_rows(xfer_top[...], {level: TOP_XFER[level] + (place >> level) for level in range(5)})
    spread_table(rows[0:5], wide_path)
    row = lax.broadcasted_iota(jnp.int32, (32, 128), 0)
    lane = lax.broadcasted_iota(jnp.int32, (32, 128), 1)
    step = [wide_path[32 * level : 32 * level + 32, :] for level in range(5)]

    def times(left, right):
        both = nn(jnp.concatenate([part[:, 0:32] for part in halves(left)], axis=0), right)
        return both[:32] + both[32:]

    pair = halves(nn(step[2][:, 0:32], step[3]))
    second = nn(step[0][:, 0:32], step[1])
    fourth = times(second, jnp.concatenate(pair, axis=1))
    fourth = fourth[:, :128] + fourth[:, 128:]
    products = [(row == (lane & 31)).astype(F32), step[0].astype(F32), second, times(second, step[2]), fourth]
    products.append(times(fourth, step[4]))
    for level in range(6):
        paths[32 * level : 32 * level + 32, :] = products[level]
        high, low = halves(products[level])
        weights[0:32, 128 * level : 128 * level + 128] = high
        weights[32:64, 128 * level : 128 * level + 128] = low


def build_top(place, couple, couple_top, paths, wide_couple, top):
    at = {level: TOP_COUPLE[level] + (place >> level) for level in range(1, 6)}
    for k in range(3):
        rows = pick_rows(couple_top[k], at) + pick_rows(couple[k], {0: LOW[4]})
        spread_table(rows[0:6], wide_couple, 6 * k)
    for level in range(6):
        high, low = halves(paths[32 * level : 32 * level + 32, :])
        left = jnp.concatenate([high[:, 0:32], low[:, 0:32]], axis=0)
        right = [wide_couple[(6 * k + level) * 32 : (6 * k + level + 1) * 32, :] for k in range(3)]
        both = nn(left, jnp.concatenate(right, axis=1))
        high, low = halves(both[:32] + both[32:])
        for k in range(3):
            at = (6 * k + level) * 128
            top[0:32, at : at + 128] = high[:, 128 * k : 128 * k + 128]
            top[32:64, at : at + 128] = low[:, 128 * k : 128 * k + 128]


def relation(place):
    lane = lax.broadcasted_iota(jnp.int32, (1, 128), 1)
    k = (lane >= 24).astype(jnp.int32) + (lane >= 48).astype(jnp.int32) + (lane >= 72).astype(jnp.int32)
    level = (lane - 24 * k) >> 2
    node = place >> level
    third = jnp.where((node & 1) == 0, node + 3, node - 3)
    slot = jnp.where(k == 0, node - 2, jnp.where(k == 1, node + 2, jnp.where(k == 2, third, -1)))
    row = lax.broadcasted_iota(jnp.int32, (4 * DEVICES, 128), 0)
    match = (((row >> 2) >> level) == slot) & ((row & 3) == (lane & 3))
    return match.astype(F32).astype(BF16)


def point_parts(points):
    high = points.astype(BF16).astype(F32)
    rest = points - high
    mid = rest.astype(BF16).astype(F32)
    low = rest - mid
    return jnp.concatenate([high, mid, low, jnp.zeros((7, points.shape[1]), F32)], axis=0).astype(BF16)


def build_tiles(place, parts, cols, counts, from_left, from_right, near_left, near_right, tiles):
    half = lanes_in(8, 0, 64, F32)
    other = 1.0 - half
    blocks = [from_left[320 + 16 * c : 336 + 16 * c, :] for c in range(4)]
    blocks += [parts[:, 128 * c : 128 * c + 128] for c in range(CHUNKS)]
    blocks += [from_right[320 + 16 * c : 336 + 16 * c, :] for c in range(4)]
    row = lax.broadcasted_iota(jnp.int32, (8, 16), 0)
    col = lax.broadcasted_iota(jnp.int32, (8, 16), 1)
    adder = ((col % 3 == row) & (col < 9) & (row < 3)).astype(F32).astype(BF16)
    for c in range(16):
        joined = nn(adder, blocks[c]) * SCALE
        turned = pltpu.roll(joined, 64, 1)
        near_left[2 * c] = joined * half
        near_right[2 * c + 1] = joined * other
        near_left[2 * c + 1] = turned * half
        near_right[2 * c] = turned * other
    row = lax.broadcasted_iota(jnp.int32, (16, 384), 0)
    col = lax.broadcasted_iota(jnp.int32, (16, 384), 1)
    column = ((row % 3 == (col >> 7)) & (row < 9)).astype(F32).astype(BF16)
    lane = lax.broadcasted_iota(jnp.int32, (1, 128), 1)
    base = place * LEAF_DEV - HALO
    for c in range(CHUNKS):
        targets = tn(parts[:, 128 * c : 128 * c + 128], column) * SCALE
        for e in range(2):
            leaf = 2 * c + e
            count = counts[leaf]
            mine = [targets[64 * e : 64 * e + 64, 128 * x : 128 * x + 128] for x in range(3)]
            for pair in range(NEAR // 2):
                first = cols[2 * pair, leaf] - base
                second = cols[2 * pair + 1, leaf] - base
                source = near_left[first] + near_right[second]
                squares = SOFT
                for x in range(3):
                    gap = mine[x] - source[x : x + 1, :]
                    squares = squares + gap * gap
                slot = jnp.where(lane < 64, 2 * pair, 2 * pair + 1)
                gain = jnp.where(slot < count, LOG_GAIN, -2000.0)
                value = jnp.exp2(gain - squares * lax.rsqrt(squares))
                tiles[64 * leaf : 64 * leaf + 64, 128 * pair : 128 * pair + 128] = value.astype(BF16)


def near_field(place, signal, from_left, from_right, cols, tiles, near_left, near_right, m):
    chunks = [from_left[16 * c : 16 * c + 16, :] for c in range(4)]
    chunks += signal
    chunks += [from_right[16 * c : 16 * c + 16, :] for c in range(4)]
    for c in range(16):
        turned = pltpu.roll(chunks[c].astype(F32), 64, 1).astype(BF16)
        near_left[2 * c] = chunks[c] * m.half[0]
        near_right[2 * c + 1] = chunks[c] * m.half[1]
        near_left[2 * c + 1] = turned * m.half[0]
        near_right[2 * c] = turned * m.half[1]
    base = place * LEAF_DEV - HALO
    result = []
    for c in range(CHUNKS):
        rows = []
        for leaf in (2 * c, 2 * c + 1):
            parts = []
            for pair in range(NEAR // 2):
                first = cols[2 * pair, leaf] - base
                second = cols[2 * pair + 1, leaf] - base
                parts.append(near_left[first] + near_right[second])
            rows.append(jnp.concatenate(parts, axis=1))
        both = nt(jnp.concatenate(rows, axis=0), tiles[128 * c : 128 * c + 128, :])
        result.append(both[:16] * m.halff[0] + both[16:] * m.halff[1])
    return result


def far_field(down, basis, m):
    n = m.rows
    result = []
    split = [halves(d) for d in down]
    for c in range(CHUNKS):
        high, low = split[c // 2]
        g = (2 * c) % 4
        left = [high * m.group[g], high * m.group[g + 1], low * m.group[g], low * m.group[g + 1]]
        wide = jnp.concatenate([basis[:, 128 * c : 128 * c + 128]] * 4, axis=0)
        far = nn(jnp.concatenate(left, axis=0), wide)
        far = far[: 2 * n] + far[2 * n :]
        result.append(far[:n] * m.halff[0] + far[n:] * m.halff[1])
    return result


def build_root_basis(basis, xfer, root_basis):
    row = lax.broadcasted_iota(jnp.int32, (32, 128), 0)
    one = (row == (lax.broadcasted_iota(jnp.int32, (32, 128), 1) & 31)).astype(F32)
    m = Masks(32)
    for c, far in enumerate(far_field(down_pass(one, None, xfer, m), basis, m)):
        high, low = halves(far)
        root_basis[0:32, 128 * c : 128 * c + 128] = high
        root_basis[32:64, 128 * c : 128 * c + 128] = low


def finish(down, local, root_basis):
    both = nn(jnp.concatenate([part[:, 0:64] for part in halves(down)], axis=0), root_basis[...])
    return (local[...] + both[:16] + both[16:]).astype(BF16)


def everywhere(parts):
    total = jnp.concatenate([parts, jnp.zeros((16, 64), F32)], axis=1)
    total = total + pltpu.roll(total, 64, 1)
    return total + pltpu.roll(total, 32, 1)


def store_heights(heights, out):
    at = 0
    for nodes in heights:
        for node in nodes:
            for part in node:
                out[at : at + 16, :] = part
                at += 16


def load_heights(source):
    heights, at = [], 0
    for count in NODES:
        heights.append([(source[b : b + 16, :], source[b + 16 : b + 32, :]) for b in range(at, at + 32 * count, 32)])
        at += 32 * count
    return heights


def store_local(near, couplings, basis, xfer, local_out, m):
    far = far_field(down_pass(None, couplings, xfer, m), basis, m)
    for c in range(CHUNKS):
        local_out[:, 128 * c : 128 * c + 128] = near[c] + far[c]


def chunks_of(signal):
    return [signal[:, 128 * c : 128 * c + 128] for c in range(CHUNKS)]


def fetch(sources, targets, sems):
    copies = [pltpu.make_async_copy(s, t, sems.at[i]) for i, (s, t) in enumerate(zip(sources, targets, strict=True))]
    for copy in copies:
        copy.start()
    return copies


def first_kernel(
    vectors_hbm, points_hbm, basis_hbm, xfer_hbm, xfer_top_hbm, near, far, gather, heights_out, xfer_out, paths, weights,
    vectors, points, basis, xfer_low, xfer_top, wide_path, sems,
):
    copies = fetch(
        (xfer_top_hbm, xfer_hbm, vectors_hbm, basis_hbm, points_hbm), (xfer_top, xfer_low, vectors, basis, points), sems
    )
    place = lax.axis_index("leaf")
    m = Masks()
    xfer_out[960:1024, :] = jnp.zeros((64, 128), BF16)
    copies[1].wait()
    spread_table(xfer_low[...], xfer_out)
    copies[0].wait()
    copies[2].wait()
    copies[3].wait()
    signal = chunks_of(vectors)
    build_paths(place, xfer_top, wide_path, paths, weights)
    heights, root = up_pass(signal, basis, xfer_out, m)
    write_halo(place, signal, heights, near, far)
    write_sends(place, root, weights, gather)
    store_heights(heights, heights_out)
    copies[4].wait()
    parts = chunks_of(point_parts(points[...]))
    exchange_rows(place, parts[:4], parts[4:], near, far, 320)


def table_kernel(
    couple_top_hbm, couple_hbm, basis_hbm, paths, xfer, top, couple_wide, root_basis,
    couple_top, couple, basis, wide_couple, sems,
):
    copies = fetch((couple_top_hbm, couple_hbm, basis_hbm), (couple_top, couple, basis), sems)
    copies[2].wait()
    build_root_basis(basis, xfer, root_basis)
    copies[1].wait()
    spread_couple(couple, couple_wide)
    copies[0].wait()
    build_top(lax.axis_index("leaf"), couple, couple_top, paths, wide_couple, top)


def local_first_kernel(
    cols_hbm, counts_hbm, vectors_hbm, points_hbm, basis_hbm, couple_wide, xfer, far, near, heights_in,
    tiles, local_out,
    cols, counts, vectors, points, basis, from_left, from_right, places_left, places_right, near_left, near_right, sems,
):
    copies = fetch(
        (cols_hbm, counts_hbm, vectors_hbm, points_hbm, basis_hbm), (cols, counts, vectors, points, basis), sems
    )
    m = Masks()
    place = lax.axis_index("leaf")
    sides(place, near, far, from_left, from_right)
    for copy in copies:
        copy.wait()
    build_tiles(
        place, point_parts(points[...]), cols, counts, from_left, from_right, places_left, places_right, tiles
    )
    couplings = couple_low(load_heights(heights_in), from_left, from_right, couple_wide, m)
    near = near_field(place, chunks_of(vectors), from_left, from_right, cols, tiles, near_left, near_right, m)
    store_local(near, couplings, basis, xfer, local_out, m)


def pack_kernel(basis_hbm, vectors, xfer, near, far, heights_out, basis, sems):
    copies = fetch((basis_hbm,), (basis,), sems)
    m = Masks()
    signal = chunks_of(vectors)
    copies[0].wait()
    heights, _ = up_pass(signal, basis, xfer, m)
    write_halo(lax.axis_index("leaf"), signal, heights, near, far)
    store_heights(heights, heights_out)


def spread_kernel(couple_hbm, after, couple_wide, couple, sems):
    del after
    fetch((couple_hbm,), (couple,), sems)[0].wait()
    spread_couple(couple, couple_wide)


def local_next_kernel(
    cols_hbm, basis_hbm, couple_wide, xfer, vectors, tiles, far, near, heights_in, local_out,
    cols, basis, from_left, from_right, near_left, near_right, sems,
):
    copies = fetch((cols_hbm, basis_hbm), (cols, basis), sems)
    m = Masks()
    place = lax.axis_index("leaf")
    sides(place, near, far, from_left, from_right)
    couplings = couple_low(load_heights(heights_in), from_left, from_right, couple_wide, m)
    copies[0].wait()
    copies[1].wait()
    near = near_field(place, chunks_of(vectors), from_left, from_right, cols, tiles, near_left, near_right, m)
    store_local(near, couplings, basis, xfer, local_out, m)


def down_up_kernel(gathered, top, root_basis, local, weights, gather, signal_out):
    place = lax.axis_index("leaf")
    signal = finish(top_apply(place, gathered, top), local, root_basis)
    signal_out[...] = signal
    write_sends(place, everywhere(nt(signal, root_basis[...])), weights, gather)


def down_last_kernel(gathered, top, root_basis, local, out):
    out[...] = finish(top_apply(lax.axis_index("leaf"), gathered, top), local, root_basis)


def call(kernel, name, arguments, arrays, outputs, scratch, flops, pinned=False):
    if pinned:
        arguments = [pltpu.with_memory_space_constraint(a, pltpu.HBM) for a in arguments]
    inputs = tuple(arguments) + tuple(arrays)
    in_specs = [pl.BlockSpec(memory_space=pltpu.HBM)] * len(arguments)
    in_specs += [pl.BlockSpec(memory_space=pltpu.VMEM)] * len(arrays)
    return pl.pallas_call(
        kernel,
        out_shape=[jax.ShapeDtypeStruct(shape, dtype) for shape, dtype in outputs],
        in_specs=in_specs,
        out_specs=[pl.BlockSpec(memory_space=pltpu.VMEM)] * len(outputs),
        scratch_shapes=scratch,
        compiler_params=pltpu.CompilerParams(vmem_limit_bytes=VMEM_LIMIT),
        cost_estimate=pl.CostEstimate(flops=flops, bytes_accessed=1 << 20, transcendentals=0),
        name=name,
    )(*inputs)


def to_all(gather):
    count = lax.axis_size("leaf")
    blocks = gather.reshape(count, 4, 128)
    return lax.all_to_all(blocks, "leaf", 0, 0, tiled=True).reshape(count * 4, 128)


def swap(near, far):
    count = lax.axis_size("leaf")
    far = lax.ppermute(far, "leaf", [(i, ((i + 1) ^ 1) - 1) for i in range(1, count - 1)])
    return far, lax.ppermute(near, "leaf", [(i, i ^ 1) for i in range(count)])


def body(vectors, points, near_cols, near_count, basis, xfer_low, couple, xfer_top, couple_top):
    vm, sm = pltpu.VMEM, pltpu.SMEM
    sems = pltpu.SemaphoreType.DMA
    signal_buf, basis_buf, points_buf = vm((16, 1024), BF16), vm((32, 1024), BF16), vm((3, 1024), F32)
    couple_buf = vm((3, 31, 1024), BF16)
    blocks = [vm((32, 16, 128), BF16)] * 2
    sends = [((512, 128), BF16), ((960, 128), BF16)]
    local_out, root_out = ((16, 1024), F32), ((64, 1024), BF16)
    near, far, gather, heights, xfer, paths, weights = call(
        first_kernel, "up_first", (vectors, points, basis, xfer_low, xfer_top), (),
        [((384, 128), BF16)] * 2 + sends + [((1024, 128), BF16), ((192, 128), F32), ((64, 768), BF16)],
        [signal_buf, points_buf, basis_buf, vm((30, 1024), BF16), vm((254, 1024), BF16), vm((160, 128), BF16), sems((5,))],
        1 << 20, True,
    )
    gathered = to_all(gather)
    far, near = swap(near, far)
    top, couple_wide, root_basis = call(
        table_kernel, "tables", (couple_top, couple, basis), (paths, xfer),
        [((64, 2304), BF16), ((1024, 128), BF16), root_out],
        [vm((3, 124, 1024), BF16), couple_buf, basis_buf, vm((576, 128), BF16), sems((3,))], 1 << 32, True,
    )
    tiles, local = call(
        local_first_kernel, "local_first", (near_cols, near_count, vectors, points, basis),
        (couple_wide, xfer, far, near, heights), [((1024, 768), BF16), local_out],
        [sm((12, 16), jnp.int32), sm((16,), jnp.int32), signal_buf, points_buf, basis_buf] + [vm((384, 128), BF16)] * 2
        + [vm((32, 8, 128), F32)] * 2 + blocks + [sems((5,))], 1 << 32,
    )
    gather, signal = call(
        down_up_kernel, "down_up", (), (gathered, top, root_basis, local, weights), [sends[0], ((16, 1024), BF16)], [],
        1 << 20,
    )
    gathered = to_all(gather)
    near, far, heights = call(
        pack_kernel, "pack", (basis,), (signal, xfer), [((320, 128), BF16)] * 2 + [sends[1]], [basis_buf, sems((1,))],
        1 << 32,
    )
    far, near = swap(near, far)
    (couple_wide,) = call(
        spread_kernel, "spread", (couple,), (heights,), [((1024, 128), BF16)], [couple_buf, sems((1,))], 1 << 32
    )
    (local,) = call(
        local_next_kernel, "local_next", (near_cols, basis), (couple_wide, xfer, signal, tiles, far, near, heights),
        [local_out],
        [sm((12, 16), jnp.int32), basis_buf] + [vm((320, 128), BF16)] * 2 + blocks + [sems((2,))], 1 << 32,
    )
    (result,) = call(
        down_last_kernel, "down_last", (), (gathered, top, root_basis, local), [((16, 1024), BF16)], [], 1 << 20
    )
    return result


def solution(mesh):
    placed = (
        P("vec", "leaf"),
        P(None, "leaf"),
        P(None, "leaf"),
        P("leaf"),
        P(None, "leaf"),
        P("leaf", None),
        P(None, "leaf", None),
        P(),
        P(),
    )
    return jax.shard_map(body, mesh=mesh, in_specs=placed, out_specs=P("vec", "leaf"), check_vma=False)
```

```python
import math

import jax
import jax.numpy as jnp
from jax import lax
from jax.experimental import pallas as pl
from jax.experimental.pallas import tpu as pltpu
from jax.sharding import PartitionSpec as P

F32 = jnp.float32
BF16 = jnp.bfloat16
HALO = 8
LEAF_DEV = 16
RANK = 32
NEAR = 12
VEC = 16
DEVICES = 128
CHUNKS = 8
LOW = (0, 16, 24, 28, 30)
NODES = (16, 8, 4, 2)
TOP_XFER = (0, 128, 192, 224, 240, 248)
TOP_COUPLE = (0, 0, 64, 96, 112, 120)
SCALE = 4.0 * math.log2(math.e)
SOFT = 0.01 * SCALE * SCALE
LOG_GAIN = math.log2(4.0 / math.sqrt(64 * NEAR))
VMEM_LIMIT = 48 * 1024 * 1024


def nn(a, b):
    return lax.dot_general(a, b, (((1,), (0,)), ((), ())), preferred_element_type=F32)


def nt(a, b):
    return lax.dot_general(a, b, (((1,), (1,)), ((), ())), preferred_element_type=F32)


def tn(a, b):
    return lax.dot_general(a, b, (((0,), (0,)), ((), ())), preferred_element_type=F32)


def halves(x):
    high = x.astype(BF16)
    return high, (x - high.astype(F32)).astype(BF16)


def lanes_in(rows, lo, size, dtype):
    lane = lax.broadcasted_iota(jnp.int32, (rows, 128), 1)
    return ((lane >= lo) & (lane < lo + size)).astype(F32).astype(dtype)


class Masks:
    def __init__(self, rows=16):
        self.rows = rows
        self.group = [lanes_in(rows, 32 * g, 32, BF16) for g in range(4)]
        self.groupf = [lanes_in(rows, 32 * g, 32, F32) for g in range(4)]
        self.half = [lanes_in(rows, 64 * g, 64, BF16) for g in range(2)]
        self.halff = [lanes_in(rows, 64 * g, 64, F32) for g in range(2)]


def repeat_matrix():
    row = lax.broadcasted_iota(jnp.int32, (128, 128), 0)
    col = lax.broadcasted_iota(jnp.int32, (128, 128), 1)
    return ((row & 31) == (col & 31)).astype(F32).astype(BF16)


def spread_rows(table, nodes):
    row = lax.broadcasted_iota(jnp.int32, (8, 128), 0)
    lane = lax.broadcasted_iota(jnp.int32, (8, 128), 1)
    mine = ((row & 3) == (lane >> 5)).astype(F32)
    parts = []
    for node in nodes:
        for j in range(4):
            one = table[node : node + 1, 256 * j : 256 * j + 128]
            two = table[node : node + 1, 256 * j + 128 : 256 * j + 256]
            parts.append(jnp.where(row < 4, one, two) * mine)
    return jnp.concatenate(parts, axis=0).astype(BF16)


def spread_table(table, out, first=0):
    table = table.astype(F32)
    repeat = repeat_matrix()
    count = table.shape[0]
    for n in range(0, count, 4):
        wide = nn(spread_rows(table, range(n, min(n + 4, count))), repeat)
        at = (first + n) * 32
        out[at : at + wide.shape[0], :] = wide.astype(out.dtype)


def spread_couple(couple, out):
    tables = [couple[k].astype(F32) for k in range(3)]
    row = lax.broadcasted_iota(jnp.int32, (384, 128), 0)
    col = lax.broadcasted_iota(jnp.int32, (384, 128), 1)
    fold = (((row & 31) == (col & 31)) & ((row >> 7) == (col >> 5))).astype(F32).astype(BF16)
    for n in range(0, 31, 4):
        nodes = range(n, min(n + 4, 31))
        wide = nn(jnp.concatenate([spread_rows(table, nodes) for table in tables], axis=1), fold)
        out[32 * n : 32 * n + wide.shape[0], :] = wide.astype(BF16)
    out[992:1024, :] = jnp.zeros((32, 128), BF16)


def up_pass(signal, basis, xfer, m):
    nodes = []
    for c in range(CHUNKS):
        wide = jnp.concatenate([basis[:, 128 * c : 128 * c + 128]] * 4, axis=0)
        both = nt(jnp.concatenate([signal[c] * m.half[0], signal[c] * m.half[1]], axis=0), wide)
        nodes += [both[:16], both[16:]]
    heights = []
    for h in range(4):
        split = [halves(node) for node in nodes]
        heights.append(split)
        nodes = []
        for t in range(0, NODES[h], 4):
            family = split[t : t + 4]
            left = [
                family[i][part] * m.group[i] + family[i + 1][part] * m.group[i + 1]
                for part in range(2)
                for i in range(0, len(family), 2)
            ]
            first = (LOW[h] + t) * 32
            both = nn(jnp.concatenate(left, axis=0), xfer[first : first + 128, :])
            size = 8 * len(family)
            both = both[:size] + both[size:]
            nodes += [both[i : i + 16] for i in range(0, size, 16)]
    return heights, nodes[0]


def exchange_rows(place, to_left, to_right, near, far, first):
    even = (place & 1) == 0
    for i, (one, two) in enumerate(zip(to_left, to_right, strict=True)):
        at = first + 16 * i
        near[at : at + 16, :] = jnp.where(even, two, one)
        far[at : at + 16, :] = jnp.where(even, one, two)


def sides(place, near, far, left, right):
    even = (place & 1) == 0
    for at in range(0, near.shape[0], 16):
        one, two = near[at : at + 16, :], far[at : at + 16, :]
        left[at : at + 16, :] = jnp.where(even, two, one)
        right[at : at + 16, :] = jnp.where(even, one, two)


def write_halo(place, signal, heights, near, far):
    exchange_rows(place, signal[:4], signal[4:], near, far, 0)
    to_left = [heights[h][i][part] for h in range(4) for i in (0, 1) for part in range(2)]
    to_right = [heights[h][i][part] for h in range(4) for i in (-2, -1) for part in range(2)]
    exchange_rows(place, to_left, to_right, near, far, 64)


def write_sends(place, root, weights, gather):
    both = nn(jnp.concatenate([part[:, 0:64] for part in halves(root)], axis=0), weights[...])
    both = both[:16] + both[16:]
    row = lax.broadcasted_iota(jnp.int32, (16, 128), 0)
    mine = ((row >> 2) == (lax.broadcasted_iota(jnp.int32, (16, 128), 1) >> 5)).astype(F32)
    packed = []
    for level in range(6):
        one = both[:, 128 * level : 128 * level + 128] * mine
        one = one[0:8] + one[8:16]
        packed.append(one[0:4] + one[4:8])
    packed = jnp.concatenate(packed, axis=0)
    packed = jnp.concatenate([packed] * 3 + [jnp.zeros((56, 128), F32)], axis=0).astype(BF16)
    gather[...] = nn(relation(place), packed).astype(BF16)


def couple_low(heights, from_left, from_right, table, m):
    result = []
    for h in range(4):
        count = NODES[h]

        def node(n, part, h=h, count=count):
            if n < 0:
                at = 64 + (4 * h + 2 * (n + 2) + part) * 16
                return from_left[at : at + 16, :]
            if n >= count:
                at = 64 + (4 * h + 2 * (n - count) + part) * 16
                return from_right[at : at + 16, :]
            return heights[h][n][part]

        chunks = []
        for t in range(0, count, 4):
            targets = range(t, min(t + 4, count))
            left = []
            for part in range(2):
                for j in targets:
                    third = j + 3 if j % 2 == 0 else j - 3
                    slots = (node(j - 2, part), node(j + 2, part), node(third, part))
                    left.append(slots[0] * m.group[0] + slots[1] * m.group[1] + slots[2] * m.group[2])
            first = (LOW[h] + t) * 32
            wide = nt(jnp.concatenate(left, axis=0), table[first : first + 128, :])
            wide = wide[: 16 * len(targets)] + wide[16 * len(targets) :]
            chunk = wide[0:16] * m.groupf[0]
            for j in range(1, len(targets)):
                chunk = chunk + wide[16 * j : 16 * j + 16] * m.groupf[j]
            chunks.append(chunk)
        result.append(chunks)
    return result


def top_apply(place, gathered, top):
    sums = tn(relation(place), gathered[...])
    row = lax.broadcasted_iota(jnp.int32, (16, 128), 0)
    mine = ((row >> 2) == (lax.broadcasted_iota(jnp.int32, (16, 128), 1) >> 5)).astype(F32)
    left = [jnp.concatenate([sums[4 * i : 4 * i + 4]] * 4, axis=0) * mine for i in range(18)]
    left = halves(jnp.concatenate(left, axis=1))
    total = nt(jnp.concatenate(left, axis=0), top[...])
    return everywhere(total[:16] + total[16:])


def down_pass(root, couplings, xfer, m):
    n = m.rows
    down = [0.0] if couplings is None else couplings[3]
    if root is not None:
        high, low = halves(root)
        first = LOW[3] * 32
        both = nt(jnp.concatenate([high * m.group[0], low * m.group[0]], axis=0), xfer[first : first + 128, :])
        down = [down[0] + both[:n] + both[n:]]
    for h in (2, 1, 0):
        first = LOW[h] * 32
        split = [halves(d) for d in down]
        down = []
        for t in range(NODES[h] // 4):
            high, low = split[t // 2]
            g = (2 * t) % 4
            left = [high * m.group[g], high * m.group[g + 1], low * m.group[g], low * m.group[g + 1]]
            both = nt(jnp.concatenate(left, axis=0), xfer[first + 128 * t : first + 128 * t + 128, :])
            both = both[: 2 * n] + both[2 * n :]
            both = both[:n] * m.halff[0] + both[n:] * m.halff[1]
            down.append(both if couplings is None else couplings[h][t] + both)
    return down


def pick_rows(table, level_rows):
    count = table.shape[0]
    row = lax.broadcasted_iota(jnp.int32, (8, count), 0)
    col = lax.broadcasted_iota(jnp.int32, (8, count), 1)
    wanted = jnp.zeros((8, count), jnp.int32) - 1
    for level, at in level_rows.items():
        wanted = jnp.where(row == level, at, wanted)
    return nn((col == wanted).astype(F32).astype(BF16), table)


def build_paths(place, xfer_top, wide_path, paths, weights):
    rows = pick_rows(xfer_top[...], {level: TOP_XFER[level] + (place >> level) for level in range(5)})
    spread_table(rows[0:5], wide_path)
    row = lax.broadcasted_iota(jnp.int32, (32, 128), 0)
    lane = lax.broadcasted_iota(jnp.int32, (32, 128), 1)
    step = [wide_path[32 * level : 32 * level + 32, :] for level in range(5)]

    def times(left, right):
        both = nn(jnp.concatenate([part[:, 0:32] for part in halves(left)], axis=0), right)
        return both[:32] + both[32:]

    pair = halves(nn(step[2][:, 0:32], step[3]))
    second = nn(step[0][:, 0:32], step[1])
    fourth = times(second, jnp.concatenate(pair, axis=1))
    fourth = fourth[:, :128] + fourth[:, 128:]
    products = [(row == (lane & 31)).astype(F32), step[0].astype(F32), second, times(second, step[2]), fourth]
    products.append(times(fourth, step[4]))
    for level in range(6):
        paths[32 * level : 32 * level + 32, :] = products[level]
        high, low = halves(products[level])
        weights[0:32, 128 * level : 128 * level + 128] = high
        weights[32:64, 128 * level : 128 * level + 128] = low


def build_top(place, couple, couple_top, paths, wide_couple, top):
    at = {level: TOP_COUPLE[level] + (place >> level) for level in range(1, 6)}
    for k in range(3):
        rows = pick_rows(couple_top[k], at) + pick_rows(couple[k], {0: LOW[4]})
        spread_table(rows[0:6], wide_couple, 6 * k)
    for level in range(6):
        high, low = halves(paths[32 * level : 32 * level + 32, :])
        left = jnp.concatenate([high[:, 0:32], low[:, 0:32]], axis=0)
        right = [wide_couple[(6 * k + level) * 32 : (6 * k + level + 1) * 32, :] for k in range(3)]
        both = nn(left, jnp.concatenate(right, axis=1))
        high, low = halves(both[:32] + both[32:])
        for k in range(3):
            at = (6 * k + level) * 128
            top[0:32, at : at + 128] = high[:, 128 * k : 128 * k + 128]
            top[32:64, at : at + 128] = low[:, 128 * k : 128 * k + 128]


def relation(place):
    lane = lax.broadcasted_iota(jnp.int32, (1, 128), 1)
    k = (lane >= 24).astype(jnp.int32) + (lane >= 48).astype(jnp.int32) + (lane >= 72).astype(jnp.int32)
    level = (lane - 24 * k) >> 2
    node = place >> level
    third = jnp.where((node & 1) == 0, node + 3, node - 3)
    slot = jnp.where(k == 0, node - 2, jnp.where(k == 1, node + 2, jnp.where(k == 2, third, -1)))
    row = lax.broadcasted_iota(jnp.int32, (4 * DEVICES, 128), 0)
    match = (((row >> 2) >> level) == slot) & ((row & 3) == (lane & 3))
    return match.astype(F32).astype(BF16)


def point_parts(points):
    high = points.astype(BF16).astype(F32)
    rest = points - high
    mid = rest.astype(BF16).astype(F32)
    low = rest - mid
    return jnp.concatenate([high, mid, low, jnp.zeros((7, points.shape[1]), F32)], axis=0).astype(BF16)


def build_tiles(place, parts, cols, counts, from_left, from_right, near_left, near_right, tiles):
    half = lanes_in(8, 0, 64, F32)
    other = 1.0 - half
    blocks = [from_left[320 + 16 * c : 336 + 16 * c, :] for c in range(4)]
    blocks += [parts[:, 128 * c : 128 * c + 128] for c in range(CHUNKS)]
    blocks += [from_right[320 + 16 * c : 336 + 16 * c, :] for c in range(4)]
    row = lax.broadcasted_iota(jnp.int32, (8, 16), 0)
    col = lax.broadcasted_iota(jnp.int32, (8, 16), 1)
    adder = ((col % 3 == row) & (col < 9) & (row < 3)).astype(F32).astype(BF16)
    for c in range(16):
        joined = nn(adder, blocks[c]) * SCALE
        turned = pltpu.roll(joined, 64, 1)
        near_left[2 * c] = joined * half
        near_right[2 * c + 1] = joined * other
        near_left[2 * c + 1] = turned * half
        near_right[2 * c] = turned * other
    row = lax.broadcasted_iota(jnp.int32, (16, 384), 0)
    col = lax.broadcasted_iota(jnp.int32, (16, 384), 1)
    column = ((row % 3 == (col >> 7)) & (row < 9)).astype(F32).astype(BF16)
    lane = lax.broadcasted_iota(jnp.int32, (1, 128), 1)
    base = place * LEAF_DEV - HALO
    for c in range(CHUNKS):
        targets = tn(parts[:, 128 * c : 128 * c + 128], column) * SCALE
        for e in range(2):
            leaf = 2 * c + e
            count = counts[leaf]
            mine = [targets[64 * e : 64 * e + 64, 128 * x : 128 * x + 128] for x in range(3)]
            for pair in range(NEAR // 2):
                first = cols[2 * pair, leaf] - base
                second = cols[2 * pair + 1, leaf] - base
                source = near_left[first] + near_right[second]
                squares = SOFT
                for x in range(3):
                    gap = mine[x] - source[x : x + 1, :]
                    squares = squares + gap * gap
                slot = jnp.where(lane < 64, 2 * pair, 2 * pair + 1)
                gain = jnp.where(slot < count, LOG_GAIN, -2000.0)
                value = jnp.exp2(gain - squares * lax.rsqrt(squares))
                tiles[64 * leaf : 64 * leaf + 64, 128 * pair : 128 * pair + 128] = value.astype(BF16)


def near_field(place, signal, from_left, from_right, cols, tiles, near_left, near_right, m):
    chunks = [from_left[16 * c : 16 * c + 16, :] for c in range(4)]
    chunks += signal
    chunks += [from_right[16 * c : 16 * c + 16, :] for c in range(4)]
    for c in range(16):
        turned = pltpu.roll(chunks[c].astype(F32), 64, 1).astype(BF16)
        near_left[2 * c] = chunks[c] * m.half[0]
        near_right[2 * c + 1] = chunks[c] * m.half[1]
        near_left[2 * c + 1] = turned * m.half[0]
        near_right[2 * c] = turned * m.half[1]
    base = place * LEAF_DEV - HALO
    result = []
    for c in range(CHUNKS):
        rows = []
        for leaf in (2 * c, 2 * c + 1):
            parts = []
            for pair in range(NEAR // 2):
                first = cols[2 * pair, leaf] - base
                second = cols[2 * pair + 1, leaf] - base
                parts.append(near_left[first] + near_right[second])
            rows.append(jnp.concatenate(parts, axis=1))
        both = nt(jnp.concatenate(rows, axis=0), tiles[128 * c : 128 * c + 128, :])
        result.append(both[:16] * m.halff[0] + both[16:] * m.halff[1])
    return result


def far_field(down, basis, m):
    n = m.rows
    result = []
    split = [halves(d) for d in down]
    for c in range(CHUNKS):
        high, low = split[c // 2]
        g = (2 * c) % 4
        left = [high * m.group[g], high * m.group[g + 1], low * m.group[g], low * m.group[g + 1]]
        wide = jnp.concatenate([basis[:, 128 * c : 128 * c + 128]] * 4, axis=0)
        far = nn(jnp.concatenate(left, axis=0), wide)
        far = far[: 2 * n] + far[2 * n :]
        result.append(far[:n] * m.halff[0] + far[n:] * m.halff[1])
    return result


def build_root_basis(basis, xfer, root_basis):
    row = lax.broadcasted_iota(jnp.int32, (32, 128), 0)
    one = (row == (lax.broadcasted_iota(jnp.int32, (32, 128), 1) & 31)).astype(F32)
    m = Masks(32)
    for c, far in enumerate(far_field(down_pass(one, None, xfer, m), basis, m)):
        high, low = halves(far)
        root_basis[0:32, 128 * c : 128 * c + 128] = high
        root_basis[32:64, 128 * c : 128 * c + 128] = low


def finish(down, local, root_basis):
    both = nn(jnp.concatenate([part[:, 0:64] for part in halves(down)], axis=0), root_basis[...])
    return (local[...] + both[:16] + both[16:]).astype(BF16)


def everywhere(parts):
    total = jnp.concatenate([parts, jnp.zeros((16, 64), F32)], axis=1)
    total = total + pltpu.roll(total, 64, 1)
    return total + pltpu.roll(total, 32, 1)


def store_heights(heights, out):
    at = 0
    for nodes in heights:
        for node in nodes:
            for part in node:
                out[at : at + 16, :] = part
                at += 16


def load_heights(source):
    heights, at = [], 0
    for count in NODES:
        heights.append([(source[b : b + 16, :], source[b + 16 : b + 32, :]) for b in range(at, at + 32 * count, 32)])
        at += 32 * count
    return heights


def store_local(near, couplings, basis, xfer, local_out, m):
    far = far_field(down_pass(None, couplings, xfer, m), basis, m)
    for c in range(CHUNKS):
        local_out[:, 128 * c : 128 * c + 128] = near[c] + far[c]


def chunks_of(signal):
    return [signal[:, 128 * c : 128 * c + 128] for c in range(CHUNKS)]


def fetch(sources, targets, sems):
    copies = [pltpu.make_async_copy(s, t, sems.at[i]) for i, (s, t) in enumerate(zip(sources, targets, strict=True))]
    for copy in copies:
        copy.start()
    return copies


def first_kernel(
    vectors_hbm, points_hbm, basis_hbm, xfer_hbm, xfer_top_hbm, near, far, gather, heights_out, xfer_out, paths, weights,
    vectors, points, basis, xfer_low, xfer_top, wide_path, sems,
):
    copies = fetch(
        (xfer_hbm, vectors_hbm, basis_hbm, points_hbm, xfer_top_hbm), (xfer_low, vectors, basis, points, xfer_top), sems
    )
    place = lax.axis_index("leaf")
    m = Masks()
    xfer_out[960:1024, :] = jnp.zeros((64, 128), BF16)
    copies[0].wait()
    spread_table(xfer_low[...], xfer_out)
    copies[1].wait()
    copies[2].wait()
    signal = chunks_of(vectors)
    heights, root = up_pass(signal, basis, xfer_out, m)
    write_halo(place, signal, heights, near, far)
    store_heights(heights, heights_out)
    copies[3].wait()
    parts = chunks_of(point_parts(points[...]))
    copies[4].wait()
    build_paths(place, xfer_top, wide_path, paths, weights)
    write_sends(place, root, weights, gather)
    exchange_rows(place, parts[:4], parts[4:], near, far, 320)


def table_kernel(
    couple_top_hbm, couple_hbm, basis_hbm, paths, xfer, top, couple_wide, root_basis,
    couple_top, couple, basis, wide_couple, sems,
):
    copies = fetch((basis_hbm, couple_hbm, couple_top_hbm), (basis, couple, couple_top), sems)
    copies[1].wait()
    spread_couple(couple, couple_wide)
    copies[0].wait()
    copies[2].wait()
    build_top(lax.axis_index("leaf"), couple, couple_top, paths, wide_couple, top)
    build_root_basis(basis, xfer, root_basis)


def local_first_kernel(
    cols_hbm, counts_hbm, vectors_hbm, points_hbm, basis_hbm, couple_wide, xfer, far, near, heights_in,
    tiles, local_out,
    cols, counts, vectors, points, basis, from_left, from_right, places_left, places_right, near_left, near_right, sems,
):
    copies = fetch(
        (cols_hbm, counts_hbm, vectors_hbm, points_hbm, basis_hbm), (cols, counts, vectors, points, basis), sems
    )
    m = Masks()
    place = lax.axis_index("leaf")
    sides(place, near, far, from_left, from_right)
    for copy in copies:
        copy.wait()
    build_tiles(
        place, point_parts(points[...]), cols, counts, from_left, from_right, places_left, places_right, tiles
    )
    couplings = couple_low(load_heights(heights_in), from_left, from_right, couple_wide, m)
    near = near_field(place, chunks_of(vectors), from_left, from_right, cols, tiles, near_left, near_right, m)
    store_local(near, couplings, basis, xfer, local_out, m)


def pack_kernel(basis_hbm, vectors, xfer, near, far, heights_out, basis, sems):
    copies = fetch((basis_hbm,), (basis,), sems)
    m = Masks()
    signal = chunks_of(vectors)
    copies[0].wait()
    heights, _ = up_pass(signal, basis, xfer, m)
    write_halo(lax.axis_index("leaf"), signal, heights, near, far)
    store_heights(heights, heights_out)


def spread_kernel(couple_hbm, after, couple_wide, couple, sems):
    del after
    fetch((couple_hbm,), (couple,), sems)[0].wait()
    spread_couple(couple, couple_wide)


def local_next_kernel(
    cols_hbm, basis_hbm, couple_wide, xfer, vectors, tiles, far, near, heights_in, local_out,
    cols, basis, from_left, from_right, near_left, near_right, sems,
):
    copies = fetch((cols_hbm, basis_hbm), (cols, basis), sems)
    m = Masks()
    place = lax.axis_index("leaf")
    sides(place, near, far, from_left, from_right)
    couplings = couple_low(load_heights(heights_in), from_left, from_right, couple_wide, m)
    copies[0].wait()
    copies[1].wait()
    near = near_field(place, chunks_of(vectors), from_left, from_right, cols, tiles, near_left, near_right, m)
    store_local(near, couplings, basis, xfer, local_out, m)


def down_up_kernel(gathered, top, root_basis, local, weights, gather, signal_out):
    place = lax.axis_index("leaf")
    signal = finish(top_apply(place, gathered, top), local, root_basis)
    signal_out[...] = signal
    write_sends(place, everywhere(nt(signal, root_basis[...])), weights, gather)


def down_last_kernel(gathered, top, root_basis, local, out):
    out[...] = finish(top_apply(lax.axis_index("leaf"), gathered, top), local, root_basis)


def call(kernel, name, arguments, arrays, outputs, scratch, flops, pinned=False):
    if pinned:
        arguments = [pltpu.with_memory_space_constraint(a, pltpu.HBM) for a in arguments]
    inputs = tuple(arguments) + tuple(arrays)
    in_specs = [pl.BlockSpec(memory_space=pltpu.HBM)] * len(arguments)
    in_specs += [pl.BlockSpec(memory_space=pltpu.VMEM)] * len(arrays)
    return pl.pallas_call(
        kernel,
        out_shape=[jax.ShapeDtypeStruct(shape, dtype) for shape, dtype in outputs],
        in_specs=in_specs,
        out_specs=[pl.BlockSpec(memory_space=pltpu.VMEM)] * len(outputs),
        scratch_shapes=scratch,
        compiler_params=pltpu.CompilerParams(vmem_limit_bytes=VMEM_LIMIT),
        cost_estimate=pl.CostEstimate(flops=flops, bytes_accessed=1 << 20, transcendentals=0),
        name=name,
    )(*inputs)


def to_all(gather):
    count = lax.axis_size("leaf")
    blocks = gather.reshape(count, 4, 128)
    return lax.all_to_all(blocks, "leaf", 0, 0, tiled=True).reshape(count * 4, 128)


def swap(near, far):
    count = lax.axis_size("leaf")
    far = lax.ppermute(far, "leaf", [(i, ((i + 1) ^ 1) - 1) for i in range(1, count - 1)])
    return far, lax.ppermute(near, "leaf", [(i, i ^ 1) for i in range(count)])


def body(vectors, points, near_cols, near_count, basis, xfer_low, couple, xfer_top, couple_top):
    vm, sm = pltpu.VMEM, pltpu.SMEM
    sems = pltpu.SemaphoreType.DMA
    signal_buf, basis_buf, points_buf = vm((16, 1024), BF16), vm((32, 1024), BF16), vm((3, 1024), F32)
    couple_buf = vm((3, 31, 1024), BF16)
    blocks = [vm((32, 16, 128), BF16)] * 2
    sends = [((512, 128), BF16), ((960, 128), BF16)]
    local_out, root_out = ((16, 1024), F32), ((64, 1024), BF16)
    near, far, gather, heights, xfer, paths, weights = call(
        first_kernel, "up_first", (vectors, points, basis, xfer_low, xfer_top), (),
        [((384, 128), BF16)] * 2 + sends + [((1024, 128), BF16), ((192, 128), F32), ((64, 768), BF16)],
        [signal_buf, points_buf, basis_buf, vm((30, 1024), BF16), vm((254, 1024), BF16), vm((160, 128), BF16), sems((5,))],
        1 << 20, True,
    )
    gathered = to_all(gather)
    far, near = swap(near, far)
    top, couple_wide, root_basis = call(
        table_kernel, "tables", (couple_top, couple, basis), (paths, xfer),
        [((64, 2304), BF16), ((1024, 128), BF16), root_out],
        [vm((3, 124, 1024), BF16), couple_buf, basis_buf, vm((576, 128), BF16), sems((3,))], 1 << 32, True,
    )
    tiles, local = call(
        local_first_kernel, "local_first", (near_cols, near_count, vectors, points, basis),
        (couple_wide, xfer, far, near, heights), [((1024, 768), BF16), local_out],
        [sm((12, 16), jnp.int32), sm((16,), jnp.int32), signal_buf, points_buf, basis_buf] + [vm((384, 128), BF16)] * 2
        + [vm((32, 8, 128), F32)] * 2 + blocks + [sems((5,))], 1 << 32,
    )
    gather, signal = call(
        down_up_kernel, "down_up", (), (gathered, top, root_basis, local, weights), [sends[0], ((16, 1024), BF16)], [],
        1 << 20,
    )
    gathered = to_all(gather)
    near, far, heights = call(
        pack_kernel, "pack", (basis,), (signal, xfer), [((320, 128), BF16)] * 2 + [sends[1]], [basis_buf, sems((1,))],
        1 << 32,
    )
    far, near = swap(near, far)
    (couple_wide,) = call(
        spread_kernel, "spread", (couple,), (heights,), [((1024, 128), BF16)], [couple_buf, sems((1,))], 1 << 32
    )
    (local,) = call(
        local_next_kernel, "local_next", (near_cols, basis), (couple_wide, xfer, signal, tiles, far, near, heights),
        [local_out],
        [sm((12, 16), jnp.int32), basis_buf] + [vm((320, 128), BF16)] * 2 + blocks + [sems((2,))], 1 << 32,
    )
    (result,) = call(
        down_last_kernel, "down_last", (), (gathered, top, root_basis, local), [((16, 1024), BF16)], [], 1 << 20
    )
    return result


def solution(mesh):
    placed = (
        P("vec", "leaf"),
        P(None, "leaf"),
        P(None, "leaf"),
        P("leaf"),
        P(None, "leaf"),
        P("leaf", None),
        P(None, "leaf", None),
        P(),
        P(),
    )
    return jax.shard_map(body, mesh=mesh, in_specs=placed, out_specs=P("vec", "leaf"), check_vma=False)
```

```python
import math

import jax
import jax.numpy as jnp
from jax import lax
from jax.experimental import pallas as pl
from jax.experimental.pallas import tpu as pltpu
from jax.sharding import PartitionSpec as P

F32 = jnp.float32
BF16 = jnp.bfloat16
HALO = 8
LEAF_DEV = 16
RANK = 32
NEAR = 12
VEC = 16
DEVICES = 128
CHUNKS = 8
LOW = (0, 16, 24, 28, 30)
NODES = (16, 8, 4, 2)
TOP_XFER = (0, 128, 192, 224, 240, 248)
TOP_COUPLE = (0, 0, 64, 96, 112, 120)
SCALE = 4.0 * math.log2(math.e)
SOFT = 0.01 * SCALE * SCALE
LOG_GAIN = math.log2(4.0 / math.sqrt(64 * NEAR))
VMEM_LIMIT = 48 * 1024 * 1024


def nn(a, b):
    return lax.dot_general(a, b, (((1,), (0,)), ((), ())), preferred_element_type=F32)


def nt(a, b):
    return lax.dot_general(a, b, (((1,), (1,)), ((), ())), preferred_element_type=F32)


def tn(a, b):
    return lax.dot_general(a, b, (((0,), (0,)), ((), ())), preferred_element_type=F32)


def halves(x):
    high = x.astype(BF16)
    return high, (x - high.astype(F32)).astype(BF16)


def lanes_in(rows, lo, size, dtype):
    lane = lax.broadcasted_iota(jnp.int32, (rows, 128), 1)
    return ((lane >= lo) & (lane < lo + size)).astype(F32).astype(dtype)


class Masks:
    def __init__(self, rows=16):
        self.rows = rows
        self.group = [lanes_in(rows, 32 * g, 32, BF16) for g in range(4)]
        self.groupf = [lanes_in(rows, 32 * g, 32, F32) for g in range(4)]
        self.half = [lanes_in(rows, 64 * g, 64, BF16) for g in range(2)]
        self.halff = [lanes_in(rows, 64 * g, 64, F32) for g in range(2)]


def repeat_matrix():
    row = lax.broadcasted_iota(jnp.int32, (128, 128), 0)
    col = lax.broadcasted_iota(jnp.int32, (128, 128), 1)
    return ((row & 31) == (col & 31)).astype(F32).astype(BF16)


def spread_rows(table, nodes):
    row = lax.broadcasted_iota(jnp.int32, (8, 128), 0)
    lane = lax.broadcasted_iota(jnp.int32, (8, 128), 1)
    mine = ((row & 3) == (lane >> 5)).astype(F32)
    parts = []
    for node in nodes:
        for j in range(4):
            one = table[node : node + 1, 256 * j : 256 * j + 128]
            two = table[node : node + 1, 256 * j + 128 : 256 * j + 256]
            parts.append(jnp.where(row < 4, one, two) * mine)
    return jnp.concatenate(parts, axis=0).astype(BF16)


def spread_table(table, out, first=0):
    table = table.astype(F32)
    repeat = repeat_matrix()
    count = table.shape[0]
    for n in range(0, count, 4):
        wide = nn(spread_rows(table, range(n, min(n + 4, count))), repeat)
        at = (first + n) * 32
        out[at : at + wide.shape[0], :] = wide.astype(out.dtype)


def spread_couple(couple, out):
    tables = [couple[k].astype(F32) for k in range(3)]
    row = lax.broadcasted_iota(jnp.int32, (384, 128), 0)
    col = lax.broadcasted_iota(jnp.int32, (384, 128), 1)
    fold = (((row & 31) == (col & 31)) & ((row >> 7) == (col >> 5))).astype(F32).astype(BF16)
    for n in range(0, 31, 4):
        nodes = range(n, min(n + 4, 31))
        wide = nn(jnp.concatenate([spread_rows(table, nodes) for table in tables], axis=1), fold)
        out[32 * n : 32 * n + wide.shape[0], :] = wide.astype(BF16)
    out[992:1024, :] = jnp.zeros((32, 128), BF16)


def up_pass(signal, basis, xfer, m):
    nodes = []
    for c in range(CHUNKS):
        wide = jnp.concatenate([basis[:, 128 * c : 128 * c + 128]] * 4, axis=0)
        both = nt(jnp.concatenate([signal[c] * m.half[0], signal[c] * m.half[1]], axis=0), wide)
        nodes += [both[:16], both[16:]]
    heights = []
    for h in range(4):
        split = [halves(node) for node in nodes]
        heights.append(split)
        nodes = []
        for t in range(0, NODES[h], 4):
            family = split[t : t + 4]
            left = [
                family[i][part] * m.group[i] + family[i + 1][part] * m.group[i + 1]
                for part in range(2)
                for i in range(0, len(family), 2)
            ]
            first = (LOW[h] + t) * 32
            both = nn(jnp.concatenate(left, axis=0), xfer[first : first + 128, :])
            size = 8 * len(family)
            both = both[:size] + both[size:]
            nodes += [both[i : i + 16] for i in range(0, size, 16)]
    return heights, nodes[0]


def exchange_rows(place, to_left, to_right, near, far, first):
    even = (place & 1) == 0
    for i, (one, two) in enumerate(zip(to_left, to_right, strict=True)):
        at = first + 16 * i
        near[at : at + 16, :] = jnp.where(even, two, one)
        far[at : at + 16, :] = jnp.where(even, one, two)


def sides(place, near, far, left, right):
    even = (place & 1) == 0
    for at in range(0, near.shape[0], 16):
        one, two = near[at : at + 16, :], far[at : at + 16, :]
        left[at : at + 16, :] = jnp.where(even, two, one)
        right[at : at + 16, :] = jnp.where(even, one, two)


def write_halo(place, signal, heights, near, far):
    exchange_rows(place, signal[:4], signal[4:], near, far, 0)
    to_left = [heights[h][i][part] for h in range(4) for i in (0, 1) for part in range(2)]
    to_right = [heights[h][i][part] for h in range(4) for i in (-2, -1) for part in range(2)]
    exchange_rows(place, to_left, to_right, near, far, 64)


def write_sends(place, root, weights, gather):
    both = nn(jnp.concatenate([part[:, 0:64] for part in halves(root)], axis=0), weights[...])
    both = both[:16] + both[16:]
    row = lax.broadcasted_iota(jnp.int32, (16, 128), 0)
    mine = ((row >> 2) == (lax.broadcasted_iota(jnp.int32, (16, 128), 1) >> 5)).astype(F32)
    packed = []
    for level in range(6):
        one = both[:, 128 * level : 128 * level + 128] * mine
        one = one[0:8] + one[8:16]
        packed.append(one[0:4] + one[4:8])
    packed = jnp.concatenate(packed, axis=0)
    packed = jnp.concatenate([packed] * 3 + [jnp.zeros((56, 128), F32)], axis=0).astype(BF16)
    gather[...] = nn(relation(place), packed).astype(BF16)


def couple_low(heights, from_left, from_right, table, m):
    result = []
    for h in range(4):
        count = NODES[h]

        def node(n, part, h=h, count=count):
            if n < 0:
                at = 64 + (4 * h + 2 * (n + 2) + part) * 16
                return from_left[at : at + 16, :]
            if n >= count:
                at = 64 + (4 * h + 2 * (n - count) + part) * 16
                return from_right[at : at + 16, :]
            return heights[h][n][part]

        chunks = []
        for t in range(0, count, 4):
            targets = range(t, min(t + 4, count))
            left = []
            for part in range(2):
                for j in targets:
                    third = j + 3 if j % 2 == 0 else j - 3
                    slots = (node(j - 2, part), node(j + 2, part), node(third, part))
                    left.append(slots[0] * m.group[0] + slots[1] * m.group[1] + slots[2] * m.group[2])
            first = (LOW[h] + t) * 32
            wide = nt(jnp.concatenate(left, axis=0), table[first : first + 128, :])
            wide = wide[: 16 * len(targets)] + wide[16 * len(targets) :]
            chunk = wide[0:16] * m.groupf[0]
            for j in range(1, len(targets)):
                chunk = chunk + wide[16 * j : 16 * j + 16] * m.groupf[j]
            chunks.append(chunk)
        result.append(chunks)
    return result


def top_apply(place, gathered, top):
    sums = tn(relation(place), gathered[...])
    row = lax.broadcasted_iota(jnp.int32, (16, 128), 0)
    mine = ((row >> 2) == (lax.broadcasted_iota(jnp.int32, (16, 128), 1) >> 5)).astype(F32)
    left = [jnp.concatenate([sums[4 * i : 4 * i + 4]] * 4, axis=0) * mine for i in range(18)]
    left = halves(jnp.concatenate(left, axis=1))
    total = nt(jnp.concatenate(left, axis=0), top[...])
    return everywhere(total[:16] + total[16:])


def down_pass(root, couplings, xfer, m):
    n = m.rows
    down = [0.0] if couplings is None else couplings[3]
    if root is not None:
        high, low = halves(root)
        first = LOW[3] * 32
        both = nt(jnp.concatenate([high * m.group[0], low * m.group[0]], axis=0), xfer[first : first + 128, :])
        down = [down[0] + both[:n] + both[n:]]
    for h in (2, 1, 0):
        first = LOW[h] * 32
        split = [halves(d) for d in down]
        down = []
        for t in range(NODES[h] // 4):
            high, low = split[t // 2]
            g = (2 * t) % 4
            left = [high * m.group[g], high * m.group[g + 1], low * m.group[g], low * m.group[g + 1]]
            both = nt(jnp.concatenate(left, axis=0), xfer[first + 128 * t : first + 128 * t + 128, :])
            both = both[: 2 * n] + both[2 * n :]
            both = both[:n] * m.halff[0] + both[n:] * m.halff[1]
            down.append(both if couplings is None else couplings[h][t] + both)
    return down


def pick_rows(table, level_rows):
    count = table.shape[0]
    row = lax.broadcasted_iota(jnp.int32, (8, count), 0)
    col = lax.broadcasted_iota(jnp.int32, (8, count), 1)
    wanted = jnp.zeros((8, count), jnp.int32) - 1
    for level, at in level_rows.items():
        wanted = jnp.where(row == level, at, wanted)
    return nn((col == wanted).astype(F32).astype(BF16), table)


def build_paths(place, xfer_top, wide_path, paths, weights):
    rows = pick_rows(xfer_top[...], {level: TOP_XFER[level] + (place >> level) for level in range(5)})
    spread_table(rows[0:5], wide_path)
    row = lax.broadcasted_iota(jnp.int32, (32, 128), 0)
    lane = lax.broadcasted_iota(jnp.int32, (32, 128), 1)
    step = [wide_path[32 * level : 32 * level + 32, :] for level in range(5)]

    def times(left, right):
        both = nn(jnp.concatenate([part[:, 0:32] for part in halves(left)], axis=0), right)
        return both[:32] + both[32:]

    pair = halves(nn(step[2][:, 0:32], step[3]))
    second = nn(step[0][:, 0:32], step[1])
    fourth = times(second, jnp.concatenate(pair, axis=1))
    fourth = fourth[:, :128] + fourth[:, 128:]
    products = [(row == (lane & 31)).astype(F32), step[0].astype(F32), second, times(second, step[2]), fourth]
    products.append(times(fourth, step[4]))
    for level in range(6):
        paths[32 * level : 32 * level + 32, :] = products[level]
        high, low = halves(products[level])
        weights[0:32, 128 * level : 128 * level + 128] = high
        weights[32:64, 128 * level : 128 * level + 128] = low


def build_top(place, couple, couple_top, paths, wide_couple, top):
    at = {level: TOP_COUPLE[level] + (place >> level) for level in range(1, 6)}
    for k in range(3):
        rows = pick_rows(couple_top[k], at) + pick_rows(couple[k], {0: LOW[4]})
        spread_table(rows[0:6], wide_couple, 6 * k)
    for level in range(6):
        high, low = halves(paths[32 * level : 32 * level + 32, :])
        left = jnp.concatenate([high[:, 0:32], low[:, 0:32]], axis=0)
        right = [wide_couple[(6 * k + level) * 32 : (6 * k + level + 1) * 32, :] for k in range(3)]
        both = nn(left, jnp.concatenate(right, axis=1))
        high, low = halves(both[:32] + both[32:])
        for k in range(3):
            at = (6 * k + level) * 128
            top[0:32, at : at + 128] = high[:, 128 * k : 128 * k + 128]
            top[32:64, at : at + 128] = low[:, 128 * k : 128 * k + 128]


def relation(place):
    lane = lax.broadcasted_iota(jnp.int32, (1, 128), 1)
    k = (lane >= 24).astype(jnp.int32) + (lane >= 48).astype(jnp.int32) + (lane >= 72).astype(jnp.int32)
    level = (lane - 24 * k) >> 2
    node = place >> level
    third = jnp.where((node & 1) == 0, node + 3, node - 3)
    slot = jnp.where(k == 0, node - 2, jnp.where(k == 1, node + 2, jnp.where(k == 2, third, -1)))
    row = lax.broadcasted_iota(jnp.int32, (4 * DEVICES, 128), 0)
    match = (((row >> 2) >> level) == slot) & ((row & 3) == (lane & 3))
    return match.astype(F32).astype(BF16)


def point_parts(points):
    high = points.astype(BF16).astype(F32)
    rest = points - high
    mid = rest.astype(BF16).astype(F32)
    low = rest - mid
    return jnp.concatenate([high, mid, low, jnp.zeros((7, points.shape[1]), F32)], axis=0).astype(BF16)


def build_tiles(place, parts, cols, counts, from_left, from_right, near_left, near_right, tiles):
    half = lanes_in(8, 0, 64, F32)
    other = 1.0 - half
    blocks = [from_left[320 + 16 * c : 336 + 16 * c, :] for c in range(4)]
    blocks += [parts[:, 128 * c : 128 * c + 128] for c in range(CHUNKS)]
    blocks += [from_right[320 + 16 * c : 336 + 16 * c, :] for c in range(4)]
    row = lax.broadcasted_iota(jnp.int32, (8, 16), 0)
    col = lax.broadcasted_iota(jnp.int32, (8, 16), 1)
    adder = ((col % 3 == row) & (col < 9) & (row < 3)).astype(F32).astype(BF16)
    for c in range(16):
        joined = nn(adder, blocks[c]) * SCALE
        turned = pltpu.roll(joined, 64, 1)
        near_left[2 * c] = joined * half
        near_right[2 * c + 1] = joined * other
        near_left[2 * c + 1] = turned * half
        near_right[2 * c] = turned * other
    row = lax.broadcasted_iota(jnp.int32, (16, 384), 0)
    col = lax.broadcasted_iota(jnp.int32, (16, 384), 1)
    column = ((row % 3 == (col >> 7)) & (row < 9)).astype(F32).astype(BF16)
    lane = lax.broadcasted_iota(jnp.int32, (1, 128), 1)
    base = place * LEAF_DEV - HALO
    for c in range(CHUNKS):
        targets = tn(parts[:, 128 * c : 128 * c + 128], column) * SCALE
        for e in range(2):
            leaf = 2 * c + e
            count = counts[leaf]
            mine = [targets[64 * e : 64 * e + 64, 128 * x : 128 * x + 128] for x in range(3)]
            for pair in range(NEAR // 2):
                first = cols[2 * pair, leaf] - base
                second = cols[2 * pair + 1, leaf] - base
                source = near_left[first] + near_right[second]
                squares = SOFT
                for x in range(3):
                    gap = mine[x] - source[x : x + 1, :]
                    squares = squares + gap * gap
                slot = jnp.where(lane < 64, 2 * pair, 2 * pair + 1)
                gain = jnp.where(slot < count, LOG_GAIN, -2000.0)
                value = jnp.exp2(gain - squares * lax.rsqrt(squares))
                tiles[64 * leaf : 64 * leaf + 64, 128 * pair : 128 * pair + 128] = value.astype(BF16)


def near_field(place, signal, from_left, from_right, cols, tiles, near_left, near_right, m):
    chunks = [from_left[16 * c : 16 * c + 16, :] for c in range(4)]
    chunks += signal
    chunks += [from_right[16 * c : 16 * c + 16, :] for c in range(4)]
    for c in range(16):
        turned = pltpu.roll(chunks[c].astype(F32), 64, 1).astype(BF16)
        near_left[2 * c] = chunks[c] * m.half[0]
        near_right[2 * c + 1] = chunks[c] * m.half[1]
        near_left[2 * c + 1] = turned * m.half[0]
        near_right[2 * c] = turned * m.half[1]
    base = place * LEAF_DEV - HALO
    result = []
    for c in range(CHUNKS):
        rows = []
        for leaf in (2 * c, 2 * c + 1):
            parts = []
            for pair in range(NEAR // 2):
                first = cols[2 * pair, leaf] - base
                second = cols[2 * pair + 1, leaf] - base
                parts.append(near_left[first] + near_right[second])
            rows.append(jnp.concatenate(parts, axis=1))
        both = nt(jnp.concatenate(rows, axis=0), tiles[128 * c : 128 * c + 128, :])
        result.append(both[:16] * m.halff[0] + both[16:] * m.halff[1])
    return result


def far_field(down, basis, m):
    n = m.rows
    result = []
    split = [halves(d) for d in down]
    for c in range(CHUNKS):
        high, low = split[c // 2]
        g = (2 * c) % 4
        left = [high * m.group[g], high * m.group[g + 1], low * m.group[g], low * m.group[g + 1]]
        wide = jnp.concatenate([basis[:, 128 * c : 128 * c + 128]] * 4, axis=0)
        far = nn(jnp.concatenate(left, axis=0), wide)
        far = far[: 2 * n] + far[2 * n :]
        result.append(far[:n] * m.halff[0] + far[n:] * m.halff[1])
    return result


def build_root_basis(basis, xfer, root_basis):
    row = lax.broadcasted_iota(jnp.int32, (32, 128), 0)
    one = (row == (lax.broadcasted_iota(jnp.int32, (32, 128), 1) & 31)).astype(F32)
    m = Masks(32)
    for c, far in enumerate(far_field(down_pass(one, None, xfer, m), basis, m)):
        high, low = halves(far)
        root_basis[0:32, 128 * c : 128 * c + 128] = high
        root_basis[32:64, 128 * c : 128 * c + 128] = low


def finish(down, local, root_basis):
    both = nn(jnp.concatenate([part[:, 0:64] for part in halves(down)], axis=0), root_basis[...])
    return (local[...] + both[:16] + both[16:]).astype(BF16)


def everywhere(parts):
    total = jnp.concatenate([parts, jnp.zeros((16, 64), F32)], axis=1)
    total = total + pltpu.roll(total, 64, 1)
    return total + pltpu.roll(total, 32, 1)


def store_heights(heights, out):
    at = 0
    for nodes in heights:
        for node in nodes:
            for part in node:
                out[at : at + 16, :] = part
                at += 16


def load_heights(source):
    heights, at = [], 0
    for count in NODES:
        heights.append([(source[b : b + 16, :], source[b + 16 : b + 32, :]) for b in range(at, at + 32 * count, 32)])
        at += 32 * count
    return heights


def store_local(near, couplings, basis, xfer, local_out, m):
    far = far_field(down_pass(None, couplings, xfer, m), basis, m)
    for c in range(CHUNKS):
        local_out[:, 128 * c : 128 * c + 128] = near[c] + far[c]


def chunks_of(signal):
    return [signal[:, 128 * c : 128 * c + 128] for c in range(CHUNKS)]


def fetch(sources, targets, sems):
    copies = [pltpu.make_async_copy(s, t, sems.at[i]) for i, (s, t) in enumerate(zip(sources, targets, strict=True))]
    for copy in copies:
        copy.start()
    return copies


def first_kernel(
    vectors_hbm, points_hbm, basis_hbm, xfer_hbm, xfer_top_hbm, near, far, gather, heights_out, xfer_out, paths, weights, basis,
    vectors, points, xfer_low, xfer_top, wide_path, sems,
):
    copies = fetch(
        (xfer_hbm, vectors_hbm, basis_hbm, points_hbm, xfer_top_hbm), (xfer_low, vectors, basis, points, xfer_top), sems
    )
    place = lax.axis_index("leaf")
    m = Masks()
    xfer_out[960:1024, :] = jnp.zeros((64, 128), BF16)
    copies[0].wait()
    spread_table(xfer_low[...], xfer_out)
    copies[1].wait()
    copies[2].wait()
    signal = chunks_of(vectors)
    heights, root = up_pass(signal, basis, xfer_out, m)
    write_halo(place, signal, heights, near, far)
    store_heights(heights, heights_out)
    copies[3].wait()
    parts = chunks_of(point_parts(points[...]))
    copies[4].wait()
    build_paths(place, xfer_top, wide_path, paths, weights)
    write_sends(place, root, weights, gather)
    exchange_rows(place, parts[:4], parts[4:], near, far, 320)


def local_first_kernel(
    cols_hbm, counts_hbm, vectors_hbm, points_hbm, couple_hbm, couple_top_hbm,
    couple_wide, basis, paths, xfer, far, near, heights_in,
    tiles, local_out, top, root_basis,
    cols, counts, vectors, points, couple, couple_top, wide_couple, from_left, from_right,
    places_left, places_right, near_left, near_right, sems,
):
    copies = fetch(
        (cols_hbm, counts_hbm, vectors_hbm, points_hbm, couple_hbm, couple_top_hbm),
        (cols, counts, vectors, points, couple, couple_top),
        sems,
    )
    m = Masks()
    place = lax.axis_index("leaf")
    build_root_basis(basis, xfer, root_basis)
    sides(place, near, far, from_left, from_right)
    for copy in copies[:4]:
        copy.wait()
    build_tiles(
        place, point_parts(points[...]), cols, counts, from_left, from_right, places_left, places_right, tiles
    )
    copies[4].wait()
    copies[5].wait()
    build_top(place, couple, couple_top, paths, wide_couple, top)
    couplings = couple_low(load_heights(heights_in), from_left, from_right, couple_wide, m)
    near = near_field(place, chunks_of(vectors), from_left, from_right, cols, tiles, near_left, near_right, m)
    store_local(near, couplings, basis, xfer, local_out, m)


def pack_kernel(basis_hbm, vectors, xfer, near, far, heights_out, basis, sems):
    copies = fetch((basis_hbm,), (basis,), sems)
    m = Masks()
    signal = chunks_of(vectors)
    copies[0].wait()
    heights, _ = up_pass(signal, basis, xfer, m)
    write_halo(lax.axis_index("leaf"), signal, heights, near, far)
    store_heights(heights, heights_out)


def spread_kernel(couple_hbm, after, couple_wide, couple, sems):
    del after
    fetch((couple_hbm,), (couple,), sems)[0].wait()
    spread_couple(couple, couple_wide)


def local_next_kernel(
    cols_hbm, basis_hbm, couple_wide, xfer, vectors, tiles, far, near, heights_in, local_out,
    cols, basis, from_left, from_right, near_left, near_right, sems,
):
    copies = fetch((cols_hbm, basis_hbm), (cols, basis), sems)
    m = Masks()
    place = lax.axis_index("leaf")
    sides(place, near, far, from_left, from_right)
    couplings = couple_low(load_heights(heights_in), from_left, from_right, couple_wide, m)
    copies[0].wait()
    copies[1].wait()
    near = near_field(place, chunks_of(vectors), from_left, from_right, cols, tiles, near_left, near_right, m)
    store_local(near, couplings, basis, xfer, local_out, m)


def down_up_kernel(gathered, top, root_basis, local, weights, gather, signal_out):
    place = lax.axis_index("leaf")
    signal = finish(top_apply(place, gathered, top), local, root_basis)
    signal_out[...] = signal
    write_sends(place, everywhere(nt(signal, root_basis[...])), weights, gather)


def down_last_kernel(gathered, top, root_basis, local, out):
    out[...] = finish(top_apply(lax.axis_index("leaf"), gathered, top), local, root_basis)


def call(kernel, name, arguments, arrays, outputs, scratch, flops, pinned=False):
    if pinned:
        arguments = [pltpu.with_memory_space_constraint(a, pltpu.HBM) for a in arguments]
    inputs = tuple(arguments) + tuple(arrays)
    in_specs = [pl.BlockSpec(memory_space=pltpu.HBM)] * len(arguments)
    in_specs += [pl.BlockSpec(memory_space=pltpu.VMEM)] * len(arrays)
    return pl.pallas_call(
        kernel,
        out_shape=[jax.ShapeDtypeStruct(shape, dtype) for shape, dtype in outputs],
        in_specs=in_specs,
        out_specs=[pl.BlockSpec(memory_space=pltpu.VMEM)] * len(outputs),
        scratch_shapes=scratch,
        compiler_params=pltpu.CompilerParams(vmem_limit_bytes=VMEM_LIMIT),
        cost_estimate=pl.CostEstimate(flops=flops, bytes_accessed=1 << 20, transcendentals=0),
        name=name,
    )(*inputs)


def to_all(gather):
    count = lax.axis_size("leaf")
    blocks = gather.reshape(count, 4, 128)
    return lax.all_to_all(blocks, "leaf", 0, 0, tiled=True).reshape(count * 4, 128)


def swap(near, far):
    count = lax.axis_size("leaf")
    far = lax.ppermute(far, "leaf", [(i, ((i + 1) ^ 1) - 1) for i in range(1, count - 1)])
    return far, lax.ppermute(near, "leaf", [(i, i ^ 1) for i in range(count)])


def body(vectors, points, near_cols, near_count, basis, xfer_low, couple, xfer_top, couple_top):
    vm, sm = pltpu.VMEM, pltpu.SMEM
    sems = pltpu.SemaphoreType.DMA
    signal_buf, basis_buf, points_buf = vm((16, 1024), BF16), vm((32, 1024), BF16), vm((3, 1024), F32)
    couple_buf = vm((3, 31, 1024), BF16)
    blocks = [vm((32, 16, 128), BF16)] * 2
    sends = [((512, 128), BF16), ((960, 128), BF16)]
    local_out, root_out = ((16, 1024), F32), ((64, 1024), BF16)
    near, far, gather, heights, xfer, paths, weights, basis_near = call(
        first_kernel, "up_first", (vectors, points, basis, xfer_low, xfer_top), (),
        [((384, 128), BF16)] * 2 + sends + [((1024, 128), BF16), ((192, 128), F32), ((64, 768), BF16)]
        + [((32, 1024), BF16)],
        [signal_buf, points_buf, vm((30, 1024), BF16), vm((254, 1024), BF16), vm((160, 128), BF16), sems((5,))],
        1 << 20, True,
    )
    gathered = to_all(gather)
    far, near = swap(near, far)
    (couple_wide,) = call(
        spread_kernel, "spread", (couple,), (heights,), [((1024, 128), BF16)], [couple_buf, sems((1,))], 1 << 32, True
    )
    tiles, local, top, root_basis = call(
        local_first_kernel, "local_first", (near_cols, near_count, vectors, points, couple, couple_top),
        (couple_wide, basis_near, paths, xfer, far, near, heights),
        [((1024, 768), BF16), local_out, ((64, 2304), BF16), root_out],
        [sm((12, 16), jnp.int32), sm((16,), jnp.int32), signal_buf, points_buf, couple_buf, vm((3, 124, 1024), BF16),
         vm((576, 128), BF16)] + [vm((384, 128), BF16)] * 2 + [vm((32, 8, 128), F32)] * 2 + blocks
        + [sems((6,))], 1 << 33, True,
    )
    gather, signal = call(
        down_up_kernel, "down_up", (), (gathered, top, root_basis, local, weights), [sends[0], ((16, 1024), BF16)], [],
        1 << 20,
    )
    gathered = to_all(gather)
    near, far, heights = call(
        pack_kernel, "pack", (basis,), (signal, xfer), [((320, 128), BF16)] * 2 + [sends[1]], [basis_buf, sems((1,))],
        1 << 32,
    )
    far, near = swap(near, far)
    (couple_wide,) = call(
        spread_kernel, "spread", (couple,), (heights,), [((1024, 128), BF16)], [couple_buf, sems((1,))], 1 << 32
    )
    (local,) = call(
        local_next_kernel, "local_next", (near_cols, basis), (couple_wide, xfer, signal, tiles, far, near, heights),
        [local_out],
        [sm((12, 16), jnp.int32), basis_buf] + [vm((320, 128), BF16)] * 2 + blocks + [sems((2,))], 1 << 32,
    )
    (result,) = call(
        down_last_kernel, "down_last", (), (gathered, top, root_basis, local), [((16, 1024), BF16)], [], 1 << 20
    )
    return result


def solution(mesh):
    placed = (
        P("vec", "leaf"),
        P(None, "leaf"),
        P(None, "leaf"),
        P("leaf"),
        P(None, "leaf"),
        P("leaf", None),
        P(None, "leaf", None),
        P(),
        P(),
    )
    return jax.shard_map(body, mesh=mesh, in_specs=placed, out_specs=P("vec", "leaf"), check_vma=False)
```
